32 devices in a mesh: dp: 8 (over y, x, core), mp: 4 (over z).
Axes of the slice: x: 2, y: 2, z: 4, core: 2. Of those that a mesh axis runs over, the one named last changes fastest.
Arguments:
- tokens: bfloat16 [2048, 24, 512], P('mp', 'dp'), may hold values from -6 to 6
- pair_ids: int32 [24], P('dp'), may hold values from 0 to 15
- lengths: int32 [24], P('dp'), may hold values from 256 to 2048, as said below
- pair_embed: float32 [16, 512], replicated, may hold values from -3 to 3
- qkv_weight: bfloat16 [512, 1536], P(None, 'mp'), may hold values from -0.25 to 0.25
- q_bias: bfloat16 [512], P('mp'), may hold values from -1.796875 to 1.796875
- v_bias: bfloat16 [512], P('mp'), may hold values from -0.29882812 to 0.29882812
- out_weight: bfloat16 [512, 512], P('mp'), may hold values from -3 to 3
- out_bias: float32 [512], replicated, may hold values from -1.8 to 1.8
- ffn_in_weight: bfloat16 [512, 2048], replicated, may hold values from -0.25 to 0.25
- ffn_in_bias: float32 [2048], replicated, may hold values from -3 to 3
- ffn_out_weight: bfloat16 [2048, 512], replicated, may hold values from -0.125 to 0.125
- ffn_out_bias: float32 [512], replicated, may hold values from -1.8 to 1.8
- cotangent: bfloat16 [2048, 24, 512], P('mp', 'dp'), may hold values from -6 to 6
Outputs:
- out: bfloat16 [2048, 24, 512], P('mp', 'dp')
- tokens_grad: float32 [2048, 24, 512], P('mp', 'dp')
- pair_embed_grad: float32 [16, 512], replicated
- qkv_weight_grad: float32 [512, 1536], P(None, 'mp')
- q_bias_grad: float32 [512], P('mp')
- v_bias_grad: float32 [512], P('mp')
- out_weight_grad: float32 [512, 512], P('mp')
- out_bias_grad: float32 [512], replicated
- ffn_in_weight_grad: float32 [512, 2048], replicated
- ffn_in_bias_grad: float32 [2048], replicated
- ffn_out_weight_grad: float32 [2048, 512], replicated
- ffn_out_bias_grad: float32 [512], replicated
The draws below stay inside these ranges and needn't reach their ends.
Inputs may be any that keep to these rules, and one draw needn't show every extreme that they name: `lengths`: in every group of 3 consecutive sequences one, drawn from the seed, has exactly 2048 tokens; positions at or after a sequence's length are padding.
All inputs are finite; a program needn't handle non-finite values.
Results may differ from the reference program's by a relative error of at most 0.018.
The reference program's roundings to bfloat16 on the way count: a program that leaves them out, or rounds other values in their place, can miss the bound.
Values may be sent and summed in bfloat16 or wider, within the bound.
A program may use at most 256 MiB of HBM per device.

```python
import math
import jax
import jax.numpy as jnp
import numpy as np
from jax import lax

D = 512
HEADS = 8
FF = 2048
HD = 64
PAIRS = 16
SEQS = 3
LENGTH = 2048
BATCH = 24


def draw_lengths(key, part):
    key = jax.random.fold_in(key, 11)
    first_key, second_key = jax.random.split(key)
    ragged = jax.random.randint(first_key, (BATCH,), LENGTH // 8, LENGTH + 1)
    groups = BATCH // SEQS
    chosen = jax.random.randint(second_key, (groups,), 0, SEQS)
    longest = (jnp.arange(SEQS)[None, :] == chosen[:, None]).reshape(BATCH)
    return jnp.where(longest, LENGTH, ragged).astype(jnp.int32)


def touch_ends(values, stream_key, least, top_value):
    index_at = [jax.random.randint(jax.random.fold_in(stream_key, axis), (), 0, length) for axis, length in enumerate(values.shape)]
    widest = values.shape.index(max(values.shape))
    next_to = index_at[:widest] + [(index_at[widest] + 1) % values.shape[widest]] + index_at[widest + 1:]
    return values.at[tuple(index_at)].set(least).at[tuple(next_to)].set(top_value)


def block_levels(rng, extent, cuts, low, largest):
    level = 1.0
    for axis_at, blocks in cuts:
        steps = jax.random.uniform(jax.random.fold_in(jax.random.fold_in(rng, 6), axis_at), (blocks,), jnp.float32, low / len(cuts), largest / len(cuts))
        level = level * jnp.repeat(jnp.exp(steps), extent[axis_at] // blocks).reshape((-1,) + (1,) * (len(extent) - 1 - axis_at))
    return level


def cumulative_ranks(number_of, lean):
    portions = [(1 << 20) // math.isqrt(standing ** lean) + 1 for standing in range(1, number_of + 1)]
    scale = 1 + sum(portions) // (1 << 30)
    return np.cumsum(np.array([max(1, weight // scale) for weight in portions]))


def ranked(own_key, dims, number_of, lean):
    table = cumulative_ranks(number_of, lean)
    lot = jax.random.randint(jax.random.fold_in(own_key, 1), dims, 0, int(table[number_of - 1]))
    rank = jnp.searchsorted(jnp.asarray(table, jnp.int32), lot, side="right")
    return jax.random.permutation(jax.random.fold_in(own_key, 2), number_of)[rank].astype(jnp.int32)


def scatter_about(own_key, shape, spread, limit, shards=(), held_as=jnp.bfloat16):
    gain = block_levels(own_key, shape, shards, -0.22, 0.18) if shards else 1.0
    entries = jax.random.normal(own_key, shape, jnp.float32) * spread * gain
    return jnp.minimum(jnp.maximum(entries, -limit), limit).astype(held_as)


def setup_inputs(seed: int = 0) -> dict:
    streams_of = jax.random.split(jax.random.key(seed), 15)
    tokens = scatter_about(streams_of[0], (LENGTH, BATCH, D), 1.0, 6.0, ((0, 4), (1, 8)))
    pair_ids = touch_ends(ranked(streams_of[1], (BATCH,), PAIRS, 2), jax.random.fold_in(streams_of[1], 3), 0, PAIRS - 1).astype(jnp.int32)
    lengths = draw_lengths(jax.random.fold_in(streams_of[14], 71), 0)
    pair_embed = scatter_about(streams_of[3], (PAIRS, D), 0.5, 3.0, (), jnp.float32)
    qkv_weight = scatter_about(streams_of[4], (D, 3 * D), D ** -0.5, 0.25, ((1, 4),))
    q_bias = scatter_about(streams_of[5], (D,), 0.3, 1.796875, ((0, 4),))
    v_bias = scatter_about(streams_of[6], (D,), 0.05, 0.29882812, ((0, 4),))
    out_weight = scatter_about(streams_of[7], (D, D), 4 ** -0.5, 3.0, ((0, 4),))
    out_bias = scatter_about(streams_of[8], (D,), 0.3, 1.8, (), jnp.float32)
    ffn_in_weight = scatter_about(streams_of[9], (D, FF), D ** -0.5, 0.25)
    ffn_in_bias = scatter_about(streams_of[10], (FF,), 0.5, 3.0, (), jnp.float32)
    ffn_out_weight = scatter_about(streams_of[11], (FF, D), FF ** -0.5, 0.125)
    ffn_out_bias = scatter_about(streams_of[12], (D,), 0.3, 1.8, (), jnp.float32)
    cotangent = scatter_about(streams_of[13], (LENGTH, BATCH, D), 1.0, 6.0, ((0, 4), (1, 8)))
    return {"tokens": tokens, "pair_ids": pair_ids, "lengths": lengths, "pair_embed": pair_embed, "qkv_weight": qkv_weight, "q_bias": q_bias, "v_bias": v_bias, "out_weight": out_weight, "out_bias": out_bias, "ffn_in_weight": ffn_in_weight, "ffn_in_bias": ffn_in_bias, "ffn_out_weight": ffn_out_weight, "ffn_out_bias": ffn_out_bias, "cotangent": cotangent}


@jax.custom_vjp
def low(v):
    return lax.optimization_barrier(v.astype(jnp.bfloat16)).astype(jnp.float32)

@jax.custom_vjp
def low_back(v):
    return v

def low_keep(v):
    return (low(v), None)

def low_pass(kept, grad):
    return (grad,)

def back_keep(v):
    return (v, None)

def back_low(kept, grad):
    return (low(grad),)
low.defvjp(low_keep, low_pass)
low_back.defvjp(back_keep, back_low)
HIGHEST = lax.Precision.HIGHEST

def encoder_layer(inputs, embed_row, qkv_weight, q_bias, v_bias, out_weight, out_bias, ffn_in_weight, ffn_in_bias, ffn_out_weight, ffn_out_bias, seq_length):
    first_sum = inputs + embed_row[None, :]
    projected = jnp.dot(low(first_sum), qkv_weight, precision=HIGHEST).reshape(LENGTH, HEADS, 3, HD)
    blank_part = jnp.zeros((HEADS, HD), jnp.float32)
    bias_all = jnp.stack([q_bias.reshape(HEADS, HD), blank_part, v_bias.reshape(HEADS, HD)], axis=1)
    qkv_value = low(low_back(projected + bias_all[None]))
    queries = qkv_value[:, :, 0]
    keys_all = qkv_value[:, :, 1]
    values_all = qkv_value[:, :, 2]
    is_valid = jnp.arange(LENGTH, dtype=jnp.int32) < seq_length
    block_rows = min(512, LENGTH)

    def attend_block(query_block):
        scores = jnp.einsum('qhe,khe->hqk', query_block, keys_all, precision=HIGHEST) * HD ** (-0.5)
        scores = low_back(scores)
        scores = jnp.where(is_valid[None, None, :], scores, -1e+30)
        probs = low(jax.nn.softmax(scores, axis=-1))
        return jnp.einsum('hqk,khe->qhe', probs, values_all, precision=HIGHEST)
    attended = lax.map(jax.checkpoint(attend_block), queries.reshape(LENGTH // block_rows, block_rows, HEADS, HD))
    attended = low(low_back(attended.reshape(LENGTH, HEADS * HD)))
    mixed = low_back(first_sum + (jnp.dot(attended, out_weight, precision=HIGHEST) + out_bias))
    pre_act = low_back(jnp.dot(low(mixed), ffn_in_weight, precision=HIGHEST) + ffn_in_bias)
    activated = low(jax.nn.gelu(pre_act))
    return mixed + (jnp.dot(activated, ffn_out_weight, precision=HIGHEST) + ffn_out_bias)

def reference(tokens, pair_ids, lengths, pair_embed, qkv_weight, q_bias, v_bias, out_weight, out_bias, ffn_in_weight, ffn_in_bias, ffn_out_weight, ffn_out_bias, cotangent):
    params = tuple((weight_arg.astype(jnp.float32) for weight_arg in (qkv_weight, q_bias, v_bias, out_weight, out_bias, ffn_in_weight, ffn_in_bias, ffn_out_weight, ffn_out_bias)))
    embed_table = pair_embed.astype(jnp.float32)
    seq_inputs = jnp.moveaxis(tokens.astype(jnp.float32), 1, 0)
    seq_cotangents = jnp.moveaxis(cotangent.astype(jnp.float32), 1, 0)

    def per_sequence(totals, seq_items):
        seq_input, seq_cotangent, pair_id, seq_length = seq_items
        embed_row = embed_table[pair_id]

        def apply_layer(inputs, row_value, *weights):
            return encoder_layer(inputs, row_value, *weights, seq_length)
        result, pullback = jax.vjp(apply_layer, seq_input, embed_row, *params)
        seq_grads = pullback(seq_cotangent)
        select = (jnp.arange(PAIRS, dtype=jnp.int32) == pair_id).astype(jnp.float32)
        table_total = totals[0] + select[:, None] * seq_grads[1][None, :]
        weight_totals = tuple((total_item + grad_item for total_item, grad_item in zip(totals[1:], seq_grads[2:])))
        return ((table_total,) + weight_totals, (result, seq_grads[0]))
    initial = (jnp.zeros((PAIRS, D), jnp.float32),) + tuple((jnp.zeros_like(weight_arg) for weight_arg in params))
    totals, (outputs, input_grads) = lax.scan(per_sequence, initial, (seq_inputs, seq_cotangents, pair_ids, lengths))
    return (jnp.moveaxis(outputs, 0, 1).astype(jnp.bfloat16), jnp.moveaxis(input_grads, 0, 1), totals[0], totals[1], totals[2], totals[3], totals[4], totals[5], totals[6], totals[7], totals[8], totals[9])
```

```python
import functools
import math

import jax
import jax.numpy as jnp
from jax import lax
from jax.experimental import pallas as pl
from jax.experimental.pallas import tpu as pltpu
from jax.sharding import PartitionSpec as P

HD = 64
PAIR = 2 * HD
HIGHEST = lax.Precision.HIGHEST
NEGATIVE = -1e30
LOG2E = math.log2(math.e)
F32 = jnp.float32
BF16 = jnp.bfloat16
VMEM_LIMIT = 56 * 1024 * 1024


def nn(a, b):
    return jnp.dot(a, b, preferred_element_type=F32)


def nt(a, b):
    return lax.dot_general(a, b, (((1,), (1,)), ((), ())), preferred_element_type=F32)


def tn(a, b):
    return lax.dot_general(a, b, (((0,), (0,)), ((), ())), preferred_element_type=F32)


def head_lanes(rows, head):
    lane = lax.broadcasted_iota(jnp.int32, (rows, PAIR), 1)
    return (lane >= head * HD) & (lane < (head + 1) * HD)


def one_head(pair_rows, head):
    return jnp.where(head_lanes(pair_rows.shape[0], head), pair_rows, jnp.zeros_like(pair_rows))


def fold8(values, op):
    rows, lanes = values.shape
    return op(values.reshape(rows // 8, 8, lanes), axis=0)


def attend_forward(length_ref, x_all, x_own, weight, q_bias, v_bias,
                   q_out, k_out, v_out, att_out, att_t_out, lse_out, s_all, acc, *, block):
    length = length_ref[0]
    blocks = (length + block - 1) // block
    rows = x_own.shape[0]
    q_pair = ((nn(x_own[...], weight[0, :, :PAIR]) + q_bias[0]).astype(BF16)) * BF16(HD ** -0.5)
    q_out[0] = q_pair
    q_heads = [one_head(q_pair, 0), one_head(q_pair, 1)]

    def score_step(j, tops):
        at = pl.ds(pl.multiple_of(j * block, block), block)
        kv = nn(x_all[at, :], weight[0, :, PAIR:])
        k_blk = kv[:, :PAIR].astype(BF16)
        k_out[0, at, :] = k_blk
        v_out[0, at, :] = (kv[:, PAIR:] + v_bias[0]).astype(BF16)
        keep = (lax.broadcasted_iota(jnp.int32, (block, rows), 0) + j * block) < length
        new = []
        for h in range(2):
            s = nt(k_blk, q_heads[h]) * LOG2E
            s = jnp.where(keep, s, NEGATIVE)
            s_all[h, at, :] = s
            new.append(jnp.maximum(tops[h], fold8(s, jnp.max)))
        return tuple(new)

    start = jnp.full((8, rows), NEGATIVE, F32)
    tops = lax.fori_loop(0, blocks, score_step, (start, start))
    tops = [jnp.max(t, axis=0, keepdims=True) for t in tops]
    acc[...] = jnp.zeros_like(acc)

    def value_step(j, sums):
        at = pl.ds(pl.multiple_of(j * block, block), block)
        v_blk = v_out[0, at, :]
        new = []
        for h in range(2):
            p = jnp.exp2(s_all[h, at, :] - tops[h])
            new.append(sums[h] + fold8(p, jnp.sum))
            acc[h] += tn(v_blk, p.astype(BF16))
        return tuple(new)

    zero = jnp.zeros((8, rows), F32)
    sums = lax.fori_loop(0, blocks, value_step, (zero, zero))
    sums = [jnp.sum(t, axis=0, keepdims=True) for t in sums]
    att_t = jnp.concatenate([acc[h, h * HD:(h + 1) * HD, :] * (1.0 / sums[h]) for h in range(2)], axis=0)
    att_t_out[0] = att_t
    att_out[...] = att_t.T.astype(BF16)
    lse_out[0] = jnp.concatenate(
        [tops[h] + jnp.log2(sums[h]) for h in range(2)] + [jnp.zeros((6, rows), F32)], axis=0)


def attend_backward(length_ref, place_ref, x_all, x_own, weight, q_in, k_in, v_in, att_t, lse, grad_in,
                    x_grad, w_grad, qb_grad, vb_grad, x_acc, kv_grad, dq_acc, *, block):
    length = length_ref[0]
    blocks = (length + block - 1) // block
    rows = x_own.shape[0]
    pair = pl.program_id(0)
    full = x_all.shape[0]
    q_pair = q_in[0]
    grad_pair = grad_in[...]
    q_heads = [one_head(q_pair, h) for h in range(2)]
    g_heads = [one_head(grad_pair, h) for h in range(2)]
    prod = grad_pair.astype(F32).T * att_t[0]
    delta = [jnp.sum(prod[h * HD:(h + 1) * HD], axis=0, keepdims=True) for h in range(2)]
    tops = [lse[0, h:h + 1, :] for h in range(2)]
    dq_acc[...] = jnp.zeros_like(dq_acc)

    @pl.when(pair == 0)
    def _():
        x_acc[...] = jnp.zeros_like(x_acc)

    w_grad[0] = jnp.zeros(w_grad.shape[1:], F32)

    def step(j, vsum):
        at = pl.ds(pl.multiple_of(j * block, block), block)
        k_blk = k_in[0, at, :]
        v_blk = v_in[0, at, :]
        keep = (lax.broadcasted_iota(jnp.int32, (block, rows), 0) + j * block) < length
        dk = jnp.zeros((block, PAIR), F32)
        dv = jnp.zeros((block, PAIR), F32)
        for h in range(2):
            s = nt(k_blk, q_heads[h]) * LOG2E
            p = jnp.where(keep, jnp.exp2(s - tops[h]), 0.0)
            dp = nt(v_blk, g_heads[h])
            ds = (p * (dp - delta[h])).astype(BF16)
            dv += nn(p.astype(BF16), g_heads[h])
            dk += nn(ds, q_heads[h])
            dq_acc[h] += tn(k_blk, ds)
        dv = dv.astype(BF16)
        both = jnp.concatenate([dk.astype(BF16), dv], axis=1)
        x_acc[at, :] += nt(both, weight[0, :, PAIR:])
        w_grad[0, PAIR:, :] += tn(both, x_all[at, :])
        return vsum + fold8(dv.astype(F32), jnp.sum)

    vsum = lax.fori_loop(0, blocks, step, jnp.zeros((8, PAIR), F32))
    vb_grad[0] = jnp.broadcast_to(jnp.sum(vsum, axis=0, keepdims=True), (8, PAIR))
    dq_t = jnp.concatenate([dq_acc[h, h * HD:(h + 1) * HD, :] for h in range(2)], axis=0) * (HD ** -0.5)
    dq = dq_t.T.astype(BF16)
    qb_grad[0] = jnp.broadcast_to(jnp.sum(dq.astype(F32), axis=0, keepdims=True), (8, PAIR))
    mine = pl.ds(pl.multiple_of(place_ref[0] * rows, rows), rows)
    x_acc[mine, :] += nt(dq, weight[0, :, :PAIR])
    w_grad[0, :PAIR, :] += tn(dq, x_own[...])

    @pl.when(pair == pl.num_programs(0) - 1)
    def _():
        x_grad[...] = x_acc[...].astype(BF16)


def feed_forward(tok, row, att, cot, w_out, b_out, w_in, b_in, w_last, b_last,
                 result, mixed_grad, att_grad, g_last, gb_last, g_in, gb_in, g_out, gb_out,
                 *, chunk):
    first = pl.program_id(0) == 0
    rows, width = tok.shape[1], tok.shape[2]
    hidden = w_in.shape[1]

    @pl.when(first)
    def _():
        for ref in (g_last, gb_last, g_in, gb_in, g_out, gb_out):
            ref[...] = jnp.zeros_like(ref)

    cot_rows = cot[0]
    att_rows = att[0]
    mixed = (tok[0].astype(F32) + row[0]) + (nn(att_rows, w_out[...]) + b_out[...])
    mixed_low = mixed.astype(BF16)
    out_sum = mixed + b_last[...]
    back_sum = cot_rows.astype(F32)
    root = math.sqrt(2.0 / math.pi)
    for c in range(hidden // chunk):
        at = slice(c * chunk, (c + 1) * chunk)
        pre = nn(mixed_low, w_in[:, at]) + b_in[:, at]
        square = pre * pre
        th = jnp.tanh(root * pre * (1.0 + 0.044715 * square))
        half = 0.5 * (1.0 + th)
        act = (pre * half).astype(BF16)
        slope = half + (0.5 * root) * pre * (1.0 - th * th) * (1.0 + (3 * 0.044715) * square)
        out_sum += nn(act, w_last[at, :])
        back = (nt(cot_rows, w_last[at, :]) * slope).astype(BF16)
        gb_in[:, at] += jnp.sum(back.astype(F32), axis=0, keepdims=True)
        back_sum += nt(back, w_in[:, at])
        g_last[at, :] += tn(act, cot_rows)
        g_in[:, at] += tn(mixed_low, back)
    result[0] = out_sum.astype(BF16)
    back_low = back_sum.astype(BF16)
    mixed_grad[0] = back_low
    gb_last[...] += jnp.sum(cot_rows.astype(F32), axis=0, keepdims=True)
    gb_out[...] += jnp.sum(back_low.astype(F32), axis=0, keepdims=True)
    g_out[...] += tn(att_rows, back_low)
    att_grad[0] = nt(back_low, w_out[...]).astype(BF16)


def whole(shape):
    return pl.BlockSpec(shape, lambda *_: (0,) * len(shape))


def call_forward(length, x_all, x_own, weight, q_bias, v_bias):
    full, width = x_all.shape
    rows = x_own.shape[0]
    pairs = weight.shape[0]
    block = min(512, full)
    per_pair = lambda *tail: pl.BlockSpec((1,) + tail, lambda p, *_: (p, 0, 0))
    flops = pairs * (2 * full * width * 2 * PAIR + 8 * full * rows * PAIR)
    return pl.pallas_call(
        functools.partial(attend_forward, block=block),
        grid_spec=pltpu.PrefetchScalarGridSpec(
            num_scalar_prefetch=1,
            grid=(pairs,),
            in_specs=[whole((full, width)), whole((rows, width)), per_pair(width, 3 * PAIR),
                      per_pair(1, PAIR), per_pair(1, PAIR)],
            out_specs=[per_pair(rows, PAIR), per_pair(full, PAIR), per_pair(full, PAIR),
                       pl.BlockSpec((rows, PAIR), lambda p, *_: (0, p)), per_pair(PAIR, rows),
                       per_pair(8, rows)],
            scratch_shapes=[pltpu.VMEM((2, full, rows), F32), pltpu.VMEM((2, PAIR, rows), F32)],
        ),
        out_shape=[
            jax.ShapeDtypeStruct((pairs, rows, PAIR), BF16),
            jax.ShapeDtypeStruct((pairs, full, PAIR), BF16),
            jax.ShapeDtypeStruct((pairs, full, PAIR), BF16),
            jax.ShapeDtypeStruct((rows, pairs * PAIR), BF16),
            jax.ShapeDtypeStruct((pairs, PAIR, rows), F32),
            jax.ShapeDtypeStruct((pairs, 8, rows), F32),
        ],
        cost_estimate=pl.CostEstimate(flops=flops * 2, bytes_accessed=16 << 20,
                                      transcendentals=2 * pairs * full * rows),
        compiler_params=pltpu.CompilerParams(vmem_limit_bytes=VMEM_LIMIT),
        name="attend_forward",
    )(length, x_all, x_own, weight, q_bias, v_bias)


def call_backward(length, place, x_all, x_own, weight, q, k, v, att_t, lse, grad):
    full, width = x_all.shape
    rows = x_own.shape[0]
    pairs = weight.shape[0]
    block = min(512, full)
    per_pair = lambda *tail: pl.BlockSpec((1,) + tail, lambda p, *_: (p, 0, 0))
    return pl.pallas_call(
        functools.partial(attend_backward, block=block),
        grid_spec=pltpu.PrefetchScalarGridSpec(
            num_scalar_prefetch=2,
            grid=(pairs,),
            in_specs=[whole((full, width)), whole((rows, width)), per_pair(width, 3 * PAIR),
                      per_pair(rows, PAIR), per_pair(full, PAIR), per_pair(full, PAIR),
                      per_pair(PAIR, rows), per_pair(8, rows),
                      pl.BlockSpec((rows, PAIR), lambda p, *_: (0, p))],
            out_specs=[whole((full, width)), per_pair(3 * PAIR, width), per_pair(8, PAIR), per_pair(8, PAIR)],
            scratch_shapes=[pltpu.VMEM((full, width), F32), pltpu.VMEM((full, 2 * PAIR), BF16),
                            pltpu.VMEM((2, PAIR, rows), F32)],
        ),
        out_shape=[
            jax.ShapeDtypeStruct((full, width), BF16),
            jax.ShapeDtypeStruct((pairs, 3 * PAIR, width), F32),
            jax.ShapeDtypeStruct((pairs, 8, PAIR), F32),
            jax.ShapeDtypeStruct((pairs, 8, PAIR), F32),
        ],
        cost_estimate=pl.CostEstimate(flops=40 * pairs * full * rows * PAIR, bytes_accessed=16 << 20,
                                      transcendentals=2 * pairs * full * rows),
        compiler_params=pltpu.CompilerParams(vmem_limit_bytes=VMEM_LIMIT),
        name="attend_backward",
    )(length, place, x_all, x_own, weight, q, k, v, att_t, lse, grad)


def call_feed(tok, row, att, cot, w_out, b_out, w_in, b_in, w_last, b_last):
    seqs, rows, width = tok.shape
    hidden = w_in.shape[1]
    per_seq = lambda: pl.BlockSpec((1, rows, width), lambda s: (s, 0, 0))
    return pl.pallas_call(
        functools.partial(feed_forward, chunk=512),
        grid=(seqs,),
        in_specs=[per_seq(), pl.BlockSpec((1, 1, width), lambda s: (s, 0, 0)), per_seq(), per_seq(),
                  whole((width, width)), whole((1, width)), whole((width, hidden)), whole((1, hidden)),
                  whole((hidden, width)), whole((1, width))],
        out_specs=[per_seq(), per_seq(), per_seq(), whole((hidden, width)), whole((1, width)),
                   whole((width, hidden)), whole((1, hidden)), whole((width, width)), whole((1, width))],
        out_shape=[
            jax.ShapeDtypeStruct((seqs, rows, width), BF16),
            jax.ShapeDtypeStruct((seqs, rows, width), BF16),
            jax.ShapeDtypeStruct((seqs, rows, width), BF16),
            jax.ShapeDtypeStruct((hidden, width), F32),
            jax.ShapeDtypeStruct((1, width), F32),
            jax.ShapeDtypeStruct((width, hidden), F32),
            jax.ShapeDtypeStruct((1, hidden), F32),
            jax.ShapeDtypeStruct((width, width), F32),
            jax.ShapeDtypeStruct((1, width), F32),
        ],
        cost_estimate=pl.CostEstimate(flops=seqs * rows * width * (12 * hidden + 6 * width) * 2,
                                      bytes_accessed=16 << 20, transcendentals=seqs * rows * hidden),
        compiler_params=pltpu.CompilerParams(vmem_limit_bytes=VMEM_LIMIT),
        name="feed_forward",
    )(tok, row, att, cot, w_out, b_out, w_in, b_in, w_last, b_last)


def body(
    tokens,
    pair_ids,
    lengths,
    pair_embed,
    qkv_weight,
    q_bias,
    v_bias,
    out_weight,
    out_bias,
    ffn_in_weight,
    ffn_in_bias,
    ffn_out_weight,
    ffn_out_bias,
    cotangent,
):
    local_rows, seqs, width = tokens.shape
    table_rows = pair_embed.shape[0]
    place = lax.axis_index("mp").astype(jnp.int32).reshape(1)
    tok = jnp.transpose(tokens, (1, 0, 2))
    cot = jnp.transpose(cotangent, (1, 0, 2))
    select = (pair_ids[:, None] == lax.iota(jnp.int32, table_rows)[None, :]).astype(F32)
    embed_rows = jnp.dot(select, pair_embed, precision=HIGHEST)
    low = [(tok[s].astype(F32) + embed_rows[s][None]).astype(BF16) for s in range(seqs)]
    gather = lambda v: lax.all_gather(v, "mp", axis=0, tiled=True)

    x_all = [gather(low[s]) for s in range(seqs)]
    w_all = gather(qkv_weight.T)
    qb_all = gather(q_bias)
    vb_all = gather(v_bias)
    out_w_all = gather(out_weight)
    pairs = w_all.shape[0] // (3 * PAIR)
    w_pairs = jnp.transpose(
        w_all.reshape(pairs, 2, 3, HD, width), (0, 4, 2, 1, 3)
    ).reshape(pairs, width, 3 * PAIR)
    qb_pairs = qb_all.astype(F32).reshape(pairs, 1, PAIR)
    vb_pairs = vb_all.astype(F32).reshape(pairs, 1, PAIR)

    fwd = [
        call_forward(lengths[s:s + 1], x_all[s], low[s], w_pairs, qb_pairs, vb_pairs)
        for s in range(seqs)
    ]
    att = jnp.stack([f[3] for f in fwd])
    result, mixed_grad, att_grad, g_last, gb_last, g_in, gb_in, g_out, gb_out = call_feed(
        tok, embed_rows[:, None, :], att, cot, out_w_all, out_bias[None], ffn_in_weight,
        ffn_in_bias[None], ffn_out_weight, ffn_out_bias[None])
    g_last_sum, g_in_sum = lax.psum((g_last.astype(BF16), g_in.astype(BF16)), ("dp", "mp"))
    g_out_own = lax.psum(
        lax.psum_scatter(g_out.astype(BF16), "mp", scatter_dimension=0, tiled=True), "dp")

    token_grads, w_grads, qb_grads, vb_grads = [], [], [], []
    for s in range(seqs):
        q, k, v, _, att_t, lse = fwd[s]
        x_grad, w_grad, qb, vb = call_backward(
            lengths[s:s + 1], place, x_all[s], low[s], w_pairs, q, k, v, att_t, lse, att_grad[s])
        own = lax.psum_scatter(x_grad, "mp", scatter_dimension=0, tiled=True)
        token_grads.append(mixed_grad[s].astype(F32) + own.astype(F32))
        w_grads.append(w_grad)
        qb_grads.append(qb[:, 0])
        vb_grads.append(vb[:, 0])

    w_grad = sum(w_grads).astype(BF16).reshape(pairs, 3, 2, HD, width)
    w_grad = jnp.transpose(w_grad, (0, 2, 1, 3, 4)).reshape(pairs * 2 * 3 * HD, width)
    w_grad = lax.psum(lax.psum_scatter(w_grad, "mp", scatter_dimension=0, tiled=True), "dp")
    qkv_sum = w_grad.astype(F32).T
    seq_sums = jnp.stack([jnp.sum(t, axis=0) for t in token_grads])
    table_grad = lax.dot_general(select, seq_sums, (((0,), (0,)), ((), ())), precision=HIGHEST)
    small = jnp.concatenate([
        table_grad.reshape(-1), sum(qb_grads).reshape(-1), sum(vb_grads).reshape(-1),
        gb_out.reshape(-1), gb_in.reshape(-1), gb_last.reshape(-1)])
    small = lax.psum(small, ("dp", "mp"))
    sizes = [table_grad.size, width, width, width, gb_in.size, width]
    parts, at = [], 0
    for size in sizes:
        parts.append(small[at:at + size])
        at += size
    table_sum, qb_sum, vb_sum, out_bias_sum, in_bias_sum, last_bias_sum = parts
    bias_len = q_bias.shape[0]
    qb_own = lax.dynamic_slice_in_dim(qb_sum, place[0] * bias_len, bias_len)
    vb_own = lax.dynamic_slice_in_dim(vb_sum, place[0] * bias_len, bias_len)
    tokens_grad = jnp.transpose(jnp.stack(token_grads), (1, 0, 2))
    return (
        jnp.transpose(result, (1, 0, 2)),
        tokens_grad,
        table_sum.reshape(table_rows, width),
        qkv_sum,
        qb_own,
        vb_own,
        g_out_own.astype(F32),
        out_bias_sum,
        g_in_sum.astype(F32),
        in_bias_sum,
        g_last_sum.astype(F32),
        last_bias_sum,
    )


def solution(mesh):
    return jax.shard_map(
        body,
        mesh=mesh,
        in_specs=(
            P("mp", "dp", None),
            P("dp"),
            P("dp"),
            P(),
            P(None, "mp"),
            P("mp"),
            P("mp"),
            P("mp", None),
            P(),
            P(),
            P(),
            P(),
            P(),
            P("mp", "dp", None),
        ),
        out_specs=(
            P("mp", "dp", None),
            P("mp", "dp", None),
            P(),
            P(None, "mp"),
            P("mp"),
            P("mp"),
            P("mp", None),
            P(),
            P(),
            P(),
            P(),
            P(),
        ),
        check_vma=False,
    )
```

```python
import functools
import math

import jax
import jax.numpy as jnp
from jax import lax
from jax.experimental import pallas as pl
from jax.experimental.pallas import tpu as pltpu
from jax.sharding import PartitionSpec as P

HD = 64
PAIR = 2 * HD
HIGHEST = lax.Precision.HIGHEST
NEGATIVE = -1e30
LOG2E = math.log2(math.e)
F32 = jnp.float32
BF16 = jnp.bfloat16
VMEM_LIMIT = 56 * 1024 * 1024


def nn(a, b):
    return jnp.dot(a, b, preferred_element_type=F32)


def nt(a, b):
    return lax.dot_general(a, b, (((1,), (1,)), ((), ())), preferred_element_type=F32)


def tn(a, b):
    return lax.dot_general(a, b, (((0,), (0,)), ((), ())), preferred_element_type=F32)


def head_lanes(rows, head):
    lane = lax.broadcasted_iota(jnp.int32, (rows, PAIR), 1)
    return (lane >= head * HD) & (lane < (head + 1) * HD)


def one_head(pair_rows, head):
    return jnp.where(head_lanes(pair_rows.shape[0], head), pair_rows, jnp.zeros_like(pair_rows))


def fold8(values, op):
    rows, lanes = values.shape
    return op(values.reshape(rows // 8, 8, lanes), axis=0)


def attend_backward(length_ref, place_ref, x_all, x_own, weight, q_in, k_in, v_in, att_t, lse, grad_in,
                    x_grad, w_grad, qb_grad, vb_grad, x_acc, kv_grad, dq_acc, *, block):
    length = length_ref[0]
    blocks = (length + block - 1) // block
    rows = x_own.shape[0]
    pair = pl.program_id(0)
    full = x_all.shape[0]
    q_pair = q_in[0]
    grad_pair = grad_in[...]
    q_heads = [one_head(q_pair, h) for h in range(2)]
    g_heads = [one_head(grad_pair, h) for h in range(2)]
    prod = grad_pair.astype(F32).T * att_t[0]
    delta = [jnp.sum(prod[h * HD:(h + 1) * HD], axis=0, keepdims=True) for h in range(2)]
    tops = [lse[0, h:h + 1, :] for h in range(2)]
    dq_acc[...] = jnp.zeros_like(dq_acc)

    @pl.when(pair == 0)
    def _():
        x_acc[...] = jnp.zeros_like(x_acc)

    w_grad[0] = jnp.zeros(w_grad.shape[1:], F32)

    def step(j, vsum):
        at = pl.ds(pl.multiple_of(j * block, block), block)
        k_blk = k_in[0, at, :]
        v_blk = v_in[0, at, :]
        keep = (lax.broadcasted_iota(jnp.int32, (block, rows), 0) + j * block) < length
        dk = jnp.zeros((block, PAIR), F32)
        dv = jnp.zeros((block, PAIR), F32)
        for h in range(2):
            s = nt(k_blk, q_heads[h]) * LOG2E
            p = jnp.where(keep, jnp.exp2(s - tops[h]), 0.0)
            dp = nt(v_blk, g_heads[h])
            ds = (p * (dp - delta[h])).astype(BF16)
            dv += nn(p.astype(BF16), g_heads[h])
            dk += nn(ds, q_heads[h])
            dq_acc[h] += tn(k_blk, ds)
        dv = dv.astype(BF16)
        both = jnp.concatenate([dk.astype(BF16), dv], axis=1)
        x_acc[at, :] += nn(both, weight[0, PAIR:, :])
        w_grad[0, PAIR:, :] += tn(both, x_all[at, :])
        return vsum + fold8(dv.astype(F32), jnp.sum)

    vsum = lax.fori_loop(0, blocks, step, jnp.zeros((8, PAIR), F32))
    vb_grad[0] = jnp.broadcast_to(jnp.sum(vsum, axis=0, keepdims=True), (8, PAIR))
    dq_t = jnp.concatenate([dq_acc[h, h * HD:(h + 1) * HD, :] for h in range(2)], axis=0) * (HD ** -0.5)
    dq = dq_t.T.astype(BF16)
    qb_grad[0] = jnp.broadcast_to(jnp.sum(dq.astype(F32), axis=0, keepdims=True), (8, PAIR))
    mine = pl.ds(pl.multiple_of(place_ref[0] * rows, rows), rows)
    x_acc[mine, :] += nn(dq, weight[0, :PAIR, :])
    w_grad[0, :PAIR, :] += tn(dq, x_own[...])

    @pl.when(pair == pl.num_programs(0) - 1)
    def _():
        x_grad[...] = x_acc[...].astype(BF16)


def whole(shape):
    return pl.BlockSpec(shape, lambda *_: (0,) * len(shape))


MESH = pl.DeviceIdType.MESH
CONSTANT = pl.Buffered(1)
PIECES = 8


class Relay:
    def __init__(self, place, count, view, send_sem, recv_sem):
        self.place, self.count, self.view = place, count, view
        self.send_sem, self.recv_sem = send_sem, recv_sem

    def copy(self, chunk, downward, step):
        return pltpu.make_async_remote_copy(
            src_ref=self.view(chunk), dst_ref=self.view(chunk),
            send_sem=self.send_sem(downward, step), recv_sem=self.recv_sem(chunk),
            device_id={"mp": self.place - 1 if downward else self.place + 1},
            device_id_type=MESH)

    def each(self, step):
        for downward in (0, 1):
            chunk = self.place + step if downward else self.place - step
            exists = chunk < self.count if downward else chunk >= 0
            onward = self.place >= 1 if downward else self.place + 1 < self.count
            yield downward, chunk, exists, onward

    def advance(self, step):
        for downward, chunk, exists, onward in self.each(step):
            if step:
                @pl.when(exists)
                def _():
                    self.copy(chunk, downward, step).wait_recv()
            if step < self.count - 1:
                @pl.when(exists & onward)
                def _():
                    self.copy(chunk, downward, step).start()

    def drain(self):
        for step in range(self.count - 1):
            for downward, chunk, exists, onward in self.each(step):
                @pl.when(exists & onward)
                def _():
                    self.copy(chunk, downward, step).wait_send()


def greet(place, count, partners):
    barrier = pltpu.get_barrier_semaphore()
    for partner in partners:
        pl.semaphore_signal(barrier, 1, device_id={"dp": partner}, device_id_type=MESH)
    for k in range(1, count):
        pl.semaphore_signal(barrier, 1, device_id={"mp": (place + k) % count}, device_id_type=MESH)


def await_greetings(count, partners):
    pl.semaphore_wait(pltpu.get_barrier_semaphore(), len(partners) + count - 1)


def flip(index, bit):
    return index + bit - 2 * bit * ((index // bit) % 2)


def forward_layer(count, heads_dev, block,
                  lengths, pair_ids, tok, embed, cot, qkv_w, q_bias, v_bias, out_w, b_out,
                  w_in, b_in, w_last, b_last,
                  x_out, w_out, q_out, k_out, v_out, att_t_out, lse_out,
                  result, mixed_grad, att_grad, g_all, g_bias,
                  x_all, w_all, w_o, biases, s_all, acc, att_rows_all, grads, grad_rows,
                  x_send, x_recv, x_copy, w_send, w_recv, plane_send, plane_recv):
    seq, pair = pl.program_id(0), pl.program_id(1)
    seqs, pairs = tok.shape[0], w_out.shape[0]
    rows, width = tok.shape[1], tok.shape[2]
    full = count * rows
    hidden = w_in.shape[1]
    base = heads_dev * 4 * HD
    piece_rows = w_all.shape[1] // PIECES
    place, data_at = lax.axis_index("mp"), lax.axis_index("dp")
    last_step = (seq == seqs - 1) & (pair == pairs - 1)

    def x_relay(s):
        return Relay(
            place, count,
            lambda chunk: x_all.at[s, pl.ds(pl.multiple_of(chunk * rows, rows), rows)],
            lambda downward, step: x_send.at[s, downward * (count - 1) + step],
            lambda chunk: x_recv.at[s, chunk])

    low_bits = [(data_at // bit) % 2 for bit in (4, 2, 1)]
    piece = low_bits[0] + 2 * low_bits[1] + 4 * low_bits[2]

    def w_span(start, size):
        return pl.ds(pl.multiple_of(start * piece_rows, piece_rows), size * piece_rows)

    w_relay = Relay(
        place, count, lambda chunk: w_all.at[chunk, w_span(piece, 1)],
        lambda downward, step: w_send.at[downward * (count - 1) + step],
        lambda chunk: w_recv.at[chunk])
    partners = [flip(data_at, bit) for bit in (4, 2, 1)]
    spans = [w_span(piece, 1), w_span(2 * low_bits[1] + 4 * low_bits[2], 2), w_span(4 * low_bits[2], 4)]

    def plane(stage):
        copies = []
        for k in range(1, count):
            source = (place + k) % count
            copies.append(pltpu.make_async_remote_copy(
                src_ref=w_all.at[source, spans[stage]], dst_ref=w_all.at[source, spans[stage]],
                send_sem=plane_send.at[stage, k - 1], recv_sem=plane_recv.at[stage, k - 1],
                device_id={"dp": partners[stage]}, device_id_type=MESH))
        return copies

    def plane_start(stage):
        for copy in plane(stage):
            copy.start()

    def plane_wait(stage):
        for copy in plane(stage):
            copy.wait()

    @pl.when((seq == 0) & (pair == 0))
    def _():
        greet(place, count, partners)
        turned = qkv_w[...].T
        parts = []
        for j in range(3):
            for h in range(heads_dev):
                parts.append(turned[(h * 3 + j) * HD:(h * 3 + j + 1) * HD])
        w_all[place, 0:heads_dev * 3 * HD, :] = jnp.concatenate(parts, axis=0)
        w_all[place, heads_dev * 3 * HD:base, :] = out_w[...]
        first = lax.broadcasted_iota(jnp.int32, (w_all.shape[1] - base, width), 0)
        w_all[place, base:, :] = jnp.where(
            first == 0, q_bias[...].astype(F32),
            jnp.where(first == 1, v_bias[...].astype(F32), 0.0)).astype(BF16)
        for s in range(seqs):
            row = embed[pl.ds(pair_ids[s], 1), :]
            own = pl.ds(pl.multiple_of(place * rows, rows), rows)
            x_all[s, own, :] = (tok[s].astype(F32) + row).astype(BF16)
        await_greetings(count, partners)
        w_relay.advance(0)
        if count > 2:
            w_relay.advance(1)
        x_relay(0).advance(0)
        for step in range(2 if count > 2 else 1, count):
            w_relay.advance(step)
        plane_start(0)
        plane_wait(0)
        plane_start(1)
        if count > 2:
            x_relay(0).advance(1)
        plane_wait(1)
        plane_start(2)
        for step in range(2, count - 1):
            x_relay(0).advance(step)
        grads[...] = jnp.zeros_like(grads)
        grad_rows[...] = jnp.zeros_like(grad_rows)
        plane_wait(2)
        w_relay.drain()
        total = jnp.zeros((16, width), F32)
        for m in range(count):
            total += w_all[m, base:base + 16, :].astype(F32)
        biases[...] = total
        for p in range(pairs):
            if heads_dev == 2:
                w_out[p] = w_all[p, 0:3 * PAIR, :]
                w_o[p * PAIR:(p + 1) * PAIR, :] = w_all[p, 3 * PAIR:4 * PAIR, :]
            else:
                for half in range(2):
                    for j in range(4):
                        strip = w_all[2 * p + half, j * HD:(j + 1) * HD, :]
                        if j < 3:
                            w_out[p, j * PAIR + half * HD:j * PAIR + (half + 1) * HD, :] = strip
                        else:
                            w_o[p * PAIR + half * HD:p * PAIR + (half + 1) * HD, :] = strip

    def hbm_copy(s):
        return pltpu.make_async_copy(x_all.at[s], x_out.at[s], x_copy.at[s])

    @pl.when(pair == 0)
    def _():
        x_relay(seq).advance(count - 1)

        @pl.when(seq + 1 < seqs)
        def _():
            x_relay(seq + 1).advance(0)
        hbm_copy(seq).start()

    length = lengths[seq]
    lanes = pl.ds(pl.multiple_of(pair * PAIR, PAIR), PAIR)
    own = pl.ds(pl.multiple_of(place * rows, rows), rows)
    q_pair = (nt(x_all[seq, own, :], w_out[pair, 0:PAIR, :]) + biases[0:1, lanes]).astype(BF16)
    q_pair = q_pair * BF16(HD ** -0.5)
    q_out[0, 0] = q_pair
    q_heads = [one_head(q_pair, 0), one_head(q_pair, 1)]
    v_row = biases[1:2, lanes]

    def score_step(j, tops):
        at = pl.ds(pl.multiple_of(j * block, block), block)
        kv = nt(x_all[seq, at, :], w_out[pair, PAIR:3 * PAIR, :])
        k_blk = kv[:, :PAIR].astype(BF16)
        k_out[0, 0, at, :] = k_blk
        v_out[0, 0, at, :] = (kv[:, PAIR:] + v_row).astype(BF16)
        keep = (lax.broadcasted_iota(jnp.int32, (block, rows), 0) + j * block) < length
        new = []
        for h in range(2):
            s = nt(k_blk, q_heads[h]) * LOG2E
            s = jnp.where(keep, s, NEGATIVE)
            s_all[h, at, :] = s
            new.append(jnp.maximum(tops[h], fold8(s, jnp.max)))
        return tuple(new)

    start = jnp.full((8, rows), NEGATIVE, F32)
    tops = lax.fori_loop(0, full // block, score_step, (start, start))
    tops = [jnp.max(t, axis=0, keepdims=True) for t in tops]
    acc[...] = jnp.zeros_like(acc)

    def value_step(j, sums):
        at = pl.ds(pl.multiple_of(j * block, block), block)
        v_blk = v_out[0, 0, at, :]
        new = []
        for h in range(2):
            p = jnp.exp2(s_all[h, at, :] - tops[h])
            new.append(sums[h] + fold8(p, jnp.sum))
            acc[h] += tn(v_blk, p.astype(BF16))
        return tuple(new)

    zero = jnp.zeros((8, rows), F32)
    sums = lax.fori_loop(0, full // block, value_step, (zero, zero))
    sums = [jnp.sum(t, axis=0, keepdims=True) for t in sums]
    att_t = jnp.concatenate([acc[h, h * HD:(h + 1) * HD, :] * (1.0 / sums[h]) for h in range(2)], axis=0)
    att_t_out[0, 0] = att_t
    att_rows_all[:, lanes] = att_t.T.astype(BF16)
    lse_out[0, 0] = jnp.concatenate(
        [tops[h] + jnp.log2(sums[h]) for h in range(2)] + [jnp.zeros((6, rows), F32)], axis=0)

    for step in range(1, count - 1):
        after = max(0, (step * pairs) // (count - 2) - 1)

        @pl.when((pair == after) & (seq + 1 < seqs))
        def _():
            x_relay(seq + 1).advance(step)

    @pl.when(pair == pairs - 1)
    def _():
        cot_rows = cot[0]
        att_rows = att_rows_all[...]
        row = embed[pl.ds(pair_ids[seq], 1), :]
        mixed = (tok[seq].astype(F32) + row) + (nn(att_rows, w_o[...]) + b_out[...])
        mixed_low = mixed.astype(BF16)
        out_sum = mixed + b_last[...]
        back_sum = cot_rows.astype(F32)
        root = math.sqrt(2.0 / math.pi)
        for c in range(hidden // width):
            at = slice(c * width, (c + 1) * width)
            pre = nn(mixed_low, w_in[:, at]) + b_in[:, at]
            square = pre * pre
            th = jnp.tanh(root * pre * (1.0 + 0.044715 * square))
            half = 0.5 * (1.0 + th)
            act = (pre * half).astype(BF16)
            slope = half + (0.5 * root) * pre * (1.0 - th * th) * (1.0 + (3 * 0.044715) * square)
            out_sum += nn(act, w_last[at, :])
            back = (nt(cot_rows, w_last[at, :]) * slope).astype(BF16)
            grad_rows[c:c + 1, :] += jnp.sum(back.astype(F32), axis=0, keepdims=True)
            back_sum += nt(back, w_in[:, at])
            grads[at, :] += tn(act, cot_rows)
            grads[hidden + c * width:hidden + (c + 1) * width, :] += tn(mixed_low, back)
        result[0] = out_sum.astype(BF16)
        back_low = back_sum.astype(BF16)
        mixed_grad[0] = back_low
        at = hidden // width
        grad_rows[at:at + 1, :] += jnp.sum(cot_rows.astype(F32), axis=0, keepdims=True)
        grad_rows[at + 1:at + 2, :] += jnp.sum(back_low.astype(F32), axis=0, keepdims=True)
        grads[2 * hidden:, :] += tn(att_rows, back_low)
        att_grad[0] = nt(back_low, w_o[...]).astype(BF16)

    @pl.when(last_step)
    def _():
        def narrow(j, _):
            at = pl.ds(pl.multiple_of(j * width, width), width)
            g_all[at, :] = grads[at, :].astype(BF16)
            return 0

        lax.fori_loop(0, grads.shape[0] // width, narrow, 0)
        g_bias[...] = grad_rows[...]
        for s in range(seqs):
            x_relay(s).drain()
            hbm_copy(s).wait()


def fixed(shape):
    return pl.BlockSpec(shape, lambda *_: (0,) * len(shape), pipeline_mode=CONSTANT)


def call_layer(count, lengths, pair_ids, tok, embed, cot, qkv_w, q_bias, v_bias, out_w, b_out,
               w_in, b_in, w_last, b_last):
    seqs, rows, width = tok.shape
    hidden = w_in.shape[1]
    heads_dev = qkv_w.shape[1] // (3 * HD)
    full = count * rows
    pairs = width // PAIR
    block = min(512, full)
    w_rows = -(-(heads_dev * 4 * HD + 16) // (16 * PIECES)) * 16 * PIECES
    in_smem = pl.BlockSpec(memory_space=pltpu.SMEM)
    per_seq = lambda: pl.BlockSpec((1, rows, width), lambda s, p: (s, 0, 0))
    per_pair = lambda *tail: pl.BlockSpec((1, 1) + tail, lambda s, p: (s, p, 0, 0))
    shape = jax.ShapeDtypeStruct
    return pl.pallas_call(
        functools.partial(forward_layer, count, heads_dev, block),
        grid=(seqs, pairs),
        in_specs=[in_smem, in_smem, fixed(tok.shape), fixed(embed.shape), per_seq(), fixed(qkv_w.shape),
                  fixed(q_bias.shape), fixed(v_bias.shape), fixed(out_w.shape), fixed(b_out.shape),
                  fixed(w_in.shape), fixed(b_in.shape), fixed(w_last.shape), fixed(b_last.shape)],
        out_specs=[pl.BlockSpec(memory_space=pl.ANY), fixed((pairs, 3 * PAIR, width)),
                   per_pair(rows, PAIR), per_pair(full, PAIR), per_pair(full, PAIR),
                   per_pair(PAIR, rows), per_pair(8, rows),
                   per_seq(), per_seq(), per_seq(), fixed((2 * hidden + width, width)), fixed((8, width))],
        out_shape=[
            shape((seqs, full, width), BF16),
            shape((pairs, 3 * PAIR, width), BF16),
            shape((seqs, pairs, rows, PAIR), BF16),
            shape((seqs, pairs, full, PAIR), BF16),
            shape((seqs, pairs, full, PAIR), BF16),
            shape((seqs, pairs, PAIR, rows), F32),
            shape((seqs, pairs, 8, rows), F32),
            shape((seqs, rows, width), BF16),
            shape((seqs, rows, width), BF16),
            shape((seqs, rows, width), BF16),
            shape((2 * hidden + width, width), BF16),
            shape((8, width), F32),
        ],
        scratch_shapes=[
            pltpu.VMEM((seqs, full, width), BF16),
            pltpu.VMEM((count, w_rows, width), BF16),
            pltpu.VMEM((width, width), BF16),
            pltpu.VMEM((16, width), F32),
            pltpu.VMEM((2, full, rows), F32),
            pltpu.VMEM((2, PAIR, rows), F32),
            pltpu.VMEM((rows, width), BF16),
            pltpu.VMEM((2 * hidden + width, width), F32),
            pltpu.VMEM((8, width), F32),
            pltpu.SemaphoreType.DMA((seqs, 2 * (count - 1))),
            pltpu.SemaphoreType.DMA((seqs, count)),
            pltpu.SemaphoreType.DMA((seqs,)),
            pltpu.SemaphoreType.DMA((2 * (count - 1),)),
            pltpu.SemaphoreType.DMA((count,)),
            pltpu.SemaphoreType.DMA((3, count - 1)),
            pltpu.SemaphoreType.DMA((3, count - 1)),
        ],
        cost_estimate=pl.CostEstimate(flops=120 * 10 ** 9, bytes_accessed=60 << 20,
                                      transcendentals=seqs * pairs * 2 * full * rows),
        compiler_params=pltpu.CompilerParams(
            collective_id=0, has_side_effects=True, vmem_limit_bytes=VMEM_LIMIT),
        name="forward_layer",
    )(lengths, pair_ids, tok, embed, cot, qkv_w, q_bias, v_bias, out_w, b_out, w_in, b_in, w_last, b_last)


def call_backward(length, place, x_all, x_own, weight, q, k, v, att_t, lse, grad):
    full, width = x_all.shape
    rows = x_own.shape[0]
    pairs = weight.shape[0]
    block = min(512, full)
    per_pair = lambda *tail: pl.BlockSpec((1,) + tail, lambda p, *_: (p, 0, 0))
    return pl.pallas_call(
        functools.partial(attend_backward, block=block),
        grid_spec=pltpu.PrefetchScalarGridSpec(
            num_scalar_prefetch=2,
            grid=(pairs,),
            in_specs=[whole((full, width)), whole((rows, width)), per_pair(3 * PAIR, width),
                      per_pair(rows, PAIR), per_pair(full, PAIR), per_pair(full, PAIR),
                      per_pair(PAIR, rows), per_pair(8, rows),
                      pl.BlockSpec((rows, PAIR), lambda p, *_: (0, p))],
            out_specs=[whole((full, width)), per_pair(3 * PAIR, width), per_pair(8, PAIR), per_pair(8, PAIR)],
            scratch_shapes=[pltpu.VMEM((full, width), F32), pltpu.VMEM((full, 2 * PAIR), BF16),
                            pltpu.VMEM((2, PAIR, rows), F32)],
        ),
        out_shape=[
            jax.ShapeDtypeStruct((full, width), BF16),
            jax.ShapeDtypeStruct((pairs, 3 * PAIR, width), F32),
            jax.ShapeDtypeStruct((pairs, 8, PAIR), F32),
            jax.ShapeDtypeStruct((pairs, 8, PAIR), F32),
        ],
        cost_estimate=pl.CostEstimate(flops=40 * pairs * full * rows * PAIR, bytes_accessed=16 << 20,
                                      transcendentals=2 * pairs * full * rows),
        compiler_params=pltpu.CompilerParams(vmem_limit_bytes=VMEM_LIMIT),
        name="attend_backward",
    )(length, place, x_all, x_own, weight, q, k, v, att_t, lse, grad)


def body(
    tokens,
    pair_ids,
    lengths,
    pair_embed,
    qkv_weight,
    q_bias,
    v_bias,
    out_weight,
    out_bias,
    ffn_in_weight,
    ffn_in_bias,
    ffn_out_weight,
    ffn_out_bias,
    cotangent,
):
    local_rows, seqs, width = tokens.shape
    table_rows = pair_embed.shape[0]
    count = lax.axis_size("mp")
    place = lax.axis_index("mp").astype(jnp.int32).reshape(1)
    tok = jnp.transpose(tokens, (1, 0, 2))
    cot = jnp.transpose(cotangent, (1, 0, 2))
    select = (pair_ids[:, None] == lax.iota(jnp.int32, table_rows)[None, :]).astype(F32)
    bias_len = q_bias.shape[0]
    spread = lambda v: lax.dynamic_update_slice(
        jnp.zeros((1, width), BF16), v[None], (0, place[0] * bias_len))
    (x_all, w_pairs, q, k, v, att_t, lse, result, mixed_grad, att_grad, g_all, g_bias) = call_layer(
        count, lengths, pair_ids, tok, pair_embed, cot, qkv_weight, spread(q_bias), spread(v_bias),
        out_weight, out_bias[None], ffn_in_weight, ffn_in_bias[None], ffn_out_weight,
        ffn_out_bias[None])
    hidden = ffn_in_weight.shape[1]
    pairs = w_pairs.shape[0]
    g_sum = lax.psum(g_all, ("dp", "mp"))
    g_last_sum = g_sum[:hidden]
    g_in_sum = jnp.transpose(
        g_sum[hidden:2 * hidden].reshape(hidden // width, width, width), (1, 0, 2)).reshape(width, hidden)
    out_rows = out_weight.shape[0]
    g_out_own = lax.dynamic_slice_in_dim(g_sum, 2 * hidden + place[0] * out_rows, out_rows)
    at = hidden // width
    gb_in, gb_last, gb_out = g_bias[:at].reshape(-1), g_bias[at], g_bias[at + 1]

    token_grads, w_grads, qb_grads, vb_grads = [], [], [], []
    for s in range(seqs):
        x_grad, w_grad, qb, vb = call_backward(
            lengths[s:s + 1], place, x_all[s],
            lax.dynamic_slice_in_dim(x_all[s], place[0] * local_rows, local_rows),
            w_pairs, q[s], k[s], v[s], att_t[s], lse[s], att_grad[s])
        own = lax.psum_scatter(x_grad, "mp", scatter_dimension=0, tiled=True)
        token_grads.append(mixed_grad[s].astype(F32) + own.astype(F32))
        w_grads.append(w_grad)
        qb_grads.append(qb[:, 0])
        vb_grads.append(vb[:, 0])

    w_grad = sum(w_grads).astype(BF16).reshape(pairs, 3, 2, HD, width)
    w_grad = jnp.transpose(w_grad, (0, 2, 1, 3, 4)).reshape(pairs * 2 * 3 * HD, width)
    w_grad = lax.psum(lax.psum_scatter(w_grad, "mp", scatter_dimension=0, tiled=True), "dp")
    qkv_sum = w_grad.astype(F32).T
    seq_sums = jnp.stack([jnp.sum(t, axis=0) for t in token_grads])
    table_grad = lax.dot_general(select, seq_sums, (((0,), (0,)), ((), ())), precision=HIGHEST)
    small = jnp.concatenate([
        table_grad.reshape(-1), sum(qb_grads).reshape(-1), sum(vb_grads).reshape(-1),
        gb_out.reshape(-1), gb_in.reshape(-1), gb_last.reshape(-1)])
    small = lax.psum(small, ("dp", "mp"))
    sizes = [table_grad.size, width, width, width, gb_in.size, width]
    parts, at = [], 0
    for size in sizes:
        parts.append(small[at:at + size])
        at += size
    table_sum, qb_sum, vb_sum, out_bias_sum, in_bias_sum, last_bias_sum = parts
    qb_own = lax.dynamic_slice_in_dim(qb_sum, place[0] * bias_len, bias_len)
    vb_own = lax.dynamic_slice_in_dim(vb_sum, place[0] * bias_len, bias_len)
    tokens_grad = jnp.transpose(jnp.stack(token_grads), (1, 0, 2))
    return (
        jnp.transpose(result, (1, 0, 2)),
        tokens_grad,
        table_sum.reshape(table_rows, width),
        qkv_sum,
        qb_own,
        vb_own,
        g_out_own.astype(F32),
        out_bias_sum,
        g_in_sum.astype(F32),
        in_bias_sum,
        g_last_sum.astype(F32),
        last_bias_sum,
    )


def solution(mesh):
    return jax.shard_map(
        body,
        mesh=mesh,
        in_specs=(
            P("mp", "dp", None),
            P("dp"),
            P("dp"),
            P(),
            P(None, "mp"),
            P("mp"),
            P("mp"),
            P("mp", None),
            P(),
            P(),
            P(),
            P(),
            P(),
            P("mp", "dp", None),
        ),
        out_specs=(
            P("mp", "dp", None),
            P("mp", "dp", None),
            P(),
            P(None, "mp"),
            P("mp"),
            P("mp"),
            P("mp", None),
            P(),
            P(),
            P(),
            P(),
            P(),
        ),
        check_vma=False,
    )
```

```python
import functools
import math

import jax
import jax.numpy as jnp
from jax import lax
from jax.experimental import pallas as pl
from jax.experimental.pallas import tpu as pltpu
from jax.sharding import PartitionSpec as P

HD = 64
PAIR = 2 * HD
NEGATIVE = -1e30
LOG2E = math.log2(math.e)
F32 = jnp.float32
BF16 = jnp.bfloat16
VMEM_LIMIT = 56 * 1024 * 1024


def nn(a, b):
    return jnp.dot(a, b, preferred_element_type=F32)


def nt(a, b):
    return lax.dot_general(a, b, (((1,), (1,)), ((), ())), preferred_element_type=F32)


def tn(a, b):
    return lax.dot_general(a, b, (((0,), (0,)), ((), ())), preferred_element_type=F32)


def head_lanes(rows, head):
    lane = lax.broadcasted_iota(jnp.int32, (rows, PAIR), 1)
    return (lane >= head * HD) & (lane < (head + 1) * HD)


def one_head(pair_rows, head):
    return jnp.where(head_lanes(pair_rows.shape[0], head), pair_rows, jnp.zeros_like(pair_rows))


def fold8(values, op):
    rows, lanes = values.shape
    return op(values.reshape(rows // 8, 8, lanes), axis=0)


MESH = pl.DeviceIdType.MESH
CONSTANT = pl.Buffered(1)
PIECES = 8
TAIL_POINTS = (0, 2, 3, 4, 6, 7, 8, 9, 11, 12)


class Relay:
    def __init__(self, place, count, view, send_sem, recv_sem):
        self.place, self.count, self.view = place, count, view
        self.send_sem, self.recv_sem = send_sem, recv_sem

    def copy(self, chunk, downward, step):
        return pltpu.make_async_remote_copy(
            src_ref=self.view(chunk), dst_ref=self.view(chunk),
            send_sem=self.send_sem(downward, step), recv_sem=self.recv_sem(chunk),
            device_id={"mp": self.place - 1 if downward else self.place + 1},
            device_id_type=MESH)

    def each(self, step):
        for downward in (0, 1):
            chunk = self.place + step if downward else self.place - step
            exists = chunk < self.count if downward else chunk >= 0
            onward = self.place >= 1 if downward else self.place + 1 < self.count
            yield downward, chunk, exists, onward

    def advance(self, step):
        for downward, chunk, exists, onward in self.each(step):
            if step:
                @pl.when(exists)
                def _():
                    self.copy(chunk, downward, step).wait_recv()
            if step < self.count - 1:
                @pl.when(exists & onward)
                def _():
                    self.copy(chunk, downward, step).start()

    def drain(self):
        for step in range(self.count - 1):
            for downward, chunk, exists, onward in self.each(step):
                @pl.when(exists & onward)
                def _():
                    self.copy(chunk, downward, step).wait_send()


def greet(place, count, partners):
    barrier = pltpu.get_barrier_semaphore()
    for partner in partners:
        pl.semaphore_signal(barrier, 1, device_id={"dp": partner}, device_id_type=MESH)
    for k in range(1, count):
        pl.semaphore_signal(barrier, 1, device_id={"mp": (place + k) % count}, device_id_type=MESH)


def await_greetings(count, partners):
    pl.semaphore_wait(pltpu.get_barrier_semaphore(), len(partners) + count - 1)


def flip(index, bit):
    return index + bit - 2 * bit * ((index // bit) % 2)


def forward_layer(count, heads_dev, block,
                  lengths, pair_ids, tok, embed, cot, qkv_w, q_bias, v_bias, out_w, b_out,
                  w_in, b_in, w_last, b_last,
                  x_out, w_out, q_out, k_out, v_out, att_t_out, lse_out,
                  result, mixed_grad, att_grad, g_all,
                  x_all, w_all, w_o, biases, s_all, acc, att_rows_all, grads, grad_rows,
                  x_send, x_recv, x_copy, w_send, w_recv, plane_send, plane_recv):
    seq, pair = pl.program_id(0), pl.program_id(1)
    seqs, pairs = tok.shape[0], w_out.shape[0]
    rows, width = tok.shape[1], tok.shape[2]
    full = count * rows
    hidden = w_in.shape[1]
    base = heads_dev * 4 * HD
    piece_rows = w_all.shape[1] // PIECES
    place, data_at = lax.axis_index("mp"), lax.axis_index("dp")
    last_step = (seq == seqs - 1) & (pair == pairs - 1)

    def x_relay(s):
        return Relay(
            place, count,
            lambda chunk: x_all.at[s, pl.ds(pl.multiple_of(chunk * rows, rows), rows)],
            lambda downward, step: x_send.at[s, downward * (count - 1) + step],
            lambda chunk: x_recv.at[s, chunk])

    low_bits = [(data_at // bit) % 2 for bit in (4, 2, 1)]
    piece = low_bits[0] + 2 * low_bits[1] + 4 * low_bits[2]

    def w_span(start, size):
        return pl.ds(pl.multiple_of(start * piece_rows, piece_rows), size * piece_rows)

    w_relay = Relay(
        place, count, lambda chunk: w_all.at[chunk, w_span(piece, 1)],
        lambda downward, step: w_send.at[downward * (count - 1) + step],
        lambda chunk: w_recv.at[chunk])
    partners = [flip(data_at, bit) for bit in (4, 2, 1)]
    spans = [w_span(piece, 1), w_span(2 * low_bits[1] + 4 * low_bits[2], 2), w_span(4 * low_bits[2], 4)]

    def plane(stage):
        copies = []
        for k in range(1, count):
            source = (place + k) % count
            copies.append(pltpu.make_async_remote_copy(
                src_ref=w_all.at[source, spans[stage]], dst_ref=w_all.at[source, spans[stage]],
                send_sem=plane_send.at[stage, k - 1], recv_sem=plane_recv.at[stage, k - 1],
                device_id={"dp": partners[stage]}, device_id_type=MESH))
        return copies

    def plane_start(stage):
        for copy in plane(stage):
            copy.start()

    def plane_wait(stage):
        for copy in plane(stage):
            copy.wait()

    @pl.when((seq == 0) & (pair == 0))
    def _():
        greet(place, count, partners)
        turned = qkv_w[...].T
        parts = []
        for j in range(3):
            for h in range(heads_dev):
                parts.append(turned[(h * 3 + j) * HD:(h * 3 + j + 1) * HD])
        w_all[place, 0:heads_dev * 3 * HD, :] = jnp.concatenate(parts, axis=0)
        w_all[place, heads_dev * 3 * HD:base, :] = out_w[...]
        first = lax.broadcasted_iota(jnp.int32, (w_all.shape[1] - base, width), 0)
        w_all[place, base:, :] = jnp.where(
            first == 0, q_bias[...].astype(F32),
            jnp.where(first == 1, v_bias[...].astype(F32), 0.0)).astype(BF16)
        for s in range(seqs):
            row = embed[pl.ds(pair_ids[s], 1), :]
            own = pl.ds(pl.multiple_of(place * rows, rows), rows)
            x_all[s, own, :] = (tok[s].astype(F32) + row).astype(BF16)
        await_greetings(count, partners)
        w_relay.advance(0)
        if count > 2:
            w_relay.advance(1)
        x_relay(0).advance(0)
        for step in range(2 if count > 2 else 1, count):
            w_relay.advance(step)
        plane_start(0)
        plane_wait(0)
        plane_start(1)
        if count > 2:
            x_relay(0).advance(1)
        plane_wait(1)
        plane_start(2)
        for step in range(2, count - 1):
            x_relay(0).advance(step)
        grads[...] = jnp.zeros_like(grads)
        grad_rows[...] = jnp.zeros_like(grad_rows)
        plane_wait(2)
        w_relay.drain()
        total = jnp.zeros((16, width), F32)
        for m in range(count):
            total += w_all[m, base:base + 16, :].astype(F32)
        biases[...] = total
        for p in range(pairs):
            if heads_dev == 2:
                w_out[p] = w_all[p, 0:3 * PAIR, :]
                w_o[p * PAIR:(p + 1) * PAIR, :] = w_all[p, 3 * PAIR:4 * PAIR, :]
            else:
                for half in range(2):
                    for j in range(4):
                        strip = w_all[2 * p + half, j * HD:(j + 1) * HD, :]
                        if j < 3:
                            w_out[p, j * PAIR + half * HD:j * PAIR + (half + 1) * HD, :] = strip
                        else:
                            w_o[p * PAIR + half * HD:p * PAIR + (half + 1) * HD, :] = strip

    def hbm_copy(s):
        return pltpu.make_async_copy(x_all.at[s], x_out.at[s], x_copy.at[s])

    @pl.when(pair == 0)
    def _():
        x_relay(seq).advance(count - 1)

        @pl.when(seq + 1 < seqs)
        def _():
            x_relay(seq + 1).advance(0)
        hbm_copy(seq).start()

    length = lengths[seq]
    lanes = pl.ds(pl.multiple_of(pair * PAIR, PAIR), PAIR)
    own = pl.ds(pl.multiple_of(place * rows, rows), rows)
    q_pair = (nt(x_all[seq, own, :], w_out[pair, 0:PAIR, :]) + biases[0:1, lanes]).astype(BF16)
    q_pair = q_pair * BF16(HD ** -0.5)
    q_out[0, 0] = q_pair
    q_heads = [one_head(q_pair, 0), one_head(q_pair, 1)]
    v_row = biases[1:2, lanes]

    def score_step(j, tops):
        at = pl.ds(pl.multiple_of(j * block, block), block)
        kv = nt(x_all[seq, at, :], w_out[pair, PAIR:3 * PAIR, :])
        k_blk = kv[:, :PAIR].astype(BF16)
        k_out[0, 0, at, :] = k_blk
        v_out[0, 0, at, :] = (kv[:, PAIR:] + v_row).astype(BF16)
        keep = (lax.broadcasted_iota(jnp.int32, (block, rows), 0) + j * block) < length
        new = []
        for h in range(2):
            s = nt(k_blk, q_heads[h]) * LOG2E
            s = jnp.where(keep, s, NEGATIVE)
            s_all[h, at, :] = s
            new.append(jnp.maximum(tops[h], fold8(s, jnp.max)))
        return tuple(new)

    start = jnp.full((8, rows), NEGATIVE, F32)
    tops = lax.fori_loop(0, full // block, score_step, (start, start))
    tops = [jnp.max(t, axis=0, keepdims=True) for t in tops]
    acc[...] = jnp.zeros_like(acc)

    def value_step(j, sums):
        at = pl.ds(pl.multiple_of(j * block, block), block)
        v_blk = v_out[0, 0, at, :]
        new = []
        for h in range(2):
            p = jnp.exp2(s_all[h, at, :] - tops[h])
            new.append(sums[h] + fold8(p, jnp.sum))
            acc[h] += tn(v_blk, p.astype(BF16))
        return tuple(new)

    zero = jnp.zeros((8, rows), F32)
    sums = lax.fori_loop(0, full // block, value_step, (zero, zero))
    sums = [jnp.sum(t, axis=0, keepdims=True) for t in sums]
    att_t = jnp.concatenate([acc[h, h * HD:(h + 1) * HD, :] * (1.0 / sums[h]) for h in range(2)], axis=0)
    att_t_out[0, 0] = att_t
    att_rows_all[:, lanes] = att_t.T.astype(BF16)
    lse_out[0, 0] = jnp.concatenate(
        [tops[h] + jnp.log2(sums[h]) for h in range(2)] + [jnp.zeros((6, rows), F32)], axis=0)

    for step in range(1, count - 1):
        after = max(0, (step * pairs) // (count - 2) - 1)

        @pl.when((pair == after) & (seq + 1 < seqs))
        def _():
            x_relay(seq + 1).advance(step)

    @pl.when(pair == pairs - 1)
    def _():
        cot_rows = cot[0]
        att_rows = att_rows_all[...]
        row = embed[pl.ds(pair_ids[seq], 1), :]
        mixed = (tok[seq].astype(F32) + row) + (nn(att_rows, w_o[...]) + b_out[...])
        mixed_low = mixed.astype(BF16)
        out_sum = mixed + b_last[...]
        back_sum = cot_rows.astype(F32)
        root = math.sqrt(2.0 / math.pi)
        for c in range(hidden // width):
            at = slice(c * width, (c + 1) * width)
            pre = nn(mixed_low, w_in[:, at]) + b_in[:, at]
            square = pre * pre
            th = jnp.tanh(root * pre * (1.0 + 0.044715 * square))
            half = 0.5 * (1.0 + th)
            act = (pre * half).astype(BF16)
            slope = half + (0.5 * root) * pre * (1.0 - th * th) * (1.0 + (3 * 0.044715) * square)
            out_sum += nn(act, w_last[at, :])
            back = (nt(cot_rows, w_last[at, :]) * slope).astype(BF16)
            grad_rows[c:c + 1, :] += jnp.sum(back.astype(F32), axis=0, keepdims=True)
            back_sum += nt(back, w_in[:, at])
            grads[at, :] += tn(act, cot_rows)
            grads[hidden + c * width:hidden + (c + 1) * width, :] += tn(mixed_low, back)
        result[0] = out_sum.astype(BF16)
        back_low = back_sum.astype(BF16)
        mixed_grad[0] = back_low
        at = hidden // width
        grad_rows[at:at + 1, :] += jnp.sum(cot_rows.astype(F32), axis=0, keepdims=True)
        grad_rows[at + 1:at + 2, :] += jnp.sum(back_low.astype(F32), axis=0, keepdims=True)
        grads[2 * hidden:, :] += tn(att_rows, back_low)
        att_grad[0] = nt(back_low, w_o[...]).astype(BF16)

    @pl.when(last_step)
    def _():
        def narrow(j, _):
            at = pl.ds(pl.multiple_of(j * width, width), width)
            g_all[at, :] = grads[at, :].astype(BF16)
            return 0

        lax.fori_loop(0, grads.shape[0] // width, narrow, 0)
        rest = g_all.shape[0] - grads.shape[0]
        g_all[grads.shape[0]:, :] = jnp.concatenate(
            [grad_rows[...], jnp.zeros((rest - 8, width), F32)], axis=0).astype(BF16)
        for s in range(seqs):
            x_relay(s).drain()
            hbm_copy(s).wait()


def fixed(shape):
    return pl.BlockSpec(shape, lambda *_: (0,) * len(shape), pipeline_mode=CONSTANT)


def call_layer(count, lengths, pair_ids, tok, embed, cot, qkv_w, q_bias, v_bias, out_w, b_out,
               w_in, b_in, w_last, b_last):
    seqs, rows, width = tok.shape
    hidden = w_in.shape[1]
    heads_dev = qkv_w.shape[1] // (3 * HD)
    full = count * rows
    pairs = width // PAIR
    block = min(512, full)
    w_rows = -(-(heads_dev * 4 * HD + 16) // (16 * PIECES)) * 16 * PIECES
    g_rows = -(-(2 * hidden + width + 16) // 1024) * 1024
    in_smem = pl.BlockSpec(memory_space=pltpu.SMEM)
    per_seq = lambda: pl.BlockSpec((1, rows, width), lambda s, p: (s, 0, 0))
    per_pair = lambda *tail: pl.BlockSpec((1, 1) + tail, lambda s, p: (s, p, 0, 0))
    shape = jax.ShapeDtypeStruct
    return pl.pallas_call(
        functools.partial(forward_layer, count, heads_dev, block),
        grid=(seqs, pairs),
        in_specs=[in_smem, in_smem, fixed(tok.shape), fixed(embed.shape), per_seq(), fixed(qkv_w.shape),
                  fixed(q_bias.shape), fixed(v_bias.shape), fixed(out_w.shape), fixed(b_out.shape),
                  fixed(w_in.shape), fixed(b_in.shape), fixed(w_last.shape), fixed(b_last.shape)],
        out_specs=[pl.BlockSpec(memory_space=pl.ANY), fixed((pairs, 3 * PAIR, width)),
                   per_pair(rows, PAIR), per_pair(full, PAIR), per_pair(full, PAIR),
                   per_pair(PAIR, rows), per_pair(8, rows),
                   per_seq(), per_seq(), per_seq(), fixed((g_rows, width))],
        out_shape=[
            shape((seqs, full, width), BF16),
            shape((pairs, 3 * PAIR, width), BF16),
            shape((seqs, pairs, rows, PAIR), BF16),
            shape((seqs, pairs, full, PAIR), BF16),
            shape((seqs, pairs, full, PAIR), BF16),
            shape((seqs, pairs, PAIR, rows), F32),
            shape((seqs, pairs, 8, rows), F32),
            shape((seqs, rows, width), BF16),
            shape((seqs, rows, width), BF16),
            shape((seqs, rows, width), BF16),
            shape((g_rows, width), BF16),
        ],
        scratch_shapes=[
            pltpu.VMEM((seqs, full, width), BF16),
            pltpu.VMEM((count, w_rows, width), BF16),
            pltpu.VMEM((width, width), BF16),
            pltpu.VMEM((16, width), F32),
            pltpu.VMEM((2, full, rows), F32),
            pltpu.VMEM((2, PAIR, rows), F32),
            pltpu.VMEM((rows, width), BF16),
            pltpu.VMEM((2 * hidden + width, width), F32),
            pltpu.VMEM((8, width), F32),
            pltpu.SemaphoreType.DMA((seqs, 2 * (count - 1))),
            pltpu.SemaphoreType.DMA((seqs, count)),
            pltpu.SemaphoreType.DMA((seqs,)),
            pltpu.SemaphoreType.DMA((2 * (count - 1),)),
            pltpu.SemaphoreType.DMA((count,)),
            pltpu.SemaphoreType.DMA((3, count - 1)),
            pltpu.SemaphoreType.DMA((3, count - 1)),
        ],
        cost_estimate=pl.CostEstimate(flops=120 * 10 ** 9, bytes_accessed=60 << 20,
                                      transcendentals=seqs * pairs * 2 * full * rows),
        compiler_params=pltpu.CompilerParams(
            collective_id=0, has_side_effects=True, vmem_limit_bytes=VMEM_LIMIT),
        name="forward_layer",
    )(lengths, pair_ids, tok, embed, cot, qkv_w, q_bias, v_bias, out_w, b_out, w_in, b_in, w_last, b_last)


def row_step(size):
    for step in (256, 160, 128, 80, 64, 32, 16):
        if size % step == 0:
            return step
    return size


def aligned(start, size, unit=16):
    return pl.ds(pl.multiple_of(start, unit), size)


class Reducer:
    def __init__(self, data, land, group, rows, bits, where_at, send_sem, recv_sem, free_sem=None):
        self.data, self.land, self.group = data, land, group
        self.send_sem, self.recv_sem, self.free_sem = send_sem, recv_sem, free_sem
        self.stages, self.landed = [], 0
        start, size = 0, rows
        for axis, bit in bits:
            index = where_at[axis]
            digit = (index // bit) % 2
            halves = (size // 2) % 16 == 0
            if halves:
                size //= 2
                keep, other = start + digit * size, start + (1 - digit) * size
            else:
                keep = other = start
            self.stages.append((axis, flip(index, bit), halves, keep, other, size, self.landed))
            self.landed += size
            start = keep
        self.start, self.size = start, size

    def copy(self, j):
        axis, partner, _, _, other, size, landed = self.stages[j]
        return pltpu.make_async_remote_copy(
            src_ref=self.data.at[self.group, :, aligned(other, size)],
            dst_ref=self.land.at[self.group, :, pl.ds(landed, size)],
            send_sem=self.send_sem.at[self.group, j],
            recv_sem=self.recv_sem.at[self.group, j],
            device_id={axis: partner}, device_id_type=MESH)

    def finish(self, j):
        self.copy(j).wait()
        axis, partner, halves, keep, _, size, landed = self.stages[j]
        if self.free_sem is not None and halves:
            pl.semaphore_signal(self.free_sem.at[self.group, j], 1, device_id={axis: partner},
                                device_id_type=MESH)
        step = row_step(size)
        slots = self.data.shape[1]
        for slot in range(slots):
            def add(r, _):
                at = aligned(keep + r * step, step)
                more = self.land[self.group, slot, aligned(landed + r * step, step), :]
                self.data[self.group, slot, at, :] = (
                    self.data[self.group, slot, at, :].astype(F32) + more.astype(F32)).astype(BF16)
                return 0

            lax.fori_loop(0, size // step, add, 0)

    def back(self, j):
        axis, partner, _, keep, _, size, _ = self.stages[j]
        view = self.data.at[self.group, :, aligned(keep, size)]
        at = len(self.stages) + j
        return pltpu.make_async_remote_copy(
            src_ref=view, dst_ref=view, send_sem=self.send_sem.at[self.group, at],
            recv_sem=self.recv_sem.at[self.group, at],
            device_id={axis: partner}, device_id_type=MESH)

    def back_start(self, j):
        pl.semaphore_wait(self.free_sem.at[self.group, j], 1)
        self.back(j).start()

    def events(self):
        doubling = [j for j in range(len(self.stages)) if self.stages[j][2]][::-1]
        run = [lambda: self.copy(0).start()]
        for j in range(len(self.stages)):
            def after(j=j):
                self.finish(j)
                if j + 1 < len(self.stages):
                    self.copy(j + 1).start()
                elif doubling:
                    self.back_start(doubling[0])
            run.append(after)
        for i, j in enumerate(doubling):
            def after_back(i=i, j=j):
                self.back(j).wait()
                if i + 1 < len(doubling):
                    self.back_start(doubling[i + 1])
            run.append(after_back)
        return run


def bit_list(size):
    return [1 << b for b in range(size.bit_length() - 1)]


def far_first(count):
    table = []
    for m in range(count):
        order = []
        for k in range(count - 1, 0, -1):
            order += [c for c in (m + k, m - k) if 0 <= c < count]
        table.append(order + [m])
    return table


def backward_layer(count, data_count, heads_dev, tail_points,
                   lengths, pair_ids, x_seq, weight, q_in, k_in, v_in, att_t, lse, grad_in, mixed_grad, g_in,
                   token_grad, g_out, own_out,
                   a_buf, a_land, b_buf, b_land, b_parts, own_buf, parts, land, x_acc, dq_acc, delta_all,
                   w_acc, bias_acc, col_acc, table_acc,
                   load_sem, a_send, a_recv, a_free, b_send, b_recv, s_send, s_recv, r_send, r_recv):
    seq, turn = pl.program_id(0), pl.program_id(1)
    seqs, pairs = token_grad.shape[0], weight.shape[0]
    rows, width = token_grad.shape[1], token_grad.shape[2]
    place, data_at = lax.axis_index("mp"), lax.axis_index("dp")
    where_at = {"mp": place, "dp": data_at}
    point = seq * count + turn
    data_bits, place_bits = bit_list(data_count), bit_list(count)
    swapped = [{2: 4, 4: 2}.get(b, b) for b in data_bits]

    order = far_first(count)
    chunk = sum(jnp.where((place == m) & (turn == i), order[m][i], 0)
                for m in range(count) for i in range(count))

    a_sums = [
        Reducer(a_buf, a_land, g, a_buf.shape[2],
                [("dp", b) for b in (data_bits, swapped)[g]] + [("mp", b) for b in place_bits],
                where_at, a_send, a_recv, a_free)
        for g in range(2)]
    a_events = [s.events() for s in a_sums]
    b_sums = [
        Reducer(b_buf, b_land, g, b_buf.shape[2], [("dp", b) for b in (data_bits, swapped)[g]],
                where_at, b_send, b_recv)
        for g in range(2)]

    def send_part(s, c, downward):
        slot = jnp.where((place - 1 == c) & (downward == 1), count, c)
        return pltpu.make_async_remote_copy(
            src_ref=parts.at[s, c], dst_ref=land.at[s, slot],
            send_sem=s_send.at[s, c], recv_sem=s_recv.at[s, slot],
            device_id={"mp": place - 1 if downward else place + 1}, device_id_type=MESH)

    def await_part(s, slot):
        pltpu.make_async_remote_copy(
            src_ref=land.at[s, slot], dst_ref=land.at[s, slot],
            send_sem=s_send.at[s, 0], recv_sem=s_recv.at[s, slot],
            device_id={"mp": (place + 1) % count}, device_id_type=MESH).wait_recv()

    def combine(s, k):
        for downward in (0, 1):
            c = place - k if downward else place + k
            go = ((c >= 0) & (place + 1 < count)) if downward else ((c < count) & (place >= 1))

            @pl.when(go)
            def _():
                await_part(s, c)
                parts[s, c] = (parts[s, c].astype(F32) + land[s, c].astype(F32)).astype(BF16)
                send_part(s, c, downward).start()

    def conclude(s):
        for downward in (0, 1):
            slot = count if downward else place

            @pl.when((place + 1 < count) if downward else (place >= 1))
            def _():
                await_part(s, slot)
                token_grad[s] += land[s, slot].astype(F32)

    def load():
        return pltpu.make_async_copy(g_in, a_buf, load_sem.at[0])

    def store():
        return pltpu.make_async_copy(a_buf, g_out, load_sem.at[1])

    partners = [flip(data_at, b) for b in data_bits]

    @pl.when(point == 0)
    def _():
        greet(place, count, partners)
        load().start()
        w_acc[...] = jnp.zeros_like(w_acc)
        bias_acc[...] = jnp.zeros_like(bias_acc)
        table_acc[...] = jnp.zeros_like(table_acc)
        await_greetings(count, partners)
        load().wait()
        for events in a_events:
            events[0]()

    @pl.when(turn == 0)
    def _():
        col_acc[...] = jnp.zeros_like(col_acc)
        dq_acc[...] = jnp.zeros_like(dq_acc)
        for p in range(pairs):
            prod = grad_in[0, :, p * PAIR:(p + 1) * PAIR].astype(F32).T * att_t[0, p]
            delta_all[p, 0:1, :] = jnp.sum(prod[:HD], axis=0, keepdims=True)
            delta_all[p, 1:2, :] = jnp.sum(prod[HD:], axis=0, keepdims=True)

    length = lengths[seq]
    at = aligned(chunk * rows, rows, rows)
    own = aligned(place * rows, rows, rows)
    x_acc[...] = jnp.zeros_like(x_acc)

    def pair_step(p, _):
        lanes = aligned(p * PAIR, PAIR, PAIR)
        q_pair = q_in[0, p]
        grad_pair = grad_in[0, :, lanes]
        k_blk = k_in[0, p, at, :]
        v_blk = v_in[0, p, at, :]
        keep = (lax.broadcasted_iota(jnp.int32, (rows, rows), 0) + chunk * rows) < length
        dk = jnp.zeros((rows, PAIR), F32)
        dv = jnp.zeros((rows, PAIR), F32)
        for h in range(2):
            q_head, g_head = one_head(q_pair, h), one_head(grad_pair, h)
            s = jnp.where(keep, nt(k_blk, q_head) * LOG2E, NEGATIVE)
            pr = jnp.exp2(s - lse[0, p, h:h + 1, :])
            dp = nt(v_blk, g_head)
            ds = (pr * (dp - delta_all[p, h:h + 1, :])).astype(BF16)
            dv += nn(pr.astype(BF16), g_head)
            dk += nn(ds, q_head)
            dq_acc[p, h] += tn(k_blk, ds)
        dv = dv.astype(BF16)
        both = jnp.concatenate([dk.astype(BF16), dv], axis=1)
        x_acc[...] += nn(both, weight[p, PAIR:, :])
        w_acc[p, PAIR:, :] += tn(both, x_seq[0, at, :])
        bias_acc[1:2, lanes] += jnp.sum(dv.astype(F32), axis=0, keepdims=True)
        return 0

    lax.fori_loop(0, pairs, pair_step, 0)

    @pl.when(turn < count - 1)
    def _():
        parts[seq, chunk] = x_acc[...].astype(BF16)
        for downward in (0, 1):
            @pl.when((place == (count - 1 if downward else 0)) & (chunk != place))
            def _():
                send_part(seq, chunk, downward).start()

    @pl.when(turn == count - 1)
    def _():
        def query_step(p, _):
            lanes = aligned(p * PAIR, PAIR, PAIR)
            dq_t = jnp.concatenate(
                [dq_acc[p, h, h * HD:(h + 1) * HD, :] for h in range(2)], axis=0) * (HD ** -0.5)
            dq = dq_t.T.astype(BF16)
            x_acc[...] += nn(dq, weight[p, :PAIR, :])
            w_acc[p, :PAIR, :] += tn(dq, x_seq[0, own, :])
            bias_acc[0:1, lanes] += jnp.sum(dq.astype(F32), axis=0, keepdims=True)
            return 0

        lax.fori_loop(0, pairs, query_step, 0)
        x_acc[...] += mixed_grad[0].astype(F32)
        token_grad[seq] = x_acc[...]

    col_acc[0:1, :] += jnp.sum(x_acc[...], axis=0, keepdims=True)

    @pl.when(turn == count - 1)
    def _():
        line = lax.broadcasted_iota(jnp.int32, table_acc.shape, 0)
        table_acc[...] += jnp.where(line == pair_ids[seq], col_acc[0:1, :], 0.0)

    slots = {2: 2, 1: 4} if count == 4 else {k: count + (count - 2 - k) for k in range(1, count - 1)}
    for k in range(count - 2, 0, -1):
        turns, seq_back = slots[k] % count, slots[k] // count

        @pl.when((turn == turns) & (seq >= seq_back))
        def _():
            combine(seq - seq_back, k)

    @pl.when((turn == count - 1) & (seq >= 1))
    def _():
        conclude(seq - 1)

    total = seqs * count
    later = len(a_events[0]) - 1
    in_tail = []
    for e in range(1, later + 1):
        when_at = tail_points[e - 1] if tail_points else (e * total) // (later + 1)
        if when_at >= total:
            in_tail.append(e)
            continue

        @pl.when(point == when_at)
        def _():
            for events in a_events:
                events[e]()

    @pl.when(point == total - 1)
    def _():
        last = seqs - 1
        base = heads_dev * 3 * HD
        half = count // 2
        for m in range(count):
            g, slot = m // half, m % half
            if heads_dev == 2:
                b_buf[g, slot, 0:base, :] = w_acc[m].astype(BF16)
            else:
                for j in range(3):
                    lo = j * PAIR + (m % 2) * HD
                    b_buf[g, slot, j * HD:(j + 1) * HD, :] = w_acc[m // 2, lo:lo + HD, :].astype(BF16)
            b_buf[g, slot, base:base + 16, :] = bias_acc[...].astype(BF16)
            b_buf[g, slot, base + 16:base + 32, :] = table_acc[...].astype(BF16)
            rest = b_buf.shape[2] - base - 32
            b_buf[g, slot, base + 32:, :] = jnp.zeros((rest, width), BF16)
        stages = len(b_sums[0].stages)
        for b in b_sums:
            b.copy(0).start()
        tail_k = [k for k in range(count - 2, 0, -1) if slots[k] >= count]
        for j in range(stages):
            for b in b_sums:
                b.finish(j)
                if j + 1 < stages:
                    b.copy(j + 1).start()
            if tail_k:
                combine(last, tail_k.pop(0))
        strip = b_sums[0].size
        mine = place // half
        start = jnp.where(mine == 0, b_sums[0].start, b_sums[1].start)

        def scatter(k):
            target = (place + k) % count
            g = target // half
            begin = jnp.where(g == 0, b_sums[0].start, b_sums[1].start)
            return pltpu.make_async_remote_copy(
                src_ref=b_buf.at[g, target % half, aligned(begin, strip)],
                dst_ref=b_parts.at[k - 1],
                send_sem=r_send.at[k - 1], recv_sem=r_recv.at[k - 1],
                device_id={"mp": target}, device_id_type=MESH)

        for k in range(1, count):
            scatter(k).start()
        for k in tail_k:
            combine(last, k)
        for e in in_tail:
            for events in a_events:
                events[e]()
        store().start()
        for k in range(1, count):
            scatter(k).wait()
        home = b_buf[mine, place % half, aligned(start, strip), :].astype(F32)
        for k in range(1, count):
            home += b_parts[k - 1].astype(F32)
        own_buf[aligned(start, strip), :] = home.astype(BF16)

        def back(j):
            partner = jnp.where(mine == 0, b_sums[0].stages[j][1], b_sums[1].stages[j][1])
            keep = jnp.where(mine == 0, b_sums[0].stages[j][3], b_sums[1].stages[j][3])
            size = b_sums[0].stages[j][5]
            view = own_buf.at[aligned(keep, size)]
            return pltpu.make_async_remote_copy(
                src_ref=view, dst_ref=view, send_sem=r_send.at[count - 1 + j],
                recv_sem=r_recv.at[count - 1 + j], device_id={"dp": partner}, device_id_type=MESH)

        for j in reversed(range(stages)):
            back(j).start()
            back(j).wait()
        own_out[...] = own_buf[...]
        conclude(last)
        store().wait()
        for s in range(seqs):
            for k in range(1, count):
                for downward in (0, 1):
                    c = place - k if downward else place + k

                    @pl.when((c >= 0) if downward else (c < count))
                    def _():
                        send_part(s, c, downward).wait_send()


def call_backward(count, data_count, heads_dev, lengths, pair_ids, x_all, weight, q, k, v, att_t, lse,
                  grad, mixed_grad, g_all):
    seqs, full, width = x_all.shape
    rows = full // count
    pairs = weight.shape[0]
    a_rows = g_all.shape[0] // 2
    base = heads_dev * 3 * HD
    slot_rows = -(-(base + 32) // 128) * 128
    data_bits, place_bits = bit_list(data_count), bit_list(count)

    def landing(size, bits):
        landed = 0
        for _ in range(bits):
            size = size // 2 if (size // 2) % 16 == 0 else size
            landed += size
        return landed, size

    a_landed, _ = landing(a_rows, len(data_bits) + len(place_bits))
    b_landed, strip = landing(slot_rows, len(data_bits))
    a_stages, b_stages = len(data_bits) + len(place_bits), len(data_bits)
    tail_points = TAIL_POINTS if (count, data_count) == (4, 8) else None
    in_smem = pl.BlockSpec(memory_space=pltpu.SMEM)
    in_hbm = pl.BlockSpec(memory_space=pl.ANY)
    seq_block = lambda shape, mode=None: pl.BlockSpec(
        (1,) + shape[1:], lambda s, i: (s,) + (0,) * (len(shape) - 1), pipeline_mode=mode)
    shape = jax.ShapeDtypeStruct
    dma = pltpu.SemaphoreType.DMA
    return pl.pallas_call(
        functools.partial(backward_layer, count, data_count, heads_dev, tail_points),
        grid=(seqs, count),
        in_specs=[in_smem, in_smem, seq_block(x_all.shape, CONSTANT), fixed(weight.shape),
                  seq_block(q.shape, CONSTANT), seq_block(k.shape, CONSTANT),
                  seq_block(v.shape, CONSTANT), seq_block(att_t.shape, CONSTANT),
                  seq_block(lse.shape), seq_block(grad.shape), seq_block(mixed_grad.shape), in_hbm],
        out_specs=[fixed((seqs, rows, width)), in_hbm, fixed((slot_rows, width))],
        out_shape=[
            shape((seqs, rows, width), F32),
            shape((2, 1, a_rows, width), BF16),
            shape((slot_rows, width), BF16),
        ],
        scratch_shapes=[
            pltpu.VMEM((2, 1, a_rows, width), BF16),
            pltpu.VMEM((2, 1, a_landed, width), BF16),
            pltpu.VMEM((2, count // 2, slot_rows, width), BF16),
            pltpu.VMEM((2, count // 2, b_landed, width), BF16),
            pltpu.VMEM((count - 1, strip, width), BF16),
            pltpu.VMEM((slot_rows, width), BF16),
            pltpu.VMEM((seqs, count, rows, width), BF16),
            pltpu.VMEM((seqs, count + 1, rows, width), BF16),
            pltpu.VMEM((rows, width), F32),
            pltpu.VMEM((pairs, 2, PAIR, rows), F32),
            pltpu.VMEM((pairs, 8, rows), F32),
            pltpu.VMEM((pairs, 3 * PAIR, width), F32),
            pltpu.VMEM((16, width), F32),
            pltpu.VMEM((8, width), F32),
            pltpu.VMEM((16, width), F32),
            dma((2,)), dma((2, 2 * a_stages)), dma((2, 2 * a_stages)),
            pltpu.SemaphoreType.REGULAR((2, a_stages)),
            dma((2, b_stages)), dma((2, b_stages)),
            dma((seqs, count)), dma((seqs, count + 1)),
            dma((count - 1 + b_stages,)), dma((count - 1 + b_stages,)),
        ],
        cost_estimate=pl.CostEstimate(flops=200 * 10 ** 9, bytes_accessed=60 << 20,
                                      transcendentals=seqs * pairs * 2 * full * rows),
        compiler_params=pltpu.CompilerParams(
            collective_id=1, has_side_effects=True, vmem_limit_bytes=VMEM_LIMIT),
        name="backward_layer",
    )(lengths, pair_ids, x_all, weight, q, k, v, att_t, lse, grad, mixed_grad,
      g_all.reshape(2, 1, a_rows, width))


def body(
    tokens,
    pair_ids,
    lengths,
    pair_embed,
    qkv_weight,
    q_bias,
    v_bias,
    out_weight,
    out_bias,
    ffn_in_weight,
    ffn_in_bias,
    ffn_out_weight,
    ffn_out_bias,
    cotangent,
):
    local_rows, seqs, width = tokens.shape
    table_rows = pair_embed.shape[0]
    count = lax.axis_size("mp")
    place = lax.axis_index("mp").astype(jnp.int32).reshape(1)
    tok = jnp.transpose(tokens, (1, 0, 2))
    cot = jnp.transpose(cotangent, (1, 0, 2))
    bias_len = q_bias.shape[0]
    spread = lambda v: lax.dynamic_update_slice(
        jnp.zeros((1, width), BF16), v[None], (0, place[0] * bias_len))
    (x_all, w_pairs, q, k, v, att_t, lse, result, mixed_grad, att_grad, g_all) = call_layer(
        count, lengths, pair_ids, tok, pair_embed, cot, qkv_weight, spread(q_bias), spread(v_bias),
        out_weight, out_bias[None], ffn_in_weight, ffn_in_bias[None], ffn_out_weight,
        ffn_out_bias[None])
    heads_dev = bias_len // HD
    tokens_grad, g_sum, own = call_backward(
        count, lax.axis_size("dp"), heads_dev, lengths, pair_ids, x_all, w_pairs, q, k, v, att_t, lse,
        att_grad, mixed_grad, g_all)

    hidden = ffn_in_weight.shape[1]
    g_sum = g_sum.reshape(-1, width)
    g_last_sum = g_sum[:hidden].astype(F32)
    g_in_sum = jnp.transpose(
        g_sum[hidden:2 * hidden].reshape(hidden // width, width, width), (1, 0, 2)
    ).reshape(width, hidden).astype(F32)
    out_rows = out_weight.shape[0]
    g_out_own = lax.dynamic_slice_in_dim(
        g_sum, 2 * hidden + place[0] * out_rows, out_rows).astype(F32)
    small = g_sum[2 * hidden + width:2 * hidden + width + 8].astype(F32)
    at = hidden // width
    base = heads_dev * 3 * HD
    qkv_sum = jnp.transpose(
        own[:base].reshape(3, heads_dev, HD, width), (3, 1, 0, 2)).reshape(width, base).astype(F32)
    bias_rows = lax.dynamic_slice_in_dim(own[base:base + 2], place[0] * bias_len, bias_len, axis=1)
    return (
        jnp.transpose(result, (1, 0, 2)),
        jnp.transpose(tokens_grad, (1, 0, 2)),
        own[base + 16:base + 16 + table_rows].astype(F32),
        qkv_sum,
        bias_rows[0].astype(F32),
        bias_rows[1].astype(F32),
        g_out_own,
        small[at + 1],
        g_in_sum,
        small[:at].reshape(-1),
        g_last_sum,
        small[at],
    )


def solution(mesh):
    return jax.shard_map(
        body,
        mesh=mesh,
        in_specs=(
            P("mp", "dp", None),
            P("dp"),
            P("dp"),
            P(),
            P(None, "mp"),
            P("mp"),
            P("mp"),
            P("mp", None),
            P(),
            P(),
            P(),
            P(),
            P(),
            P("mp", "dp", None),
        ),
        out_specs=(
            P("mp", "dp", None),
            P("mp", "dp", None),
            P(),
            P(None, "mp"),
            P("mp"),
            P("mp"),
            P("mp", None),
            P(),
            P(),
            P(),
            P(),
            P(),
        ),
        check_vma=False,
    )
```

```python
import functools
import math

import jax
import jax.numpy as jnp
from jax import lax
from jax.experimental import pallas as pl
from jax.experimental.pallas import tpu as pltpu
from jax.sharding import PartitionSpec as P

HD = 64
PAIR = 2 * HD
NEGATIVE = -1e30
LOG2E = math.log2(math.e)
F32 = jnp.float32
BF16 = jnp.bfloat16
VMEM_LIMIT = 56 * 1024 * 1024


def nn(a, b):
    return jnp.dot(a, b, preferred_element_type=F32)


def nt(a, b):
    return lax.dot_general(a, b, (((1,), (1,)), ((), ())), preferred_element_type=F32)


def tn(a, b):
    return lax.dot_general(a, b, (((0,), (0,)), ((), ())), preferred_element_type=F32)


def head_lanes(rows, head):
    lane = lax.broadcasted_iota(jnp.int32, (rows, PAIR), 1)
    return (lane >= head * HD) & (lane < (head + 1) * HD)


def one_head(pair_rows, head):
    return jnp.where(head_lanes(pair_rows.shape[0], head), pair_rows, jnp.zeros_like(pair_rows))


def fold8(values, op):
    rows, lanes = values.shape
    return op(values.reshape(rows // 8, 8, lanes), axis=0)


MESH = pl.DeviceIdType.MESH
CONSTANT = pl.Buffered(1)
PIECES = 8
TAIL_POINTS = (0, 2, 3, 5, 7, 9, 10, 12, 12)


class Relay:
    def __init__(self, place, count, view, send_sem, recv_sem):
        self.place, self.count, self.view = place, count, view
        self.send_sem, self.recv_sem = send_sem, recv_sem

    def copy(self, chunk, downward, step):
        return pltpu.make_async_remote_copy(
            src_ref=self.view(chunk), dst_ref=self.view(chunk),
            send_sem=self.send_sem(downward, step), recv_sem=self.recv_sem(chunk),
            device_id={"mp": self.place - 1 if downward else self.place + 1},
            device_id_type=MESH)

    def each(self, step):
        for downward in (0, 1):
            chunk = self.place + step if downward else self.place - step
            exists = chunk < self.count if downward else chunk >= 0
            onward = self.place >= 1 if downward else self.place + 1 < self.count
            yield downward, chunk, exists, onward

    def advance(self, step):
        for downward, chunk, exists, onward in self.each(step):
            if step:
                @pl.when(exists)
                def _():
                    self.copy(chunk, downward, step).wait_recv()
            if step < self.count - 1:
                @pl.when(exists & onward)
                def _():
                    self.copy(chunk, downward, step).start()

    def drain(self):
        for step in range(self.count - 1):
            for downward, chunk, exists, onward in self.each(step):
                @pl.when(exists & onward)
                def _():
                    self.copy(chunk, downward, step).wait_send()


def greet(place, count, partners):
    barrier = pltpu.get_barrier_semaphore()
    for partner in partners:
        pl.semaphore_signal(barrier, 1, device_id={"dp": partner}, device_id_type=MESH)
    for k in range(1, count):
        pl.semaphore_signal(barrier, 1, device_id={"mp": (place + k) % count}, device_id_type=MESH)


def await_greetings(count, partners):
    pl.semaphore_wait(pltpu.get_barrier_semaphore(), len(partners) + count - 1)


def flip(index, bit):
    return index + bit - 2 * bit * ((index // bit) % 2)


def forward_layer(count, heads_dev, block,
                  lengths, pair_ids, tok, embed, cot, qkv_w, q_bias, v_bias, out_w, b_out,
                  w_in, b_in, w_last, b_last,
                  x_out, w_out, q_out, k_out, v_out, att_t_out, lse_out,
                  result, mixed_grad, att_grad, g_all,
                  x_all, w_all, w_o, biases, s_all, acc, att_rows_all, grads, grad_rows,
                  x_send, x_recv, x_copy, w_send, w_recv, plane_send, plane_recv):
    seq, pair = pl.program_id(0), pl.program_id(1)
    seqs, pairs = tok.shape[0], w_out.shape[0]
    rows, width = tok.shape[1], tok.shape[2]
    full = count * rows
    hidden = w_in.shape[1]
    base = heads_dev * 4 * HD
    piece_rows = w_all.shape[1] // PIECES
    place, data_at = lax.axis_index("mp"), lax.axis_index("dp")
    last_step = (seq == seqs - 1) & (pair == pairs - 1)

    def x_relay(s):
        return Relay(
            place, count,
            lambda chunk: x_all.at[s, pl.ds(pl.multiple_of(chunk * rows, rows), rows)],
            lambda downward, step: x_send.at[s, downward * (count - 1) + step],
            lambda chunk: x_recv.at[s, chunk])

    low_bits = [(data_at // bit) % 2 for bit in (4, 2, 1)]
    piece = low_bits[0] + 2 * low_bits[1] + 4 * low_bits[2]

    def w_span(start, size):
        return pl.ds(pl.multiple_of(start * piece_rows, piece_rows), size * piece_rows)

    w_relay = Relay(
        place, count, lambda chunk: w_all.at[chunk, w_span(piece, 1)],
        lambda downward, step: w_send.at[downward * (count - 1) + step],
        lambda chunk: w_recv.at[chunk])
    partners = [flip(data_at, bit) for bit in (4, 2, 1)]
    spans = [w_span(piece, 1), w_span(2 * low_bits[1] + 4 * low_bits[2], 2), w_span(4 * low_bits[2], 4)]

    def plane(stage):
        copies = []
        for k in range(1, count):
            source = (place + k) % count
            copies.append(pltpu.make_async_remote_copy(
                src_ref=w_all.at[source, spans[stage]], dst_ref=w_all.at[source, spans[stage]],
                send_sem=plane_send.at[stage, k - 1], recv_sem=plane_recv.at[stage, k - 1],
                device_id={"dp": partners[stage]}, device_id_type=MESH))
        return copies

    def plane_start(stage):
        for copy in plane(stage):
            copy.start()

    def plane_wait(stage):
        for copy in plane(stage):
            copy.wait()

    @pl.when((seq == 0) & (pair == 0))
    def _():
        greet(place, count, partners)
        turned = qkv_w[...].T
        parts = []
        for j in range(3):
            for h in range(heads_dev):
                parts.append(turned[(h * 3 + j) * HD:(h * 3 + j + 1) * HD])
        w_all[place, 0:heads_dev * 3 * HD, :] = jnp.concatenate(parts, axis=0)
        w_all[place, heads_dev * 3 * HD:base, :] = out_w[...]
        first = lax.broadcasted_iota(jnp.int32, (w_all.shape[1] - base, width), 0)
        w_all[place, base:, :] = jnp.where(
            first == 0, q_bias[...].astype(F32),
            jnp.where(first == 1, v_bias[...].astype(F32), 0.0)).astype(BF16)
        for s in range(seqs):
            row = embed[pl.ds(pair_ids[s], 1), :]
            own = pl.ds(pl.multiple_of(place * rows, rows), rows)
            x_all[s, own, :] = (tok[s].astype(F32) + row).astype(BF16)
        await_greetings(count, partners)
        w_relay.advance(0)
        if count > 2:
            w_relay.advance(1)
        x_relay(0).advance(0)
        for step in range(2 if count > 2 else 1, count):
            w_relay.advance(step)
        plane_start(0)
        plane_wait(0)
        plane_start(1)
        if count > 2:
            x_relay(0).advance(1)
        plane_wait(1)
        plane_start(2)
        for step in range(2, count - 1):
            x_relay(0).advance(step)
        grads[...] = jnp.zeros_like(grads)
        grad_rows[...] = jnp.zeros_like(grad_rows)
        plane_wait(2)
        w_relay.drain()
        total = jnp.zeros((16, width), F32)
        for m in range(count):
            total += w_all[m, base:base + 16, :].astype(F32)
        biases[...] = total
        for p in range(pairs):
            if heads_dev == 2:
                w_out[p] = w_all[p, 0:3 * PAIR, :]
                w_o[p * PAIR:(p + 1) * PAIR, :] = w_all[p, 3 * PAIR:4 * PAIR, :]
            else:
                for half in range(2):
                    for j in range(4):
                        strip = w_all[2 * p + half, j * HD:(j + 1) * HD, :]
                        if j < 3:
                            w_out[p, j * PAIR + half * HD:j * PAIR + (half + 1) * HD, :] = strip
                        else:
                            w_o[p * PAIR + half * HD:p * PAIR + (half + 1) * HD, :] = strip

    def hbm_copy(s):
        return pltpu.make_async_copy(x_all.at[s], x_out.at[s], x_copy.at[s])

    @pl.when(pair == 0)
    def _():
        x_relay(seq).advance(count - 1)

        @pl.when(seq + 1 < seqs)
        def _():
            x_relay(seq + 1).advance(0)
        hbm_copy(seq).start()

    length = lengths[seq]
    lanes = pl.ds(pl.multiple_of(pair * PAIR, PAIR), PAIR)
    own = pl.ds(pl.multiple_of(place * rows, rows), rows)
    q_pair = (nt(x_all[seq, own, :], w_out[pair, 0:PAIR, :]) + biases[0:1, lanes]).astype(BF16)
    q_pair = q_pair * BF16(HD ** -0.5)
    q_out[0, 0] = q_pair
    q_heads = [one_head(q_pair, 0), one_head(q_pair, 1)]
    v_row = biases[1:2, lanes]

    def score_step(j, tops):
        at = pl.ds(pl.multiple_of(j * block, block), block)
        kv = nt(x_all[seq, at, :], w_out[pair, PAIR:3 * PAIR, :])
        k_blk = kv[:, :PAIR].astype(BF16)
        k_out[0, 0, at, :] = k_blk
        v_out[0, 0, at, :] = (kv[:, PAIR:] + v_row).astype(BF16)
        keep = (lax.broadcasted_iota(jnp.int32, (block, rows), 0) + j * block) < length
        new = []
        for h in range(2):
            s = nt(k_blk, q_heads[h]) * LOG2E
            s = jnp.where(keep, s, NEGATIVE)
            s_all[h, at, :] = s
            new.append(jnp.maximum(tops[h], fold8(s, jnp.max)))
        return tuple(new)

    start = jnp.full((8, rows), NEGATIVE, F32)
    tops = lax.fori_loop(0, full // block, score_step, (start, start))
    tops = [jnp.max(t, axis=0, keepdims=True) for t in tops]
    acc[...] = jnp.zeros_like(acc)

    def value_step(j, sums):
        at = pl.ds(pl.multiple_of(j * block, block), block)
        v_blk = v_out[0, 0, at, :]
        new = []
        for h in range(2):
            p = jnp.exp2(s_all[h, at, :] - tops[h])
            new.append(sums[h] + fold8(p, jnp.sum))
            acc[h] += tn(v_blk, p.astype(BF16))
        return tuple(new)

    zero = jnp.zeros((8, rows), F32)
    sums = lax.fori_loop(0, full // block, value_step, (zero, zero))
    sums = [jnp.sum(t, axis=0, keepdims=True) for t in sums]
    att_t = jnp.concatenate([acc[h, h * HD:(h + 1) * HD, :] * (1.0 / sums[h]) for h in range(2)], axis=0)
    att_t_out[0, 0] = att_t
    att_rows_all[:, lanes] = att_t.T.astype(BF16)
    lse_out[0, 0] = jnp.concatenate(
        [tops[h] + jnp.log2(sums[h]) for h in range(2)] + [jnp.zeros((6, rows), F32)], axis=0)

    for step in range(1, count - 1):
        after = max(0, (step * pairs) // (count - 2) - 1)

        @pl.when((pair == after) & (seq + 1 < seqs))
        def _():
            x_relay(seq + 1).advance(step)

    @pl.when(pair == pairs - 1)
    def _():
        cot_rows = cot[0]
        att_rows = att_rows_all[...]
        row = embed[pl.ds(pair_ids[seq], 1), :]
        mixed = (tok[seq].astype(F32) + row) + (nn(att_rows, w_o[...]) + b_out[...])
        mixed_low = mixed.astype(BF16)
        out_sum = mixed + b_last[...]
        back_sum = cot_rows.astype(F32)
        root = math.sqrt(2.0 / math.pi)
        for c in range(hidden // width):
            at = slice(c * width, (c + 1) * width)
            pre = nn(mixed_low, w_in[:, at]) + b_in[:, at]
            square = pre * pre
            th = jnp.tanh(root * pre * (1.0 + 0.044715 * square))
            half = 0.5 * (1.0 + th)
            act = (pre * half).astype(BF16)
            slope = half + (0.5 * root) * pre * (1.0 - th * th) * (1.0 + (3 * 0.044715) * square)
            out_sum += nn(act, w_last[at, :])
            back = (nt(cot_rows, w_last[at, :]) * slope).astype(BF16)
            grad_rows[c:c + 1, :] += jnp.sum(back.astype(F32), axis=0, keepdims=True)
            back_sum += nt(back, w_in[:, at])
            grads[at, :] += tn(act, cot_rows)
            grads[hidden + c * width:hidden + (c + 1) * width, :] += tn(mixed_low, back)
        result[0] = out_sum.astype(BF16)
        back_low = back_sum.astype(BF16)
        mixed_grad[0] = back_low
        at = hidden // width
        grad_rows[at:at + 1, :] += jnp.sum(cot_rows.astype(F32), axis=0, keepdims=True)
        grad_rows[at + 1:at + 2, :] += jnp.sum(back_low.astype(F32), axis=0, keepdims=True)
        grads[2 * hidden:, :] += tn(att_rows, back_low)
        att_grad[0] = nt(back_low, w_o[...]).astype(BF16)

    @pl.when(last_step)
    def _():
        def narrow(j, _):
            at = pl.ds(pl.multiple_of(j * width, width), width)
            g_all[at, :] = grads[at, :].astype(BF16)
            return 0

        lax.fori_loop(0, grads.shape[0] // width, narrow, 0)
        rest = g_all.shape[0] - grads.shape[0]
        g_all[grads.shape[0]:, :] = jnp.concatenate(
            [grad_rows[...], jnp.zeros((rest - 8, width), F32)], axis=0).astype(BF16)
        for s in range(seqs):
            x_relay(s).drain()
            hbm_copy(s).wait()


def fixed(shape):
    return pl.BlockSpec(shape, lambda *_: (0,) * len(shape), pipeline_mode=CONSTANT)


def call_layer(count, lengths, pair_ids, tok, embed, cot, qkv_w, q_bias, v_bias, out_w, b_out,
               w_in, b_in, w_last, b_last):
    seqs, rows, width = tok.shape
    hidden = w_in.shape[1]
    heads_dev = qkv_w.shape[1] // (3 * HD)
    full = count * rows
    pairs = width // PAIR
    block = min(512, full)
    w_rows = -(-(heads_dev * 4 * HD + 16) // (16 * PIECES)) * 16 * PIECES
    g_rows = -(-(2 * hidden + width + 16) // 256) * 256
    in_smem = pl.BlockSpec(memory_space=pltpu.SMEM)
    per_seq = lambda: pl.BlockSpec((1, rows, width), lambda s, p: (s, 0, 0))
    per_pair = lambda *tail: pl.BlockSpec((1, 1) + tail, lambda s, p: (s, p, 0, 0))
    shape = jax.ShapeDtypeStruct
    return pl.pallas_call(
        functools.partial(forward_layer, count, heads_dev, block),
        grid=(seqs, pairs),
        in_specs=[in_smem, in_smem, fixed(tok.shape), fixed(embed.shape), per_seq(), fixed(qkv_w.shape),
                  fixed(q_bias.shape), fixed(v_bias.shape), fixed(out_w.shape), fixed(b_out.shape),
                  fixed(w_in.shape), fixed(b_in.shape), fixed(w_last.shape), fixed(b_last.shape)],
        out_specs=[pl.BlockSpec(memory_space=pl.ANY), fixed((pairs, 3 * PAIR, width)),
                   per_pair(rows, PAIR), per_pair(full, PAIR), per_pair(full, PAIR),
                   per_pair(PAIR, rows), per_pair(8, rows),
                   per_seq(), per_seq(), per_seq(), fixed((g_rows, width))],
        out_shape=[
            shape((seqs, full, width), BF16),
            shape((pairs, 3 * PAIR, width), BF16),
            shape((seqs, pairs, rows, PAIR), BF16),
            shape((seqs, pairs, full, PAIR), BF16),
            shape((seqs, pairs, full, PAIR), BF16),
            shape((seqs, pairs, PAIR, rows), F32),
            shape((seqs, pairs, 8, rows), F32),
            shape((seqs, rows, width), BF16),
            shape((seqs, rows, width), BF16),
            shape((seqs, rows, width), BF16),
            shape((g_rows, width), BF16),
        ],
        scratch_shapes=[
            pltpu.VMEM((seqs, full, width), BF16),
            pltpu.VMEM((count, w_rows, width), BF16),
            pltpu.VMEM((width, width), BF16),
            pltpu.VMEM((16, width), F32),
            pltpu.VMEM((2, full, rows), F32),
            pltpu.VMEM((2, PAIR, rows), F32),
            pltpu.VMEM((rows, width), BF16),
            pltpu.VMEM((2 * hidden + width, width), F32),
            pltpu.VMEM((8, width), F32),
            pltpu.SemaphoreType.DMA((seqs, 2 * (count - 1))),
            pltpu.SemaphoreType.DMA((seqs, count)),
            pltpu.SemaphoreType.DMA((seqs,)),
            pltpu.SemaphoreType.DMA((2 * (count - 1),)),
            pltpu.SemaphoreType.DMA((count,)),
            pltpu.SemaphoreType.DMA((3, count - 1)),
            pltpu.SemaphoreType.DMA((3, count - 1)),
        ],
        cost_estimate=pl.CostEstimate(flops=120 * 10 ** 9, bytes_accessed=60 << 20,
                                      transcendentals=seqs * pairs * 2 * full * rows),
        compiler_params=pltpu.CompilerParams(
            collective_id=0, has_side_effects=True, vmem_limit_bytes=VMEM_LIMIT),
        name="forward_layer",
    )(lengths, pair_ids, tok, embed, cot, qkv_w, q_bias, v_bias, out_w, b_out, w_in, b_in, w_last, b_last)


def row_step(size):
    for step in (256, 160, 128, 80, 64, 32, 16):
        if size % step == 0:
            return step
    return size


def aligned(start, size, unit=16):
    return pl.ds(pl.multiple_of(start, unit), size)


class Reducer:
    def __init__(self, data, land, group, rows, bits, where_at, send_sem, recv_sem, free_sem=None):
        self.data, self.land, self.group = data, land, group
        self.send_sem, self.recv_sem, self.free_sem = send_sem, recv_sem, free_sem
        self.stages, self.landed = [], 0
        start, size = 0, rows
        for axis, bit in bits:
            index = where_at[axis]
            digit = (index // bit) % 2
            halves = (size // 2) % 16 == 0
            if halves:
                size //= 2
                keep, other = start + digit * size, start + (1 - digit) * size
            else:
                keep = other = start
            self.stages.append((axis, flip(index, bit), halves, keep, other, size, self.landed))
            self.landed += size
            start = keep
        self.start, self.size = start, size

    def copy(self, j):
        axis, partner, _, _, other, size, landed = self.stages[j]
        return pltpu.make_async_remote_copy(
            src_ref=self.data.at[self.group, :, aligned(other, size)],
            dst_ref=self.land.at[self.group, :, pl.ds(landed, size)],
            send_sem=self.send_sem.at[self.group, j],
            recv_sem=self.recv_sem.at[self.group, j],
            device_id={axis: partner}, device_id_type=MESH)

    def finish(self, j):
        self.copy(j).wait()
        axis, partner, halves, keep, _, size, landed = self.stages[j]
        if self.free_sem is not None and halves:
            pl.semaphore_signal(self.free_sem.at[self.group, j], 1, device_id={axis: partner},
                                device_id_type=MESH)
        step = row_step(size)
        slots = self.data.shape[1]
        for slot in range(slots):
            def add(r, _):
                at = aligned(keep + r * step, step)
                more = self.land[self.group, slot, aligned(landed + r * step, step), :]
                self.data[self.group, slot, at, :] = self.data[self.group, slot, at, :] + more
                return 0

            lax.fori_loop(0, size // step, add, 0)

    def back(self, j):
        axis, partner, _, keep, _, size, _ = self.stages[j]
        view = self.data.at[self.group, :, aligned(keep, size)]
        at = len(self.stages) + j
        return pltpu.make_async_remote_copy(
            src_ref=view, dst_ref=view, send_sem=self.send_sem.at[self.group, at],
            recv_sem=self.recv_sem.at[self.group, at],
            device_id={axis: partner}, device_id_type=MESH)

    def back_start(self, j):
        pl.semaphore_wait(self.free_sem.at[self.group, j], 1)
        self.back(j).start()

    def events(self, line=None):
        doubling = [j for j in range(len(self.stages)) if self.stages[j][2]][::-1]
        middle = line.events(self.start, self.size) if line else []
        run = [lambda: self.copy(0).start()]
        for j in range(len(self.stages)):
            def after(j=j):
                self.finish(j)
                if j + 1 < len(self.stages):
                    self.copy(j + 1).start()
                elif middle:
                    middle[0]()
                else:
                    self.back_start(doubling[0])
            run.append(after)
        for i in range(1, len(middle)):
            def after_line(i=i):
                middle[i]()
                if i + 1 == len(middle):
                    self.back_start(doubling[0])
            run.append(after_line)
        for i, j in enumerate(doubling):
            def after_back(i=i, j=j):
                self.back(j).wait()
                if i + 1 < len(doubling):
                    self.back_start(doubling[i + 1])
            run.append(after_back)
        return run


class Line:
    def __init__(self, data, land, group, landed, place, send_sem, recv_sem):
        self.data, self.land, self.group, self.landed = data, land, group, landed
        self.place, self.send_sem, self.recv_sem = place, send_sem, recv_sem
        self.end = (place == 0) | (place == 3)
        self.inner = (place == 1) | (place == 2)

    def copy(self, step, target, start, size):
        return pltpu.make_async_remote_copy(
            src_ref=self.data.at[self.group, :, aligned(start, size)],
            dst_ref=self.land.at[self.group, :, pl.ds(self.landed + step * size, size)],
            send_sem=self.send_sem.at[self.group, step], recv_sem=self.recv_sem.at[self.group, step],
            device_id={"mp": target}, device_id_type=MESH)

    def events(self, start, size):
        inward = jnp.where(self.place < 2, 1, 2)
        across = jnp.where(self.place < 2, 2, 1)
        outward = jnp.where(self.place < 2, 0, 3)
        first = self.copy(0, inward, start, size)
        second = self.copy(1, across, start, size)
        third = self.copy(2, outward, start, size)
        unit = row_step(size)

        def take(step, add):
            def move(r, _):
                at = aligned(start + r * unit, unit)
                more = self.land[self.group, 0, aligned(self.landed + step * size + r * unit, unit), :]
                if add:
                    more = self.data[self.group, 0, at, :] + more
                self.data[self.group, 0, at, :] = more
                return 0

            lax.fori_loop(0, size // unit, move, 0)

        def begin():
            pl.when(self.end)(first.start)

        def swap():
            @pl.when(self.inner)
            def _():
                first.wait_recv()
                take(0, True)
                second.start()

        def hand_back():
            @pl.when(self.inner)
            def _():
                second.wait()
                take(1, True)
                third.start()

        def close():
            @pl.when(self.inner)
            def _():
                third.wait_send()

            @pl.when(self.end)
            def _():
                first.wait_send()
                third.wait_recv()
                take(2, False)

        return [begin, swap, hand_back, close]


def bit_list(size):
    return [1 << b for b in range(size.bit_length() - 1)]


def far_first(count):
    table = []
    for m in range(count):
        order = []
        for k in range(count - 1, 0, -1):
            order += [c for c in (m + k, m - k) if 0 <= c < count]
        table.append(order + [m])
    return table


def backward_layer(count, data_count, heads_dev, tail_points,
                   lengths, pair_ids, x_seq, weight, q_in, k_in, v_in, att_t, lse, grad_in, mixed_grad, g_in,
                   token_grad, g_out, own_out,
                   a_buf, a_land, b_buf, b_land, b_parts, own_buf, parts, land, x_acc, dq_acc, delta_all,
                   w_acc, bias_acc, col_acc, table_acc,
                   load_sem, a_send, a_recv, a_free, l_send, l_recv, b_send, b_recv, s_send, s_recv, r_send, r_recv):
    seq, turn = pl.program_id(0), pl.program_id(1)
    seqs, pairs = token_grad.shape[0], weight.shape[0]
    rows, width = token_grad.shape[1], token_grad.shape[2]
    place, data_at = lax.axis_index("mp"), lax.axis_index("dp")
    where_at = {"mp": place, "dp": data_at}
    point = seq * count + turn
    data_bits, place_bits = bit_list(data_count), bit_list(count)
    swapped = [{2: 4, 4: 2}.get(b, b) for b in data_bits]

    order = far_first(count)
    chunk = sum(jnp.where((place == m) & (turn == i), order[m][i], 0)
                for m in range(count) for i in range(count))

    in_line = count == 4
    a_sums = [
        Reducer(a_buf, a_land, g, a_buf.shape[2],
                [("dp", b) for b in (data_bits, swapped)[g]] + [("mp", b) for b in place_bits if not in_line],
                where_at, a_send, a_recv, a_free)
        for g in range(2)]
    a_events = [
        a.events(Line(a_buf, a_land, g, a.landed, place, l_send, l_recv) if in_line else None)
        for g, a in enumerate(a_sums)]
    b_sums = [
        Reducer(b_buf, b_land, g, b_buf.shape[2], [("dp", b) for b in (data_bits, swapped)[g]],
                where_at, b_send, b_recv)
        for g in range(2)]

    def send_part(s, c, downward):
        slot = jnp.where((place - 1 == c) & (downward == 1), count, c)
        return pltpu.make_async_remote_copy(
            src_ref=parts.at[s, c], dst_ref=land.at[s, slot],
            send_sem=s_send.at[s, c], recv_sem=s_recv.at[s, slot],
            device_id={"mp": place - 1 if downward else place + 1}, device_id_type=MESH)

    def await_part(s, slot):
        pltpu.make_async_remote_copy(
            src_ref=land.at[s, slot], dst_ref=land.at[s, slot],
            send_sem=s_send.at[s, 0], recv_sem=s_recv.at[s, slot],
            device_id={"mp": (place + 1) % count}, device_id_type=MESH).wait_recv()

    def combine(s, k):
        for downward in (0, 1):
            c = place - k if downward else place + k
            go = ((c >= 0) & (place + 1 < count)) if downward else ((c < count) & (place >= 1))

            @pl.when(go)
            def _():
                await_part(s, c)
                parts[s, c] = parts[s, c] + land[s, c]
                send_part(s, c, downward).start()

    def conclude(s):
        for downward in (0, 1):
            slot = count if downward else place

            @pl.when((place + 1 < count) if downward else (place >= 1))
            def _():
                await_part(s, slot)
                token_grad[s] += land[s, slot].astype(F32)

    def load():
        return pltpu.make_async_copy(g_in, a_buf, load_sem.at[0])

    def store():
        return pltpu.make_async_copy(a_buf, g_out, load_sem.at[1])

    partners = [flip(data_at, b) for b in data_bits]

    @pl.when(point == 0)
    def _():
        greet(place, count, partners)
        load().start()
        w_acc[...] = jnp.zeros_like(w_acc)
        bias_acc[...] = jnp.zeros_like(bias_acc)
        table_acc[...] = jnp.zeros_like(table_acc)
        await_greetings(count, partners)
        load().wait()
        for events in a_events:
            events[0]()

    @pl.when(turn == 0)
    def _():
        col_acc[...] = jnp.zeros_like(col_acc)
        dq_acc[...] = jnp.zeros_like(dq_acc)
        for p in range(pairs):
            prod = grad_in[0, :, p * PAIR:(p + 1) * PAIR].astype(F32).T * att_t[0, p]
            delta_all[p, 0:1, :] = jnp.sum(prod[:HD], axis=0, keepdims=True)
            delta_all[p, 1:2, :] = jnp.sum(prod[HD:], axis=0, keepdims=True)

    length = lengths[seq]
    at = aligned(chunk * rows, rows, rows)
    own = aligned(place * rows, rows, rows)
    x_acc[...] = jnp.zeros_like(x_acc)

    def pair_step(p, _):
        lanes = aligned(p * PAIR, PAIR, PAIR)
        q_pair = q_in[0, p]
        grad_pair = grad_in[0, :, lanes]
        k_blk = k_in[0, p, at, :]
        v_blk = v_in[0, p, at, :]
        keep = (lax.broadcasted_iota(jnp.int32, (rows, rows), 0) + chunk * rows) < length
        dk = jnp.zeros((rows, PAIR), F32)
        dv = jnp.zeros((rows, PAIR), F32)
        for h in range(2):
            q_head, g_head = one_head(q_pair, h), one_head(grad_pair, h)
            s = jnp.where(keep, nt(k_blk, q_head) * LOG2E, NEGATIVE)
            pr = jnp.exp2(s - lse[0, p, h:h + 1, :])
            dp = nt(v_blk, g_head)
            ds = (pr * (dp - delta_all[p, h:h + 1, :])).astype(BF16)
            dv += nn(pr.astype(BF16), g_head)
            dk += nn(ds, q_head)
            dq_acc[p, h] += tn(k_blk, ds)
        dv = dv.astype(BF16)
        both = jnp.concatenate([dk.astype(BF16), dv], axis=1)
        x_acc[...] += nn(both, weight[p, PAIR:, :])
        w_acc[p, PAIR:, :] += tn(both, x_seq[0, at, :])
        bias_acc[1:2, lanes] += jnp.sum(dv.astype(F32), axis=0, keepdims=True)
        return 0

    lax.fori_loop(0, pairs, pair_step, 0, unroll=4)

    @pl.when(turn < count - 1)
    def _():
        parts[seq, chunk] = x_acc[...].astype(BF16)
        for downward in (0, 1):
            @pl.when((place == (count - 1 if downward else 0)) & (chunk != place))
            def _():
                send_part(seq, chunk, downward).start()

    @pl.when(turn == count - 1)
    def _():
        def query_step(p, _):
            lanes = aligned(p * PAIR, PAIR, PAIR)
            dq_t = jnp.concatenate(
                [dq_acc[p, h, h * HD:(h + 1) * HD, :] for h in range(2)], axis=0) * (HD ** -0.5)
            dq = dq_t.T.astype(BF16)
            x_acc[...] += nn(dq, weight[p, :PAIR, :])
            w_acc[p, :PAIR, :] += tn(dq, x_seq[0, own, :])
            bias_acc[0:1, lanes] += jnp.sum(dq.astype(F32), axis=0, keepdims=True)
            return 0

        lax.fori_loop(0, pairs, query_step, 0)
        x_acc[...] += mixed_grad[0].astype(F32)
        token_grad[seq] = x_acc[...]

    col_acc[0:1, :] += jnp.sum(x_acc[...], axis=0, keepdims=True)

    @pl.when(turn == count - 1)
    def _():
        line = lax.broadcasted_iota(jnp.int32, table_acc.shape, 0)
        table_acc[...] += jnp.where(line == pair_ids[seq], col_acc[0:1, :], 0.0)

    slots = {2: 2, 1: 4} if count == 4 else {k: count + (count - 2 - k) for k in range(1, count - 1)}
    for k in range(count - 2, 0, -1):
        turns, seq_back = slots[k] % count, slots[k] // count

        @pl.when((turn == turns) & (seq >= seq_back))
        def _():
            combine(seq - seq_back, k)

    @pl.when((turn == count - 1) & (seq >= 1))
    def _():
        conclude(seq - 1)

    total = seqs * count
    later = len(a_events[0]) - 1
    in_tail = []
    for e in range(1, later + 1):
        when_at = tail_points[e - 1] if tail_points else (e * total) // (later + 1)
        if when_at >= total:
            in_tail.append(e)
            continue

        @pl.when(point == when_at)
        def _():
            for events in a_events:
                events[e]()

    @pl.when(point == total - 1)
    def _():
        last = seqs - 1
        base = heads_dev * 3 * HD
        half = count // 2
        for m in range(count):
            g, slot = m // half, m % half
            if heads_dev == 2:
                b_buf[g, slot, 0:base, :] = w_acc[m].astype(BF16)
            else:
                for j in range(3):
                    lo = j * PAIR + (m % 2) * HD
                    b_buf[g, slot, j * HD:(j + 1) * HD, :] = w_acc[m // 2, lo:lo + HD, :].astype(BF16)
            b_buf[g, slot, base:base + 16, :] = bias_acc[...].astype(BF16)
            b_buf[g, slot, base + 16:base + 32, :] = table_acc[...].astype(BF16)
            rest = b_buf.shape[2] - base - 32
            b_buf[g, slot, base + 32:, :] = jnp.zeros((rest, width), BF16)
        stages = len(b_sums[0].stages)
        for b in b_sums:
            b.copy(0).start()
        tail_k = [k for k in range(count - 2, 0, -1) if slots[k] >= count]
        for j in range(stages):
            for b in b_sums:
                b.finish(j)
                if j + 1 < stages:
                    b.copy(j + 1).start()
            if tail_k:
                combine(last, tail_k.pop(0))
        strip = b_sums[0].size
        mine = place // half
        start = jnp.where(mine == 0, b_sums[0].start, b_sums[1].start)

        def scatter(k):
            target = (place + k) % count
            g = target // half
            begin = jnp.where(g == 0, b_sums[0].start, b_sums[1].start)
            return pltpu.make_async_remote_copy(
                src_ref=b_buf.at[g, target % half, aligned(begin, strip)],
                dst_ref=b_parts.at[k - 1],
                send_sem=r_send.at[k - 1], recv_sem=r_recv.at[k - 1],
                device_id={"mp": target}, device_id_type=MESH)

        for k in range(1, count):
            scatter(k).start()
        for k in tail_k:
            combine(last, k)
        for e in in_tail:
            for events in a_events:
                events[e]()
        store().start()
        for k in range(1, count):
            scatter(k).wait()
        home = b_buf[mine, place % half, aligned(start, strip), :].astype(F32)
        for k in range(1, count):
            home += b_parts[k - 1].astype(F32)
        own_buf[aligned(start, strip), :] = home.astype(BF16)

        def back(j):
            partner = jnp.where(mine == 0, b_sums[0].stages[j][1], b_sums[1].stages[j][1])
            keep = jnp.where(mine == 0, b_sums[0].stages[j][3], b_sums[1].stages[j][3])
            size = b_sums[0].stages[j][5]
            view = own_buf.at[aligned(keep, size)]
            return pltpu.make_async_remote_copy(
                src_ref=view, dst_ref=view, send_sem=r_send.at[count - 1 + j],
                recv_sem=r_recv.at[count - 1 + j], device_id={"dp": partner}, device_id_type=MESH)

        for j in reversed(range(stages)):
            back(j).start()
            back(j).wait()
        own_out[...] = own_buf[...]
        conclude(last)
        store().wait()
        for s in range(seqs):
            for k in range(1, count):
                for downward in (0, 1):
                    c = place - k if downward else place + k

                    @pl.when((c >= 0) if downward else (c < count))
                    def _():
                        send_part(s, c, downward).wait_send()


def call_backward(count, data_count, heads_dev, lengths, pair_ids, x_all, weight, q, k, v, att_t, lse,
                  grad, mixed_grad, g_all):
    seqs, full, width = x_all.shape
    rows = full // count
    pairs = weight.shape[0]
    a_rows = g_all.shape[0] // 2
    base = heads_dev * 3 * HD
    slot_rows = -(-(base + 32) // 128) * 128
    data_bits, place_bits = bit_list(data_count), bit_list(count)

    def landing(size, bits):
        landed = 0
        for _ in range(bits):
            size = size // 2 if (size // 2) % 16 == 0 else size
            landed += size
        return landed, size

    if count == 4:
        a_landed, strip = landing(a_rows, len(data_bits))
        a_landed += 3 * strip
    else:
        a_landed, _ = landing(a_rows, len(data_bits) + len(place_bits))
    b_landed, strip = landing(slot_rows, len(data_bits))
    a_stages, b_stages = len(data_bits) + len(place_bits), len(data_bits)
    tail_points = TAIL_POINTS if (count, data_count) == (4, 8) else None
    in_smem = pl.BlockSpec(memory_space=pltpu.SMEM)
    in_hbm = pl.BlockSpec(memory_space=pl.ANY)
    seq_block = lambda shape, mode=None: pl.BlockSpec(
        (1,) + shape[1:], lambda s, i: (s,) + (0,) * (len(shape) - 1), pipeline_mode=mode)
    shape = jax.ShapeDtypeStruct
    dma = pltpu.SemaphoreType.DMA
    return pl.pallas_call(
        functools.partial(backward_layer, count, data_count, heads_dev, tail_points),
        grid=(seqs, count),
        in_specs=[in_smem, in_smem, seq_block(x_all.shape, CONSTANT), fixed(weight.shape),
                  seq_block(q.shape, CONSTANT), seq_block(k.shape, CONSTANT),
                  seq_block(v.shape, CONSTANT), seq_block(att_t.shape, CONSTANT),
                  seq_block(lse.shape), seq_block(grad.shape), seq_block(mixed_grad.shape), in_hbm],
        out_specs=[fixed((seqs, rows, width)), in_hbm, fixed((slot_rows, width))],
        out_shape=[
            shape((seqs, rows, width), F32),
            shape((2, 1, a_rows, width), BF16),
            shape((slot_rows, width), BF16),
        ],
        scratch_shapes=[
            pltpu.VMEM((2, 1, a_rows, width), BF16),
            pltpu.VMEM((2, 1, a_landed, width), BF16),
            pltpu.VMEM((2, count // 2, slot_rows, width), BF16),
            pltpu.VMEM((2, count // 2, b_landed, width), BF16),
            pltpu.VMEM((count - 1, strip, width), BF16),
            pltpu.VMEM((slot_rows, width), BF16),
            pltpu.VMEM((seqs, count, rows, width), BF16),
            pltpu.VMEM((seqs, count + 1, rows, width), BF16),
            pltpu.VMEM((rows, width), F32),
            pltpu.VMEM((pairs, 2, PAIR, rows), F32),
            pltpu.VMEM((pairs, 8, rows), F32),
            pltpu.VMEM((pairs, 3 * PAIR, width), F32),
            pltpu.VMEM((16, width), F32),
            pltpu.VMEM((8, width), F32),
            pltpu.VMEM((16, width), F32),
            dma((2,)), dma((2, 2 * a_stages)), dma((2, 2 * a_stages)),
            pltpu.SemaphoreType.REGULAR((2, a_stages)), dma((2, 3)), dma((2, 3)),
            dma((2, b_stages)), dma((2, b_stages)),
            dma((seqs, count)), dma((seqs, count + 1)),
            dma((count - 1 + b_stages,)), dma((count - 1 + b_stages,)),
        ],
        cost_estimate=pl.CostEstimate(flops=200 * 10 ** 9, bytes_accessed=60 << 20,
                                      transcendentals=seqs * pairs * 2 * full * rows),
        compiler_params=pltpu.CompilerParams(
            collective_id=1, has_side_effects=True, vmem_limit_bytes=VMEM_LIMIT),
        name="backward_layer",
    )(lengths, pair_ids, x_all, weight, q, k, v, att_t, lse, grad, mixed_grad,
      g_all.reshape(2, 1, a_rows, width))


def finish(place_ref, sums, own, token_in, result_in, last_grad, in_grad, small_sums, out_grad,
           qkv_grad, q_bias_grad, v_bias_grad, table, token_out, result_out, *, heads_dev, hidden):
    part = pl.program_id(0)
    width = own.shape[1]
    place = place_ref[0]
    last_grad[...] = sums[pl.ds(pl.multiple_of(part * width, width), width), :].astype(F32)
    in_grad[...] = sums[pl.ds(pl.multiple_of(hidden + part * width, width), width), :].astype(F32)
    token_out[...] = token_in[...]
    result_out[...] = result_in[...]

    @pl.when(part == 0)
    def _():
        base = heads_dev * 3 * HD
        out_rows = out_grad.shape[0]
        out_grad[...] = sums[
            pl.ds(pl.multiple_of(2 * hidden + place * out_rows, out_rows), out_rows), :].astype(F32)
        small_sums[...] = sums[2 * hidden + width:2 * hidden + width + 16, :].astype(F32)[:8]
        turned = own[:base, :].astype(F32).T
        parts = []
        for h in range(heads_dev):
            for j in range(3):
                lo = (j * heads_dev + h) * HD
                parts.append(turned[:, lo:lo + HD])
        qkv_grad[...] = jnp.concatenate(parts, axis=1)
        rows = own[base:base + 16, :].astype(F32)
        q_bias_grad[...] = rows[0:1]
        v_bias_grad[...] = rows[1:2]
        table[...] = own[base + 16:base + 32, :].astype(F32)[:table.shape[0]]


def call_finish(place, sums, own, token_grad, result, heads_dev, hidden, table_rows):
    seqs, rows, width = token_grad.shape
    parts = hidden // width
    base = heads_dev * 3 * HD
    out_rows = heads_dev * HD
    shape = jax.ShapeDtypeStruct
    strip = lambda: pl.BlockSpec((seqs, rows // parts, width), lambda i, *_: (0, i, 0))
    return pl.pallas_call(
        functools.partial(finish, heads_dev=heads_dev, hidden=hidden),
        grid_spec=pltpu.PrefetchScalarGridSpec(
            num_scalar_prefetch=1,
            grid=(parts,),
            in_specs=[fixed(sums.shape), fixed(own.shape), strip(), strip()],
            out_specs=[pl.BlockSpec((width, width), lambda i, *_: (i, 0)),
                       pl.BlockSpec((width, width), lambda i, *_: (0, i)),
                       fixed((8, width)), fixed((out_rows, width)), fixed((width, base)),
                       fixed((1, width)), fixed((1, width)), fixed((table_rows, width)),
                       strip(), strip()],
        ),
        out_shape=[shape((hidden, width), F32), shape((width, hidden), F32), shape((8, width), F32),
                   shape((out_rows, width), F32), shape((width, base), F32), shape((1, width), F32),
                   shape((1, width), F32), shape((table_rows, width), F32),
                   shape(token_grad.shape, F32), shape(result.shape, BF16)],
        compiler_params=pltpu.CompilerParams(vmem_limit_bytes=VMEM_LIMIT),
        name="finish",
    )(place, sums, own, token_grad, result)


def body(
    tokens,
    pair_ids,
    lengths,
    pair_embed,
    qkv_weight,
    q_bias,
    v_bias,
    out_weight,
    out_bias,
    ffn_in_weight,
    ffn_in_bias,
    ffn_out_weight,
    ffn_out_bias,
    cotangent,
):
    local_rows, seqs, width = tokens.shape
    table_rows = pair_embed.shape[0]
    count = lax.axis_size("mp")
    place = lax.axis_index("mp").astype(jnp.int32).reshape(1)
    tok = jnp.transpose(tokens, (1, 0, 2))
    cot = jnp.transpose(cotangent, (1, 0, 2))
    bias_len = q_bias.shape[0]
    spread = lambda v: lax.dynamic_update_slice(
        jnp.zeros((1, width), BF16), v[None], (0, place[0] * bias_len))
    (x_all, w_pairs, q, k, v, att_t, lse, result, mixed_grad, att_grad, g_all) = call_layer(
        count, lengths, pair_ids, tok, pair_embed, cot, qkv_weight, spread(q_bias), spread(v_bias),
        out_weight, out_bias[None], ffn_in_weight, ffn_in_bias[None], ffn_out_weight,
        ffn_out_bias[None])
    heads_dev = bias_len // HD
    tokens_grad, g_sum, own = call_backward(
        count, lax.axis_size("dp"), heads_dev, lengths, pair_ids, x_all, w_pairs, q, k, v, att_t, lse,
        att_grad, mixed_grad, g_all)

    hidden = ffn_in_weight.shape[1]
    (g_last_sum, g_in_sum, small, g_out_own, qkv_sum, qb_sum, vb_sum, table_sum, tokens_grad,
     result) = call_finish(
        place, g_sum.reshape(-1, width), own, tokens_grad, result, heads_dev, hidden, table_rows)
    at = hidden // width
    own_bias = lambda v: lax.dynamic_slice_in_dim(v[0], place[0] * bias_len, bias_len)
    return (
        jnp.transpose(result, (1, 0, 2)),
        jnp.transpose(tokens_grad, (1, 0, 2)),
        table_sum,
        qkv_sum,
        own_bias(qb_sum),
        own_bias(vb_sum),
        g_out_own,
        small[at + 1],
        g_in_sum,
        small[:at].reshape(-1),
        g_last_sum,
        small[at],
    )


def solution(mesh):
    return jax.shard_map(
        body,
        mesh=mesh,
        in_specs=(
            P("mp", "dp", None),
            P("dp"),
            P("dp"),
            P(),
            P(None, "mp"),
            P("mp"),
            P("mp"),
            P("mp", None),
            P(),
            P(),
            P(),
            P(),
            P(),
            P("mp", "dp", None),
        ),
        out_specs=(
            P("mp", "dp", None),
            P("mp", "dp", None),
            P(),
            P(None, "mp"),
            P("mp"),
            P("mp"),
            P("mp", None),
            P(),
            P(),
            P(),
            P(),
            P(),
        ),
        check_vma=False,
    )
```

```python
import functools
import math

import jax
import jax.numpy as jnp
from jax import lax
from jax.experimental import pallas as pl
from jax.experimental.pallas import tpu as pltpu
from jax.sharding import PartitionSpec as P

HD = 64
PAIR = 2 * HD
NEGATIVE = -1e30
LOG2E = math.log2(math.e)
F32 = jnp.float32
BF16 = jnp.bfloat16
VMEM_LIMIT = 60 * 1024 * 1024


def nn(a, b):
    return jnp.dot(a, b, preferred_element_type=F32)


def nt(a, b):
    return lax.dot_general(a, b, (((1,), (1,)), ((), ())), preferred_element_type=F32)


def tn(a, b):
    return lax.dot_general(a, b, (((0,), (0,)), ((), ())), preferred_element_type=F32)


def head_lanes(rows, head):
    lane = lax.broadcasted_iota(jnp.int32, (rows, PAIR), 1)
    return (lane >= head * HD) & (lane < (head + 1) * HD)


def one_head(pair_rows, head):
    return jnp.where(head_lanes(pair_rows.shape[0], head), pair_rows, jnp.zeros_like(pair_rows))


def fold8(values, op):
    rows, lanes = values.shape
    return op(values.reshape(rows // 8, 8, lanes), axis=0)


MESH = pl.DeviceIdType.MESH
CONSTANT = pl.Buffered(1)
PIECES = 8
UNROLL = 4
TAIL_POINTS = (0, 2, 3, 5, 7, 9, 10, 12, 12)


class Relay:
    def __init__(self, place, count, view, send_sem, recv_sem):
        self.place, self.count, self.view = place, count, view
        self.send_sem, self.recv_sem = send_sem, recv_sem

    def copy(self, chunk, downward, step):
        return pltpu.make_async_remote_copy(
            src_ref=self.view(chunk), dst_ref=self.view(chunk),
            send_sem=self.send_sem(downward, step), recv_sem=self.recv_sem(chunk),
            device_id={"mp": self.place - 1 if downward else self.place + 1},
            device_id_type=MESH)

    def each(self, step):
        for downward in (0, 1):
            chunk = self.place + step if downward else self.place - step
            exists = chunk < self.count if downward else chunk >= 0
            onward = self.place >= 1 if downward else self.place + 1 < self.count
            yield downward, chunk, exists, onward

    def advance(self, step):
        for downward, chunk, exists, onward in self.each(step):
            if step:
                @pl.when(exists)
                def _():
                    self.copy(chunk, downward, step).wait_recv()
            if step < self.count - 1:
                @pl.when(exists & onward)
                def _():
                    self.copy(chunk, downward, step).start()

    def drain(self):
        for step in range(self.count - 1):
            for downward, chunk, exists, onward in self.each(step):
                @pl.when(exists & onward)
                def _():
                    self.copy(chunk, downward, step).wait_send()


def greet(place, count, partners):
    barrier = pltpu.get_barrier_semaphore()
    for partner in partners:
        pl.semaphore_signal(barrier, 1, device_id={"dp": partner}, device_id_type=MESH)
    for k in range(1, count):
        pl.semaphore_signal(barrier, 1, device_id={"mp": (place + k) % count}, device_id_type=MESH)


def await_greetings(count, partners):
    pl.semaphore_wait(pltpu.get_barrier_semaphore(), len(partners) + count - 1)


def flip(index, bit):
    return index + bit - 2 * bit * ((index // bit) % 2)


def near_first(count):
    return [order[::-1] for order in far_first(count)]


def forward_layer(count, heads_dev,
                  lengths, pair_ids, tok, embed, cot, qkv_w, q_bias, v_bias, out_w, b_out,
                  w_in, b_in, w_last, b_last,
                  x_out, w_out, q_out, k_out, v_out, att_t_out, lse_out,
                  result, mixed_grad, att_grad, g_all,
                  x_all, w_all, w_o, bias_land, biases, acc, stats, att_rows_all, grads, grad_rows,
                  x_send, x_recv, x_copy, w_send, w_recv, plane_send, plane_recv, bias_send, bias_recv):
    seq, turn = pl.program_id(0), pl.program_id(1)
    seqs, pairs = tok.shape[0], w_out.shape[0]
    rows, width = tok.shape[1], tok.shape[2]
    hidden = w_in.shape[1]
    base = heads_dev * 4 * HD
    piece_rows = base // PIECES
    place, data_at = lax.axis_index("mp"), lax.axis_index("dp")
    order = near_first(count)
    chunk = sum(jnp.where((place == m) & (turn == i), order[m][i], 0)
                for m in range(count) for i in range(count))

    def x_relay(s):
        return Relay(
            place, count,
            lambda c: x_all.at[s, pl.ds(pl.multiple_of(c * rows, rows), rows)],
            lambda downward, step: x_send.at[s, downward * (count - 1) + step],
            lambda c: x_recv.at[s, c])

    core, near_x, near_y = [(data_at // bit) % 2 for bit in (1, 2, 4)]
    piece = near_x + 2 * near_y + 4 * core

    def w_span(start, size):
        return pl.ds(pl.multiple_of(start * piece_rows, piece_rows), size * piece_rows)

    w_relay = Relay(
        place, count, lambda c: w_all.at[c, w_span(piece, 1)],
        lambda downward, step: w_send.at[downward * (count - 1) + step],
        lambda c: w_recv.at[c])
    partners = [flip(data_at, 2), flip(data_at, 4), flip(flip(data_at, 2), 4), flip(data_at, 1)]

    def plane(stage):
        span = w_span(4 * core, 4) if stage == 3 else w_span(piece, 1)
        copies = []
        for k in range(1, count):
            source = (place + k) % count
            copies.append(pltpu.make_async_remote_copy(
                src_ref=w_all.at[source, span], dst_ref=w_all.at[source, span],
                send_sem=plane_send.at[stage, k - 1], recv_sem=plane_recv.at[stage, k - 1],
                device_id={"dp": partners[stage]}, device_id_type=MESH))
        return copies

    def bias_copies():
        copies = []
        for k in range(1, count):
            copies.append(pltpu.make_async_remote_copy(
                src_ref=bias_land.at[0], dst_ref=bias_land.at[k],
                send_sem=bias_send.at[k - 1], recv_sem=bias_recv.at[k - 1],
                device_id={"mp": (place + k) % count}, device_id_type=MESH))
        return copies

    @pl.when((seq == 0) & (turn == 0))
    def _():
        greet(place, count, partners)
        turned = qkv_w[...].T
        parts = []
        for j in range(3):
            for h in range(heads_dev):
                parts.append(turned[(h * 3 + j) * HD:(h * 3 + j + 1) * HD])
        w_all[place, 0:heads_dev * 3 * HD, :] = jnp.concatenate(parts, axis=0)
        w_all[place, heads_dev * 3 * HD:base, :] = out_w[...]
        line = lax.broadcasted_iota(jnp.int32, bias_land.shape[1:], 0)
        bias_land[0] = jnp.where(
            line == 0, q_bias[...].astype(F32),
            jnp.where(line == 1, v_bias[...].astype(F32), 0.0)).astype(BF16)
        await_greetings(count, partners)
        w_relay.advance(0)
        for copy in bias_copies():
            copy.start()
        own = pl.ds(pl.multiple_of(place * rows, rows), rows)
        for s in range(seqs):
            row = embed[pl.ds(pair_ids[s], 1), :]
            x_all[s, own, :] = (tok[s].astype(F32) + row).astype(BF16)
        if count > 2:
            w_relay.advance(1)
        x_relay(0).advance(0)
        for step in range(2 if count > 2 else 1, count):
            w_relay.advance(step)
        across = [plane(stage) for stage in range(3)]
        for copies in across:
            for copy in copies:
                copy.start()
        grads[...] = jnp.zeros_like(grads)
        grad_rows[...] = jnp.zeros_like(grad_rows)
        for copies in across:
            for copy in copies:
                copy.wait()
        for copy in plane(3):
            copy.start()
        for copy in bias_copies():
            copy.wait()
        for p in range(pairs):
            if heads_dev == 2:
                both = bias_land[(place + count - p) % count].astype(F32)
            else:
                both = jnp.concatenate(
                    [bias_land[(place + count - 2 * p - half) % count].astype(F32) for half in range(2)],
                    axis=1)
            biases[:, p * PAIR:(p + 1) * PAIR] = both
        for copy in plane(3):
            copy.wait()
        w_relay.drain()
        for p in range(pairs):
            if heads_dev == 2:
                w_out[p] = w_all[p, 0:3 * PAIR, :]
                w_o[p * PAIR:(p + 1) * PAIR, :] = w_all[p, 3 * PAIR:4 * PAIR, :]
            else:
                for half in range(2):
                    for j in range(4):
                        strip = w_all[2 * p + half, j * HD:(j + 1) * HD, :]
                        if j < 3:
                            w_out[p, j * PAIR + half * HD:j * PAIR + (half + 1) * HD, :] = strip
                        else:
                            w_o[p * PAIR + half * HD:p * PAIR + (half + 1) * HD, :] = strip

    def hbm_copy(s):
        return pltpu.make_async_copy(x_all.at[s], x_out.at[s], x_copy.at[s])

    for t in range(1, count):
        @pl.when((seq == 0) & (turn == t))
        def _():
            x_relay(0).advance(t)
    for t in range(2, count - 1):
        @pl.when((seq >= 1) & (turn == t - 1))
        def _():
            x_relay(seq).advance(t)
    if count > 2:
        @pl.when((seq >= 1) & (turn == count - 1))
        def _():
            x_relay(seq).advance(count - 1)

    ahead = jnp.where(seq == 0, max(count - 2, 0), max(count - 3, 0))

    @pl.when((turn == ahead) & (seq + 1 < seqs))
    def _():
        x_relay(seq + 1).advance(0)

    length = lengths[seq]
    own = pl.ds(pl.multiple_of(place * rows, rows), rows)
    at = pl.ds(pl.multiple_of(chunk * rows, rows), rows)

    @pl.when(turn == 0)
    def _():
        acc[...] = jnp.zeros_like(acc)
        line = lax.broadcasted_iota(jnp.int32, stats.shape, 1)
        stats[...] = jnp.where(line < 2, NEGATIVE, 0.0)

        def query_step(p, _):
            lanes = pl.ds(pl.multiple_of(p * PAIR, PAIR), PAIR)
            q_pair = (nt(x_all[seq, own, :], w_out[p, 0:PAIR, :]) + biases[0:1, lanes]).astype(BF16)
            q_out[0, p] = q_pair * BF16(HD ** -0.5)
            return 0

        lax.fori_loop(0, pairs, query_step, 0)

    for p in range(pairs):
        kv = nt(x_all[seq, at, :], w_out[p, PAIR:3 * PAIR, :])
        k_out[0, p, at, :] = kv[:, :PAIR].astype(BF16)
        v_out[0, p, at, :] = (kv[:, PAIR:] + biases[1:2, p * PAIR:(p + 1) * PAIR]).astype(BF16)

    def pair_step(p, _):
        k_blk, v_blk, q_pair = k_out[0, p, at, :], v_out[0, p, at, :], q_out[0, p]
        keep = (lax.broadcasted_iota(jnp.int32, (rows, rows), 0) + chunk * rows) < length
        scores = [jnp.where(keep, nt(k_blk, one_head(q_pair, h)), NEGATIVE) for h in range(2)]
        before = [stats[p, h:h + 1, :] for h in range(2)]
        tops = [jnp.maximum(before[h], jnp.max(scores[h], axis=0, keepdims=True) * LOG2E) for h in range(2)]
        probs = [jnp.exp2(scores[h] * LOG2E - tops[h]) for h in range(2)]
        added = tn(v_blk, jnp.concatenate([pr.astype(BF16) for pr in probs], axis=1))
        for h in range(2):
            half = slice(h * HD, (h + 1) * HD)
            shrink = jnp.exp2(before[h] - tops[h])
            stats[p, h:h + 1, :] = tops[h]
            stats[p, 2 + h:3 + h, :] = (
                stats[p, 2 + h:3 + h, :] * shrink + jnp.sum(probs[h], axis=0, keepdims=True))
            acc[p, half, :] = acc[p, half, :] * shrink + added[half, h * rows:(h + 1) * rows]
        return 0

    lax.fori_loop(0, pairs, pair_step, 0, unroll=UNROLL)

    @pl.when(turn == count - 1)
    def _():
        hbm_copy(seq).start()

        @pl.when(seq + 1 < seqs)
        def _():
            x_relay(seq + 1).advance(1)
        for p in range(pairs):
            total = stats[p, 2:4, :]
            inverse = 1.0 / total
            att_t = jnp.concatenate(
                [acc[p, h * HD:(h + 1) * HD, :] * inverse[h:h + 1] for h in range(2)], axis=0)
            att_t_out[0, p] = att_t
            att_rows_all[:, p * PAIR:(p + 1) * PAIR] = att_t.T.astype(BF16)
            lse_out[0, p] = jnp.concatenate(
                [stats[p, 0:2, :] + jnp.log2(total), jnp.zeros((6, rows), F32)], axis=0)

        cot_rows = cot[0]
        att_rows = att_rows_all[...]
        row = embed[pl.ds(pair_ids[seq], 1), :]
        mixed = (tok[seq].astype(F32) + row) + (nn(att_rows, w_o[...]) + b_out[...])
        mixed_low = mixed.astype(BF16)
        out_sum = mixed + b_last[...]
        back_sum = cot_rows.astype(F32)
        root = math.sqrt(2.0 / math.pi)
        for c in range(hidden // width):
            at = slice(c * width, (c + 1) * width)
            pre = nn(mixed_low, w_in[:, at]) + b_in[:, at]
            square = pre * pre
            th = jnp.tanh(root * pre * (1.0 + 0.044715 * square))
            half = 0.5 * (1.0 + th)
            act = (pre * half).astype(BF16)
            slope = half + (0.5 * root) * pre * (1.0 - th * th) * (1.0 + (3 * 0.044715) * square)
            out_sum += nn(act, w_last[at, :])
            back = (nt(cot_rows, w_last[at, :]) * slope).astype(BF16)
            grad_rows[c:c + 1, :] += jnp.sum(back.astype(F32), axis=0, keepdims=True)
            back_sum += nt(back, w_in[:, at])
            grads[at, :] += tn(act, cot_rows)
            grads[hidden + c * width:hidden + (c + 1) * width, :] += tn(mixed_low, back)
        result[0] = out_sum.astype(BF16)
        back_low = back_sum.astype(BF16)
        mixed_grad[0] = back_low
        at = hidden // width
        grad_rows[at:at + 1, :] += jnp.sum(cot_rows.astype(F32), axis=0, keepdims=True)
        grad_rows[at + 1:at + 2, :] += jnp.sum(back_low.astype(F32), axis=0, keepdims=True)
        grads[2 * hidden:, :] += tn(att_rows, back_low)
        att_grad[0] = nt(back_low, w_o[...]).astype(BF16)

    @pl.when((seq == seqs - 1) & (turn == count - 1))
    def _():
        def narrow(j, _):
            at = pl.ds(pl.multiple_of(j * width, width), width)
            g_all[at, :] = grads[at, :].astype(BF16)
            return 0

        lax.fori_loop(0, grads.shape[0] // width, narrow, 0)
        rest = g_all.shape[0] - grads.shape[0]
        g_all[grads.shape[0]:, :] = jnp.concatenate(
            [grad_rows[...], jnp.zeros((rest - 8, width), F32)], axis=0).astype(BF16)
        for s in range(seqs):
            x_relay(s).drain()
            hbm_copy(s).wait()


def fixed(shape):
    return pl.BlockSpec(shape, lambda *_: (0,) * len(shape), pipeline_mode=CONSTANT)


def call_layer(count, lengths, pair_ids, tok, embed, cot, qkv_w, q_bias, v_bias, out_w, b_out,
               w_in, b_in, w_last, b_last):
    seqs, rows, width = tok.shape
    hidden = w_in.shape[1]
    heads_dev = qkv_w.shape[1] // (3 * HD)
    full = count * rows
    pairs = width // PAIR
    g_rows = -(-(2 * hidden + width + 16) // 256) * 256
    in_smem = pl.BlockSpec(memory_space=pltpu.SMEM)
    per_seq = lambda: pl.BlockSpec((1, rows, width), lambda s, p: (s, 0, 0))
    per_pair = lambda *tail: pl.BlockSpec((1, pairs) + tail, lambda s, p: (s, 0, 0, 0))
    shape = jax.ShapeDtypeStruct
    return pl.pallas_call(
        functools.partial(forward_layer, count, heads_dev),
        grid=(seqs, count),
        in_specs=[in_smem, in_smem, fixed(tok.shape), fixed(embed.shape), per_seq(), fixed(qkv_w.shape),
                  fixed(q_bias.shape), fixed(v_bias.shape), fixed(out_w.shape), fixed(b_out.shape),
                  fixed(w_in.shape), fixed(b_in.shape), fixed(w_last.shape), fixed(b_last.shape)],
        out_specs=[pl.BlockSpec(memory_space=pl.ANY), fixed((pairs, 3 * PAIR, width)),
                   per_pair(rows, PAIR), per_pair(full, PAIR), per_pair(full, PAIR),
                   per_pair(PAIR, rows), per_pair(8, rows),
                   per_seq(), per_seq(), per_seq(), fixed((g_rows, width))],
        out_shape=[
            shape((seqs, full, width), BF16),
            shape((pairs, 3 * PAIR, width), BF16),
            shape((seqs, pairs, rows, PAIR), BF16),
            shape((seqs, pairs, full, PAIR), BF16),
            shape((seqs, pairs, full, PAIR), BF16),
            shape((seqs, pairs, PAIR, rows), F32),
            shape((seqs, pairs, 8, rows), F32),
            shape((seqs, rows, width), BF16),
            shape((seqs, rows, width), BF16),
            shape((seqs, rows, width), BF16),
            shape((g_rows, width), BF16),
        ],
        scratch_shapes=[
            pltpu.VMEM((seqs, full, width), BF16),
            pltpu.VMEM((count, heads_dev * 4 * HD, width), BF16),
            pltpu.VMEM((width, width), BF16),
            pltpu.VMEM((count, 16, heads_dev * HD), BF16),
            pltpu.VMEM((16, width), F32),
            pltpu.VMEM((pairs, PAIR, rows), F32),
            pltpu.VMEM((pairs, 8, rows), F32),
            pltpu.VMEM((rows, width), BF16),
            pltpu.VMEM((2 * hidden + width, width), F32),
            pltpu.VMEM((8, width), F32),
            pltpu.SemaphoreType.DMA((seqs, 2 * (count - 1))),
            pltpu.SemaphoreType.DMA((seqs, count)),
            pltpu.SemaphoreType.DMA((seqs,)),
            pltpu.SemaphoreType.DMA((2 * (count - 1),)),
            pltpu.SemaphoreType.DMA((count,)),
            pltpu.SemaphoreType.DMA((4, count - 1)),
            pltpu.SemaphoreType.DMA((4, count - 1)),
            pltpu.SemaphoreType.DMA((count - 1,)),
            pltpu.SemaphoreType.DMA((count - 1,)),
        ],
        cost_estimate=pl.CostEstimate(flops=120 * 10 ** 9, bytes_accessed=60 << 20,
                                      transcendentals=seqs * pairs * 2 * full * rows),
        compiler_params=pltpu.CompilerParams(
            collective_id=0, has_side_effects=True, vmem_limit_bytes=VMEM_LIMIT),
        name="forward_layer",
    )(lengths, pair_ids, tok, embed, cot, qkv_w, q_bias, v_bias, out_w, b_out, w_in, b_in, w_last, b_last)


def row_step(size):
    for step in (256, 160, 128, 80, 64, 32, 16):
        if size % step == 0:
            return step
    return size


def aligned(start, size, unit=16):
    return pl.ds(pl.multiple_of(start, unit), size)


class Reducer:
    def __init__(self, data, land, group, rows, bits, where_at, send_sem, recv_sem, free_sem=None):
        self.data, self.land, self.group = data, land, group
        self.send_sem, self.recv_sem, self.free_sem = send_sem, recv_sem, free_sem
        self.stages, self.landed = [], 0
        start, size = 0, rows
        for axis, bit in bits:
            index = where_at[axis]
            digit = (index // bit) % 2
            halves = (size // 2) % 16 == 0
            if halves:
                size //= 2
                keep, other = start + digit * size, start + (1 - digit) * size
            else:
                keep = other = start
            self.stages.append((axis, flip(index, bit), halves, keep, other, size, self.landed))
            self.landed += size
            start = keep
        self.start, self.size = start, size

    def copy(self, j):
        axis, partner, _, _, other, size, landed = self.stages[j]
        return pltpu.make_async_remote_copy(
            src_ref=self.data.at[self.group, :, aligned(other, size)],
            dst_ref=self.land.at[self.group, :, pl.ds(landed, size)],
            send_sem=self.send_sem.at[self.group, j],
            recv_sem=self.recv_sem.at[self.group, j],
            device_id={axis: partner}, device_id_type=MESH)

    def finish(self, j):
        self.copy(j).wait()
        axis, partner, halves, keep, _, size, landed = self.stages[j]
        if self.free_sem is not None and halves:
            pl.semaphore_signal(self.free_sem.at[self.group, j], 1, device_id={axis: partner},
                                device_id_type=MESH)
        step = row_step(size)
        slots = self.data.shape[1]
        for slot in range(slots):
            def add(r, _):
                at = aligned(keep + r * step, step)
                more = self.land[self.group, slot, aligned(landed + r * step, step), :]
                self.data[self.group, slot, at, :] = self.data[self.group, slot, at, :] + more
                return 0

            lax.fori_loop(0, size // step, add, 0)

    def back(self, j):
        axis, partner, _, keep, _, size, _ = self.stages[j]
        view = self.data.at[self.group, :, aligned(keep, size)]
        at = len(self.stages) + j
        return pltpu.make_async_remote_copy(
            src_ref=view, dst_ref=view, send_sem=self.send_sem.at[self.group, at],
            recv_sem=self.recv_sem.at[self.group, at],
            device_id={axis: partner}, device_id_type=MESH)

    def back_start(self, j):
        pl.semaphore_wait(self.free_sem.at[self.group, j], 1)
        self.back(j).start()

    def events(self, line=None):
        doubling = [j for j in range(len(self.stages)) if self.stages[j][2]][::-1]
        middle = line.events(self.start, self.size) if line else []
        run = [lambda: self.copy(0).start()]
        for j in range(len(self.stages)):
            def after(j=j):
                self.finish(j)
                if j + 1 < len(self.stages):
                    self.copy(j + 1).start()
                elif middle:
                    middle[0]()
                else:
                    self.back_start(doubling[0])
            run.append(after)
        for i in range(1, len(middle)):
            def after_line(i=i):
                middle[i]()
                if i + 1 == len(middle):
                    self.back_start(doubling[0])
            run.append(after_line)
        for i, j in enumerate(doubling):
            def after_back(i=i, j=j):
                self.back(j).wait()
                if i + 1 < len(doubling):
                    self.back_start(doubling[i + 1])
            run.append(after_back)
        return run


class Line:
    def __init__(self, data, land, group, landed, place, send_sem, recv_sem):
        self.data, self.land, self.group, self.landed = data, land, group, landed
        self.place, self.send_sem, self.recv_sem = place, send_sem, recv_sem
        self.end = (place == 0) | (place == 3)
        self.inner = (place == 1) | (place == 2)

    def copy(self, step, target, start, size):
        return pltpu.make_async_remote_copy(
            src_ref=self.data.at[self.group, :, aligned(start, size)],
            dst_ref=self.land.at[self.group, :, pl.ds(self.landed + step * size, size)],
            send_sem=self.send_sem.at[self.group, step], recv_sem=self.recv_sem.at[self.group, step],
            device_id={"mp": target}, device_id_type=MESH)

    def events(self, start, size):
        inward = jnp.where(self.place < 2, 1, 2)
        across = jnp.where(self.place < 2, 2, 1)
        outward = jnp.where(self.place < 2, 0, 3)
        first = self.copy(0, inward, start, size)
        second = self.copy(1, across, start, size)
        third = self.copy(2, outward, start, size)
        unit = row_step(size)

        def take(step, add):
            def move(r, _):
                at = aligned(start + r * unit, unit)
                more = self.land[self.group, 0, aligned(self.landed + step * size + r * unit, unit), :]
                if add:
                    more = self.data[self.group, 0, at, :] + more
                self.data[self.group, 0, at, :] = more
                return 0

            lax.fori_loop(0, size // unit, move, 0)

        def begin():
            pl.when(self.end)(first.start)

        def swap():
            @pl.when(self.inner)
            def _():
                first.wait_recv()
                take(0, True)
                second.start()

        def hand_back():
            @pl.when(self.inner)
            def _():
                second.wait()
                take(1, True)
                third.start()

        def close():
            @pl.when(self.inner)
            def _():
                third.wait_send()

            @pl.when(self.end)
            def _():
                first.wait_send()
                third.wait_recv()
                take(2, False)

        return [begin, swap, hand_back, close]


def bit_list(size):
    return [1 << b for b in range(size.bit_length() - 1)]


def far_first(count):
    table = []
    for m in range(count):
        order = []
        for k in range(count - 1, 0, -1):
            order += [c for c in (m + k, m - k) if 0 <= c < count]
        table.append(order + [m])
    return table


def backward_layer(count, data_count, heads_dev, tail_points,
                   lengths, pair_ids, x_seq, weight, q_in, k_in, v_in, att_t, lse, grad_in, mixed_grad, g_in,
                   token_grad, g_out, own_out,
                   a_buf, a_land, b_buf, b_land, b_parts, own_buf, parts, land, x_acc, dq_acc, delta_all,
                   w_acc, bias_acc, col_acc, table_acc,
                   load_sem, a_send, a_recv, a_free, l_send, l_recv, b_send, b_recv, s_send, s_recv, r_send, r_recv):
    seq, turn = pl.program_id(0), pl.program_id(1)
    seqs, pairs = token_grad.shape[0], weight.shape[0]
    rows, width = token_grad.shape[1], token_grad.shape[2]
    place, data_at = lax.axis_index("mp"), lax.axis_index("dp")
    where_at = {"mp": place, "dp": data_at}
    point = seq * count + turn
    data_bits, place_bits = bit_list(data_count), bit_list(count)
    swapped = [{2: 4, 4: 2}.get(b, b) for b in data_bits]

    order = far_first(count)
    chunk = sum(jnp.where((place == m) & (turn == i), order[m][i], 0)
                for m in range(count) for i in range(count))

    in_line = count == 4
    a_sums = [
        Reducer(a_buf, a_land, g, a_buf.shape[2],
                [("dp", b) for b in (data_bits, swapped)[g]] + [("mp", b) for b in place_bits if not in_line],
                where_at, a_send, a_recv, a_free)
        for g in range(2)]
    a_events = [
        a.events(Line(a_buf, a_land, g, a.landed, place, l_send, l_recv) if in_line else None)
        for g, a in enumerate(a_sums)]
    b_sums = [
        Reducer(b_buf, b_land, g, b_buf.shape[2], [("dp", b) for b in (data_bits, swapped)[g]],
                where_at, b_send, b_recv)
        for g in range(2)]

    def send_part(s, c, downward):
        slot = jnp.where((place - 1 == c) & (downward == 1), count, c)
        return pltpu.make_async_remote_copy(
            src_ref=parts.at[s, c], dst_ref=land.at[s, slot],
            send_sem=s_send.at[s, c], recv_sem=s_recv.at[s, slot],
            device_id={"mp": place - 1 if downward else place + 1}, device_id_type=MESH)

    def await_part(s, slot):
        pltpu.make_async_remote_copy(
            src_ref=land.at[s, slot], dst_ref=land.at[s, slot],
            send_sem=s_send.at[s, 0], recv_sem=s_recv.at[s, slot],
            device_id={"mp": (place + 1) % count}, device_id_type=MESH).wait_recv()

    def combine(s, k):
        for downward in (0, 1):
            c = place - k if downward else place + k
            go = ((c >= 0) & (place + 1 < count)) if downward else ((c < count) & (place >= 1))

            @pl.when(go)
            def _():
                await_part(s, c)
                parts[s, c] = parts[s, c] + land[s, c]
                send_part(s, c, downward).start()

    def conclude(s):
        for downward in (0, 1):
            slot = count if downward else place

            @pl.when((place + 1 < count) if downward else (place >= 1))
            def _():
                await_part(s, slot)
                token_grad[s] += land[s, slot].astype(F32)

    def load():
        return pltpu.make_async_copy(g_in, a_buf, load_sem.at[0])

    def store():
        return pltpu.make_async_copy(a_buf, g_out, load_sem.at[1])

    partners = [flip(data_at, b) for b in data_bits]

    @pl.when(point == 0)
    def _():
        greet(place, count, partners)
        load().start()
        w_acc[...] = jnp.zeros_like(w_acc)
        bias_acc[...] = jnp.zeros_like(bias_acc)
        table_acc[...] = jnp.zeros_like(table_acc)
        await_greetings(count, partners)
        load().wait()
        for events in a_events:
            events[0]()

    @pl.when(turn == 0)
    def _():
        col_acc[...] = jnp.zeros_like(col_acc)
        dq_acc[...] = jnp.zeros_like(dq_acc)
        for p in range(pairs):
            prod = grad_in[0, :, p * PAIR:(p + 1) * PAIR].astype(F32).T * att_t[0, p]
            delta_all[p, 0:1, :] = jnp.sum(prod[:HD], axis=0, keepdims=True)
            delta_all[p, 1:2, :] = jnp.sum(prod[HD:], axis=0, keepdims=True)

    length = lengths[seq]
    at = aligned(chunk * rows, rows, rows)
    own = aligned(place * rows, rows, rows)
    x_acc[...] = jnp.zeros_like(x_acc)

    def pair_step(p, _):
        lanes = aligned(p * PAIR, PAIR, PAIR)
        q_pair = q_in[0, p]
        grad_pair = grad_in[0, :, lanes]
        k_blk = k_in[0, p, at, :]
        v_blk = v_in[0, p, at, :]
        keep = (lax.broadcasted_iota(jnp.int32, (rows, rows), 0) + chunk * rows) < length
        dk = jnp.zeros((rows, PAIR), F32)
        dv = jnp.zeros((rows, PAIR), F32)
        for h in range(2):
            q_head, g_head = one_head(q_pair, h), one_head(grad_pair, h)
            s = jnp.where(keep, nt(k_blk, q_head) * LOG2E, NEGATIVE)
            pr = jnp.exp2(s - lse[0, p, h:h + 1, :])
            dp = nt(v_blk, g_head)
            ds = (pr * (dp - delta_all[p, h:h + 1, :])).astype(BF16)
            dv += nn(pr.astype(BF16), g_head)
            dk += nn(ds, q_head)
            dq_acc[p, h] += tn(k_blk, ds)
        dv = dv.astype(BF16)
        both = jnp.concatenate([dk.astype(BF16), dv], axis=1)
        x_acc[...] += nn(both, weight[p, PAIR:, :])
        w_acc[p, PAIR:, :] += tn(both, x_seq[0, at, :])
        bias_acc[1:2, lanes] += jnp.sum(dv.astype(F32), axis=0, keepdims=True)
        return 0

    lax.fori_loop(0, pairs, pair_step, 0, unroll=4)

    @pl.when(turn < count - 1)
    def _():
        parts[seq, chunk] = x_acc[...].astype(BF16)
        for downward in (0, 1):
            @pl.when((place == (count - 1 if downward else 0)) & (chunk != place))
            def _():
                send_part(seq, chunk, downward).start()

    @pl.when(turn == count - 1)
    def _():
        def query_step(p, _):
            lanes = aligned(p * PAIR, PAIR, PAIR)
            dq_t = jnp.concatenate(
                [dq_acc[p, h, h * HD:(h + 1) * HD, :] for h in range(2)], axis=0) * (HD ** -0.5)
            dq = dq_t.T.astype(BF16)
            x_acc[...] += nn(dq, weight[p, :PAIR, :])
            w_acc[p, :PAIR, :] += tn(dq, x_seq[0, own, :])
            bias_acc[0:1, lanes] += jnp.sum(dq.astype(F32), axis=0, keepdims=True)
            return 0

        lax.fori_loop(0, pairs, query_step, 0)
        x_acc[...] += mixed_grad[0].astype(F32)
        token_grad[seq] = x_acc[...]

    col_acc[0:1, :] += jnp.sum(x_acc[...], axis=0, keepdims=True)

    @pl.when(turn == count - 1)
    def _():
        line = lax.broadcasted_iota(jnp.int32, table_acc.shape, 0)
        table_acc[...] += jnp.where(line == pair_ids[seq], col_acc[0:1, :], 0.0)

    slots = {2: 2, 1: 4} if count == 4 else {k: count + (count - 2 - k) for k in range(1, count - 1)}
    for k in range(count - 2, 0, -1):
        turns, seq_back = slots[k] % count, slots[k] // count

        @pl.when((turn == turns) & (seq >= seq_back))
        def _():
            combine(seq - seq_back, k)

    @pl.when((turn == count - 1) & (seq >= 1))
    def _():
        conclude(seq - 1)

    total = seqs * count
    later = len(a_events[0]) - 1
    in_tail = []
    for e in range(1, later + 1):
        when_at = tail_points[e - 1] if tail_points else (e * total) // (later + 1)
        if when_at >= total:
            in_tail.append(e)
            continue

        @pl.when(point == when_at)
        def _():
            for events in a_events:
                events[e]()

    @pl.when(point == total - 1)
    def _():
        last = seqs - 1
        base = heads_dev * 3 * HD
        half = count // 2
        for m in range(count):
            g, slot = m // half, m % half
            if heads_dev == 2:
                b_buf[g, slot, 0:base, :] = w_acc[m].astype(BF16)
            else:
                for j in range(3):
                    lo = j * PAIR + (m % 2) * HD
                    b_buf[g, slot, j * HD:(j + 1) * HD, :] = w_acc[m // 2, lo:lo + HD, :].astype(BF16)
            b_buf[g, slot, base:base + 16, :] = bias_acc[...].astype(BF16)
            b_buf[g, slot, base + 16:base + 32, :] = table_acc[...].astype(BF16)
            rest = b_buf.shape[2] - base - 32
            b_buf[g, slot, base + 32:, :] = jnp.zeros((rest, width), BF16)
        stages = len(b_sums[0].stages)
        for b in b_sums:
            b.copy(0).start()
        tail_k = [k for k in range(count - 2, 0, -1) if slots[k] >= count]
        for j in range(stages):
            for b in b_sums:
                b.finish(j)
                if j + 1 < stages:
                    b.copy(j + 1).start()
            if tail_k:
                combine(last, tail_k.pop(0))
        strip = b_sums[0].size
        mine = place // half
        start = jnp.where(mine == 0, b_sums[0].start, b_sums[1].start)

        def scatter(k):
            target = (place + k) % count
            g = target // half
            begin = jnp.where(g == 0, b_sums[0].start, b_sums[1].start)
            return pltpu.make_async_remote_copy(
                src_ref=b_buf.at[g, target % half, aligned(begin, strip)],
                dst_ref=b_parts.at[k - 1],
                send_sem=r_send.at[k - 1], recv_sem=r_recv.at[k - 1],
                device_id={"mp": target}, device_id_type=MESH)

        for k in range(1, count):
            scatter(k).start()
        for k in tail_k:
            combine(last, k)
        for e in in_tail:
            for events in a_events:
                events[e]()
        store().start()
        for k in range(1, count):
            scatter(k).wait()
        home = b_buf[mine, place % half, aligned(start, strip), :].astype(F32)
        for k in range(1, count):
            home += b_parts[k - 1].astype(F32)
        own_buf[aligned(start, strip), :] = home.astype(BF16)

        def back(j):
            partner = jnp.where(mine == 0, b_sums[0].stages[j][1], b_sums[1].stages[j][1])
            keep = jnp.where(mine == 0, b_sums[0].stages[j][3], b_sums[1].stages[j][3])
            size = b_sums[0].stages[j][5]
            view = own_buf.at[aligned(keep, size)]
            return pltpu.make_async_remote_copy(
                src_ref=view, dst_ref=view, send_sem=r_send.at[count - 1 + j],
                recv_sem=r_recv.at[count - 1 + j], device_id={"dp": partner}, device_id_type=MESH)

        for j in reversed(range(stages)):
            back(j).start()
            back(j).wait()
        own_out[...] = own_buf[...]
        conclude(last)
        store().wait()
        for s in range(seqs):
            for k in range(1, count):
                for downward in (0, 1):
                    c = place - k if downward else place + k

                    @pl.when((c >= 0) if downward else (c < count))
                    def _():
                        send_part(s, c, downward).wait_send()


def call_backward(count, data_count, heads_dev, lengths, pair_ids, x_all, weight, q, k, v, att_t, lse,
                  grad, mixed_grad, g_all):
    seqs, full, width = x_all.shape
    rows = full // count
    pairs = weight.shape[0]
    a_rows = g_all.shape[0] // 2
    base = heads_dev * 3 * HD
    slot_rows = -(-(base + 32) // 128) * 128
    data_bits, place_bits = bit_list(data_count), bit_list(count)

    def landing(size, bits):
        landed = 0
        for _ in range(bits):
            size = size // 2 if (size // 2) % 16 == 0 else size
            landed += size
        return landed, size

    if count == 4:
        a_landed, strip = landing(a_rows, len(data_bits))
        a_landed += 3 * strip
    else:
        a_landed, _ = landing(a_rows, len(data_bits) + len(place_bits))
    b_landed, strip = landing(slot_rows, len(data_bits))
    a_stages, b_stages = len(data_bits) + len(place_bits), len(data_bits)
    tail_points = TAIL_POINTS if (count, data_count) == (4, 8) else None
    in_smem = pl.BlockSpec(memory_space=pltpu.SMEM)
    in_hbm = pl.BlockSpec(memory_space=pl.ANY)
    seq_block = lambda shape, mode=None: pl.BlockSpec(
        (1,) + shape[1:], lambda s, i: (s,) + (0,) * (len(shape) - 1), pipeline_mode=mode)
    shape = jax.ShapeDtypeStruct
    dma = pltpu.SemaphoreType.DMA
    return pl.pallas_call(
        functools.partial(backward_layer, count, data_count, heads_dev, tail_points),
        grid=(seqs, count),
        in_specs=[in_smem, in_smem, seq_block(x_all.shape, CONSTANT), fixed(weight.shape),
                  seq_block(q.shape, CONSTANT), seq_block(k.shape, CONSTANT),
                  seq_block(v.shape, CONSTANT), seq_block(att_t.shape, CONSTANT),
                  seq_block(lse.shape), seq_block(grad.shape), seq_block(mixed_grad.shape), in_hbm],
        out_specs=[fixed((seqs, rows, width)), in_hbm, fixed((slot_rows, width))],
        out_shape=[
            shape((seqs, rows, width), F32),
            shape((2, 1, a_rows, width), BF16),
            shape((slot_rows, width), BF16),
        ],
        scratch_shapes=[
            pltpu.VMEM((2, 1, a_rows, width), BF16),
            pltpu.VMEM((2, 1, a_landed, width), BF16),
            pltpu.VMEM((2, count // 2, slot_rows, width), BF16),
            pltpu.VMEM((2, count // 2, b_landed, width), BF16),
            pltpu.VMEM((count - 1, strip, width), BF16),
            pltpu.VMEM((slot_rows, width), BF16),
            pltpu.VMEM((seqs, count, rows, width), BF16),
            pltpu.VMEM((seqs, count + 1, rows, width), BF16),
            pltpu.VMEM((rows, width), F32),
            pltpu.VMEM((pairs, 2, PAIR, rows), F32),
            pltpu.VMEM((pairs, 8, rows), F32),
            pltpu.VMEM((pairs, 3 * PAIR, width), F32),
            pltpu.VMEM((16, width), F32),
            pltpu.VMEM((8, width), F32),
            pltpu.VMEM((16, width), F32),
            dma((2,)), dma((2, 2 * a_stages)), dma((2, 2 * a_stages)),
            pltpu.SemaphoreType.REGULAR((2, a_stages)), dma((2, 3)), dma((2, 3)),
            dma((2, b_stages)), dma((2, b_stages)),
            dma((seqs, count)), dma((seqs, count + 1)),
            dma((count - 1 + b_stages,)), dma((count - 1 + b_stages,)),
        ],
        cost_estimate=pl.CostEstimate(flops=200 * 10 ** 9, bytes_accessed=60 << 20,
                                      transcendentals=seqs * pairs * 2 * full * rows),
        compiler_params=pltpu.CompilerParams(
            collective_id=1, has_side_effects=True, vmem_limit_bytes=VMEM_LIMIT),
        name="backward_layer",
    )(lengths, pair_ids, x_all, weight, q, k, v, att_t, lse, grad, mixed_grad,
      g_all.reshape(2, 1, a_rows, width))


def finish(place_ref, sums, own, token_in, result_in, last_grad, in_grad, small_sums, out_grad,
           qkv_grad, q_bias_grad, v_bias_grad, table, token_out, result_out, *, heads_dev, hidden):
    part = pl.program_id(0)
    width = own.shape[1]
    place = place_ref[0]
    last_grad[...] = sums[pl.ds(pl.multiple_of(part * width, width), width), :].astype(F32)
    in_grad[...] = sums[pl.ds(pl.multiple_of(hidden + part * width, width), width), :].astype(F32)
    token_out[...] = token_in[...]
    result_out[...] = result_in[...]

    @pl.when(part == 0)
    def _():
        base = heads_dev * 3 * HD
        out_rows = out_grad.shape[0]
        out_grad[...] = sums[
            pl.ds(pl.multiple_of(2 * hidden + place * out_rows, out_rows), out_rows), :].astype(F32)
        small_sums[...] = sums[2 * hidden + width:2 * hidden + width + 16, :].astype(F32)[:8]
        turned = own[:base, :].astype(F32).T
        parts = []
        for h in range(heads_dev):
            for j in range(3):
                lo = (j * heads_dev + h) * HD
                parts.append(turned[:, lo:lo + HD])
        qkv_grad[...] = jnp.concatenate(parts, axis=1)
        rows = own[base:base + 16, :].astype(F32)
        q_bias_grad[...] = rows[0:1]
        v_bias_grad[...] = rows[1:2]
        table[...] = own[base + 16:base + 32, :].astype(F32)[:table.shape[0]]


def call_finish(place, sums, own, token_grad, result, heads_dev, hidden, table_rows):
    seqs, rows, width = token_grad.shape
    parts = hidden // width
    base = heads_dev * 3 * HD
    out_rows = heads_dev * HD
    shape = jax.ShapeDtypeStruct
    strip = lambda: pl.BlockSpec((seqs, rows // parts, width), lambda i, *_: (0, i, 0))
    return pl.pallas_call(
        functools.partial(finish, heads_dev=heads_dev, hidden=hidden),
        grid_spec=pltpu.PrefetchScalarGridSpec(
            num_scalar_prefetch=1,
            grid=(parts,),
            in_specs=[fixed(sums.shape), fixed(own.shape), strip(), strip()],
            out_specs=[pl.BlockSpec((width, width), lambda i, *_: (i, 0)),
                       pl.BlockSpec((width, width), lambda i, *_: (0, i)),
                       fixed((8, width)), fixed((out_rows, width)), fixed((width, base)),
                       fixed((1, width)), fixed((1, width)), fixed((table_rows, width)),
                       strip(), strip()],
        ),
        out_shape=[shape((hidden, width), F32), shape((width, hidden), F32), shape((8, width), F32),
                   shape((out_rows, width), F32), shape((width, base), F32), shape((1, width), F32),
                   shape((1, width), F32), shape((table_rows, width), F32),
                   shape(token_grad.shape, F32), shape(result.shape, BF16)],
        compiler_params=pltpu.CompilerParams(vmem_limit_bytes=VMEM_LIMIT),
        name="finish",
    )(place, sums, own, token_grad, result)


def body(
    tokens,
    pair_ids,
    lengths,
    pair_embed,
    qkv_weight,
    q_bias,
    v_bias,
    out_weight,
    out_bias,
    ffn_in_weight,
    ffn_in_bias,
    ffn_out_weight,
    ffn_out_bias,
    cotangent,
):
    local_rows, seqs, width = tokens.shape
    table_rows = pair_embed.shape[0]
    count = lax.axis_size("mp")
    place = lax.axis_index("mp").astype(jnp.int32).reshape(1)
    tok = jnp.transpose(tokens, (1, 0, 2))
    cot = jnp.transpose(cotangent, (1, 0, 2))
    bias_len = q_bias.shape[0]
    (x_all, w_pairs, q, k, v, att_t, lse, result, mixed_grad, att_grad, g_all) = call_layer(
        count, lengths, pair_ids, tok, pair_embed, cot, qkv_weight, q_bias[None], v_bias[None],
        out_weight, out_bias[None], ffn_in_weight, ffn_in_bias[None], ffn_out_weight,
        ffn_out_bias[None])
    heads_dev = bias_len // HD
    tokens_grad, g_sum, own = call_backward(
        count, lax.axis_size("dp"), heads_dev, lengths, pair_ids, x_all, w_pairs, q, k, v, att_t, lse,
        att_grad, mixed_grad, g_all)

    hidden = ffn_in_weight.shape[1]
    (g_last_sum, g_in_sum, small, g_out_own, qkv_sum, qb_sum, vb_sum, table_sum, tokens_grad,
     result) = call_finish(
        place, g_sum.reshape(-1, width), own, tokens_grad, result, heads_dev, hidden, table_rows)
    at = hidden // width
    own_bias = lambda v: lax.dynamic_slice_in_dim(v[0], place[0] * bias_len, bias_len)
    return (
        jnp.transpose(result, (1, 0, 2)),
        jnp.transpose(tokens_grad, (1, 0, 2)),
        table_sum,
        qkv_sum,
        own_bias(qb_sum),
        own_bias(vb_sum),
        g_out_own,
        small[at + 1],
        g_in_sum,
        small[:at].reshape(-1),
        g_last_sum,
        small[at],
    )


def solution(mesh):
    return jax.shard_map(
        body,
        mesh=mesh,
        in_specs=(
            P("mp", "dp", None),
            P("dp"),
            P("dp"),
            P(),
            P(None, "mp"),
            P("mp"),
            P("mp"),
            P("mp", None),
            P(),
            P(),
            P(),
            P(),
            P(),
            P("mp", "dp", None),
        ),
        out_specs=(
            P("mp", "dp", None),
            P("mp", "dp", None),
            P(),
            P(None, "mp"),
            P("mp"),
            P("mp"),
            P("mp", None),
            P(),
            P(),
            P(),
            P(),
            P(),
        ),
        check_vma=False,
    )
```

```python
import functools
import math

import jax
import jax.numpy as jnp
from jax import lax
from jax.experimental import pallas as pl
from jax.experimental.pallas import tpu as pltpu
from jax.sharding import PartitionSpec as P

HD = 64
PAIR = 2 * HD
NEGATIVE = -1e30
LOG2E = math.log2(math.e)
F32 = jnp.float32
BF16 = jnp.bfloat16
VMEM_LIMIT = 60 * 1024 * 1024


def nn(a, b):
    return jnp.dot(a, b, preferred_element_type=F32)


def nt(a, b):
    return lax.dot_general(a, b, (((1,), (1,)), ((), ())), preferred_element_type=F32)


def tn(a, b):
    return lax.dot_general(a, b, (((0,), (0,)), ((), ())), preferred_element_type=F32)


def head_lanes(rows, head):
    lane = lax.broadcasted_iota(jnp.int32, (rows, PAIR), 1)
    return (lane >= head * HD) & (lane < (head + 1) * HD)


def one_head(pair_rows, head):
    return jnp.where(head_lanes(pair_rows.shape[0], head), pair_rows, jnp.zeros_like(pair_rows))


def fold8(values, op):
    rows, lanes = values.shape
    return op(values.reshape(rows // 8, 8, lanes), axis=0)


MESH = pl.DeviceIdType.MESH
CONSTANT = pl.Buffered(1)
PIECES = 8
UNROLL = 4
TAIL_POINTS = (0, 2, 3, 5, 7, 9, 10, 12, 12)


class Relay:
    def __init__(self, place, count, view, send_sem, recv_sem):
        self.place, self.count, self.view = place, count, view
        self.send_sem, self.recv_sem = send_sem, recv_sem

    def copy(self, chunk, downward, step):
        return pltpu.make_async_remote_copy(
            src_ref=self.view(chunk), dst_ref=self.view(chunk),
            send_sem=self.send_sem(downward, step), recv_sem=self.recv_sem(chunk),
            device_id={"mp": self.place - 1 if downward else self.place + 1},
            device_id_type=MESH)

    def each(self, step):
        for downward in (0, 1):
            chunk = self.place + step if downward else self.place - step
            exists = chunk < self.count if downward else chunk >= 0
            onward = self.place >= 1 if downward else self.place + 1 < self.count
            yield downward, chunk, exists, onward

    def advance(self, step):
        for downward, chunk, exists, onward in self.each(step):
            if step:
                @pl.when(exists)
                def _():
                    self.copy(chunk, downward, step).wait_recv()
            if step < self.count - 1:
                @pl.when(exists & onward)
                def _():
                    self.copy(chunk, downward, step).start()

    def drain(self):
        for step in range(self.count - 1):
            for downward, chunk, exists, onward in self.each(step):
                @pl.when(exists & onward)
                def _():
                    self.copy(chunk, downward, step).wait_send()


def greet(place, count, partners):
    barrier = pltpu.get_barrier_semaphore()
    for partner in partners:
        pl.semaphore_signal(barrier, 1, device_id={"dp": partner}, device_id_type=MESH)
    for k in range(1, count):
        pl.semaphore_signal(barrier, 1, device_id={"mp": (place + k) % count}, device_id_type=MESH)


def await_greetings(count, partners):
    pl.semaphore_wait(pltpu.get_barrier_semaphore(), len(partners) + count - 1)


def flip(index, bit):
    return index + bit - 2 * bit * ((index // bit) % 2)


def near_first(count):
    return [order[::-1] for order in far_first(count)]


def forward_layer(count, heads_dev,
                  lengths, pair_ids, tok, embed, cot, qkv_w, q_bias, v_bias, out_w, b_out,
                  w_in, b_in, w_last, b_last,
                  x_out, w_out, q_out, k_out, v_out, att_t_out, lse_out,
                  result, mixed_grad, att_grad, g_all,
                  x_all, w_all, w_o, bias_land, biases, acc, stats, att_rows_all, grads, grad_rows,
                  x_send, x_recv, x_copy, w_send, w_recv, plane_send, plane_recv, bias_send, bias_recv):
    seq, turn = pl.program_id(0), pl.program_id(1)
    seqs, pairs = tok.shape[0], w_out.shape[0]
    rows, width = tok.shape[1], tok.shape[2]
    hidden = w_in.shape[1]
    base = heads_dev * 4 * HD
    piece_rows = base // PIECES
    place, data_at = lax.axis_index("mp"), lax.axis_index("dp")
    order = near_first(count)
    chunk = sum(jnp.where((place == m) & (turn == i), order[m][i], 0)
                for m in range(count) for i in range(count))

    def x_relay(s):
        return Relay(
            place, count,
            lambda c: x_all.at[s, pl.ds(pl.multiple_of(c * rows, rows), rows)],
            lambda downward, step: x_send.at[s, downward * (count - 1) + step],
            lambda c: x_recv.at[s, c])

    core, near_x, near_y = [(data_at // bit) % 2 for bit in (1, 2, 4)]
    piece = near_x + 2 * near_y + 4 * core

    def w_span(start, size):
        return pl.ds(pl.multiple_of(start * piece_rows, piece_rows), size * piece_rows)

    w_relay = Relay(
        place, count, lambda c: w_all.at[c, w_span(piece, 1)],
        lambda downward, step: w_send.at[downward * (count - 1) + step],
        lambda c: w_recv.at[c])
    partners = [flip(data_at, 2), flip(data_at, 4), flip(flip(data_at, 2), 4), flip(data_at, 1)]

    def plane(stage):
        span = w_span(4 * core, 4) if stage == 3 else w_span(piece, 1)
        copies = []
        for k in range(1, count):
            source = (place + k) % count
            copies.append(pltpu.make_async_remote_copy(
                src_ref=w_all.at[source, span], dst_ref=w_all.at[source, span],
                send_sem=plane_send.at[stage, k - 1], recv_sem=plane_recv.at[stage, k - 1],
                device_id={"dp": partners[stage]}, device_id_type=MESH))
        return copies

    def bias_copies():
        copies = []
        for k in range(1, count):
            copies.append(pltpu.make_async_remote_copy(
                src_ref=bias_land.at[0], dst_ref=bias_land.at[k],
                send_sem=bias_send.at[k - 1], recv_sem=bias_recv.at[k - 1],
                device_id={"mp": (place + k) % count}, device_id_type=MESH))
        return copies

    @pl.when((seq == 0) & (turn == 0))
    def _():
        greet(place, count, partners)
        turned = qkv_w[...].T
        parts = []
        for j in range(3):
            for h in range(heads_dev):
                parts.append(turned[(h * 3 + j) * HD:(h * 3 + j + 1) * HD])
        w_all[place, 0:heads_dev * 3 * HD, :] = jnp.concatenate(parts, axis=0)
        w_all[place, heads_dev * 3 * HD:base, :] = out_w[...]
        line = lax.broadcasted_iota(jnp.int32, bias_land.shape[1:], 0)
        bias_land[0] = jnp.where(
            line == 0, q_bias[...].astype(F32),
            jnp.where(line == 1, v_bias[...].astype(F32), 0.0)).astype(BF16)
        await_greetings(count, partners)
        w_relay.advance(0)
        for copy in bias_copies():
            copy.start()
        own = pl.ds(pl.multiple_of(place * rows, rows), rows)
        for s in range(seqs):
            row = embed[pl.ds(pair_ids[s], 1), :]
            x_all[s, own, :] = (tok[s].astype(F32) + row).astype(BF16)
        if count > 2:
            w_relay.advance(1)
        x_relay(0).advance(0)
        for step in range(2 if count > 2 else 1, count):
            w_relay.advance(step)
        across = [plane(stage) for stage in range(3)]
        for copies in across:
            for copy in copies:
                copy.start()
        grads[...] = jnp.zeros_like(grads)
        grad_rows[...] = jnp.zeros_like(grad_rows)
        x_relay(0).advance(1)
        for copies in across:
            for copy in copies:
                copy.wait()
        for copy in plane(3):
            copy.start()
        for copy in bias_copies():
            copy.wait()
        for p in range(pairs):
            if heads_dev == 2:
                both = bias_land[(place + count - p) % count].astype(F32)
            else:
                both = jnp.concatenate(
                    [bias_land[(place + count - 2 * p - half) % count].astype(F32) for half in range(2)],
                    axis=1)
            biases[:, p * PAIR:(p + 1) * PAIR] = both
        for copy in plane(3):
            copy.wait()
        w_relay.drain()
        for p in range(pairs):
            if heads_dev == 2:
                w_out[p] = w_all[p, 0:3 * PAIR, :]
                w_o[p * PAIR:(p + 1) * PAIR, :] = w_all[p, 3 * PAIR:4 * PAIR, :]
            else:
                for half in range(2):
                    for j in range(4):
                        strip = w_all[2 * p + half, j * HD:(j + 1) * HD, :]
                        if j < 3:
                            w_out[p, j * PAIR + half * HD:j * PAIR + (half + 1) * HD, :] = strip
                        else:
                            w_o[p * PAIR + half * HD:p * PAIR + (half + 1) * HD, :] = strip

    def hbm_copy(s):
        return pltpu.make_async_copy(x_all.at[s], x_out.at[s], x_copy.at[s])

    for t in range(2, count - 1):
        @pl.when(turn == t - 1)
        def _():
            x_relay(seq).advance(t)
    if count > 2:
        @pl.when(turn == count - 1)
        def _():
            x_relay(seq).advance(count - 1)

    @pl.when((turn == max(count - 3, 0)) & (seq + 1 < seqs))
    def _():
        x_relay(seq + 1).advance(0)

    length = lengths[seq]
    own = pl.ds(pl.multiple_of(place * rows, rows), rows)
    at = pl.ds(pl.multiple_of(chunk * rows, rows), rows)

    @pl.when(turn == 0)
    def _():
        acc[...] = jnp.zeros_like(acc)
        line = lax.broadcasted_iota(jnp.int32, stats.shape, 1)
        stats[...] = jnp.where(line < 2, NEGATIVE, 0.0)

        def query_step(p, _):
            lanes = pl.ds(pl.multiple_of(p * PAIR, PAIR), PAIR)
            q_pair = (nt(x_all[seq, own, :], w_out[p, 0:PAIR, :]) + biases[0:1, lanes]).astype(BF16)
            q_out[0, p] = q_pair * BF16(HD ** -0.5)
            return 0

        lax.fori_loop(0, pairs, query_step, 0)

    for p in range(pairs):
        kv = nt(x_all[seq, at, :], w_out[p, PAIR:3 * PAIR, :])
        k_out[0, p, at, :] = kv[:, :PAIR].astype(BF16)
        v_out[0, p, at, :] = (kv[:, PAIR:] + biases[1:2, p * PAIR:(p + 1) * PAIR]).astype(BF16)

    def pair_step(p, _):
        k_blk, v_blk, q_pair = k_out[0, p, at, :], v_out[0, p, at, :], q_out[0, p]
        keep = (lax.broadcasted_iota(jnp.int32, (rows, rows), 0) + chunk * rows) < length
        scores = [jnp.where(keep, nt(k_blk, one_head(q_pair, h)), NEGATIVE) for h in range(2)]
        before = [stats[p, h:h + 1, :] for h in range(2)]
        tops = [jnp.maximum(before[h], jnp.max(scores[h], axis=0, keepdims=True) * LOG2E) for h in range(2)]
        probs = [jnp.exp2(scores[h] * LOG2E - tops[h]) for h in range(2)]
        added = tn(v_blk, jnp.concatenate([pr.astype(BF16) for pr in probs], axis=1))
        for h in range(2):
            half = slice(h * HD, (h + 1) * HD)
            shrink = jnp.exp2(before[h] - tops[h])
            stats[p, h:h + 1, :] = tops[h]
            stats[p, 2 + h:3 + h, :] = (
                stats[p, 2 + h:3 + h, :] * shrink + jnp.sum(probs[h], axis=0, keepdims=True))
            acc[p, half, :] = acc[p, half, :] * shrink + added[half, h * rows:(h + 1) * rows]
        return 0

    lax.fori_loop(0, pairs, pair_step, 0, unroll=UNROLL)

    @pl.when(turn == count - 1)
    def _():
        hbm_copy(seq).start()

        @pl.when(seq + 1 < seqs)
        def _():
            x_relay(seq + 1).advance(1)
        for p in range(pairs):
            total = stats[p, 2:4, :]
            inverse = 1.0 / total
            att_t = jnp.concatenate(
                [acc[p, h * HD:(h + 1) * HD, :] * inverse[h:h + 1] for h in range(2)], axis=0)
            att_t_out[0, p] = att_t
            att_rows_all[:, p * PAIR:(p + 1) * PAIR] = att_t.T.astype(BF16)
            lse_out[0, p] = jnp.concatenate(
                [stats[p, 0:2, :] + jnp.log2(total), jnp.zeros((6, rows), F32)], axis=0)

        cot_rows = cot[0]
        att_rows = att_rows_all[...]
        row = embed[pl.ds(pair_ids[seq], 1), :]
        mixed = (tok[seq].astype(F32) + row) + (nn(att_rows, w_o[...]) + b_out[...])
        mixed_low = mixed.astype(BF16)
        out_sum = mixed + b_last[...]
        back_sum = cot_rows.astype(F32)
        root = math.sqrt(2.0 / math.pi)
        for c in range(hidden // width):
            at = slice(c * width, (c + 1) * width)
            pre = nn(mixed_low, w_in[:, at]) + b_in[:, at]
            square = pre * pre
            th = jnp.tanh(root * pre * (1.0 + 0.044715 * square))
            half = 0.5 * (1.0 + th)
            act = (pre * half).astype(BF16)
            slope = half + (0.5 * root) * pre * (1.0 - th * th) * (1.0 + (3 * 0.044715) * square)
            out_sum += nn(act, w_last[at, :])
            back = (nt(cot_rows, w_last[at, :]) * slope).astype(BF16)
            grad_rows[c:c + 1, :] += jnp.sum(back.astype(F32), axis=0, keepdims=True)
            back_sum += nt(back, w_in[:, at])
            grads[at, :] += tn(act, cot_rows)
            grads[hidden + c * width:hidden + (c + 1) * width, :] += tn(mixed_low, back)
        result[0] = out_sum.astype(BF16)
        back_low = back_sum.astype(BF16)
        mixed_grad[0] = back_low
        at = hidden // width
        grad_rows[at:at + 1, :] += jnp.sum(cot_rows.astype(F32), axis=0, keepdims=True)
        grad_rows[at + 1:at + 2, :] += jnp.sum(back_low.astype(F32), axis=0, keepdims=True)
        grads[2 * hidden:, :] += tn(att_rows, back_low)
        att_grad[0] = nt(back_low, w_o[...]).astype(BF16)

    @pl.when((seq == seqs - 1) & (turn == count - 1))
    def _():
        def narrow(j, _):
            at = pl.ds(pl.multiple_of(j * width, width), width)
            g_all[at, :] = grads[at, :].astype(BF16)
            return 0

        lax.fori_loop(0, grads.shape[0] // width, narrow, 0)
        rest = g_all.shape[0] - grads.shape[0]
        g_all[grads.shape[0]:, :] = jnp.concatenate(
            [grad_rows[...], jnp.zeros((rest - 8, width), F32)], axis=0).astype(BF16)
        for s in range(seqs):
            x_relay(s).drain()
            hbm_copy(s).wait()


def fixed(shape):
    return pl.BlockSpec(shape, lambda *_: (0,) * len(shape), pipeline_mode=CONSTANT)


def call_layer(count, lengths, pair_ids, tok, embed, cot, qkv_w, q_bias, v_bias, out_w, b_out,
               w_in, b_in, w_last, b_last):
    seqs, rows, width = tok.shape
    hidden = w_in.shape[1]
    heads_dev = qkv_w.shape[1] // (3 * HD)
    full = count * rows
    pairs = width // PAIR
    g_rows = -(-(2 * hidden + width + 16) // 256) * 256
    in_smem = pl.BlockSpec(memory_space=pltpu.SMEM)
    per_seq = lambda: pl.BlockSpec((1, rows, width), lambda s, p: (s, 0, 0))
    per_pair = lambda *tail: pl.BlockSpec((1, pairs) + tail, lambda s, p: (s, 0, 0, 0))
    shape = jax.ShapeDtypeStruct
    return pl.pallas_call(
        functools.partial(forward_layer, count, heads_dev),
        grid=(seqs, count),
        in_specs=[in_smem, in_smem, fixed(tok.shape), fixed(embed.shape), per_seq(), fixed(qkv_w.shape),
                  fixed(q_bias.shape), fixed(v_bias.shape), fixed(out_w.shape), fixed(b_out.shape),
                  fixed(w_in.shape), fixed(b_in.shape), fixed(w_last.shape), fixed(b_last.shape)],
        out_specs=[pl.BlockSpec(memory_space=pl.ANY), fixed((pairs, 3 * PAIR, width)),
                   per_pair(rows, PAIR), per_pair(full, PAIR), per_pair(full, PAIR),
                   per_pair(PAIR, rows), per_pair(8, rows),
                   per_seq(), per_seq(), per_seq(), fixed((g_rows, width))],
        out_shape=[
            shape((seqs, full, width), BF16),
            shape((pairs, 3 * PAIR, width), BF16),
            shape((seqs, pairs, rows, PAIR), BF16),
            shape((seqs, pairs, full, PAIR), BF16),
            shape((seqs, pairs, full, PAIR), BF16),
            shape((seqs, pairs, PAIR, rows), F32),
            shape((seqs, pairs, 8, rows), F32),
            shape((seqs, rows, width), BF16),
            shape((seqs, rows, width), BF16),
            shape((seqs, rows, width), BF16),
            shape((g_rows, width), BF16),
        ],
        scratch_shapes=[
            pltpu.VMEM((seqs, full, width), BF16),
            pltpu.VMEM((count, heads_dev * 4 * HD, width), BF16),
            pltpu.VMEM((width, width), BF16),
            pltpu.VMEM((count, 16, heads_dev * HD), BF16),
            pltpu.VMEM((16, width), F32),
            pltpu.VMEM((pairs, PAIR, rows), F32),
            pltpu.VMEM((pairs, 8, rows), F32),
            pltpu.VMEM((rows, width), BF16),
            pltpu.VMEM((2 * hidden + width, width), F32),
            pltpu.VMEM((8, width), F32),
            pltpu.SemaphoreType.DMA((seqs, 2 * (count - 1))),
            pltpu.SemaphoreType.DMA((seqs, count)),
            pltpu.SemaphoreType.DMA((seqs,)),
            pltpu.SemaphoreType.DMA((2 * (count - 1),)),
            pltpu.SemaphoreType.DMA((count,)),
            pltpu.SemaphoreType.DMA((4, count - 1)),
            pltpu.SemaphoreType.DMA((4, count - 1)),
            pltpu.SemaphoreType.DMA((count - 1,)),
            pltpu.SemaphoreType.DMA((count - 1,)),
        ],
        cost_estimate=pl.CostEstimate(flops=120 * 10 ** 9, bytes_accessed=60 << 20,
                                      transcendentals=seqs * pairs * 2 * full * rows),
        compiler_params=pltpu.CompilerParams(
            collective_id=0, has_side_effects=True, vmem_limit_bytes=VMEM_LIMIT),
        name="forward_layer",
    )(lengths, pair_ids, tok, embed, cot, qkv_w, q_bias, v_bias, out_w, b_out, w_in, b_in, w_last, b_last)


def row_step(size):
    for step in (256, 160, 128, 80, 64, 32, 16):
        if size % step == 0:
            return step
    return size


def aligned(start, size, unit=16):
    return pl.ds(pl.multiple_of(start, unit), size)


class Reducer:
    def __init__(self, data, land, group, rows, bits, where_at, send_sem, recv_sem, free_sem=None):
        self.data, self.land, self.group = data, land, group
        self.send_sem, self.recv_sem, self.free_sem = send_sem, recv_sem, free_sem
        self.stages, self.landed = [], 0
        start, size = 0, rows
        for axis, bit in bits:
            index = where_at[axis]
            digit = (index // bit) % 2
            halves = (size // 2) % 16 == 0
            if halves:
                size //= 2
                keep, other = start + digit * size, start + (1 - digit) * size
            else:
                keep = other = start
            self.stages.append((axis, flip(index, bit), halves, keep, other, size, self.landed))
            self.landed += size
            start = keep
        self.start, self.size = start, size

    def copy(self, j):
        axis, partner, _, _, other, size, landed = self.stages[j]
        return pltpu.make_async_remote_copy(
            src_ref=self.data.at[self.group, :, aligned(other, size)],
            dst_ref=self.land.at[self.group, :, pl.ds(landed, size)],
            send_sem=self.send_sem.at[self.group, j],
            recv_sem=self.recv_sem.at[self.group, j],
            device_id={axis: partner}, device_id_type=MESH)

    def finish(self, j):
        self.copy(j).wait()
        axis, partner, halves, keep, _, size, landed = self.stages[j]
        if self.free_sem is not None and halves:
            pl.semaphore_signal(self.free_sem.at[self.group, j], 1, device_id={axis: partner},
                                device_id_type=MESH)
        step = row_step(size)
        slots = self.data.shape[1]
        for slot in range(slots):
            def add(r, _):
                at = aligned(keep + r * step, step)
                more = self.land[self.group, slot, aligned(landed + r * step, step), :]
                self.data[self.group, slot, at, :] = self.data[self.group, slot, at, :] + more
                return 0

            lax.fori_loop(0, size // step, add, 0)

    def back(self, j):
        axis, partner, _, keep, _, size, _ = self.stages[j]
        view = self.data.at[self.group, :, aligned(keep, size)]
        at = len(self.stages) + j
        return pltpu.make_async_remote_copy(
            src_ref=view, dst_ref=view, send_sem=self.send_sem.at[self.group, at],
            recv_sem=self.recv_sem.at[self.group, at],
            device_id={axis: partner}, device_id_type=MESH)

    def back_start(self, j):
        pl.semaphore_wait(self.free_sem.at[self.group, j], 1)
        self.back(j).start()

    def events(self, line=None):
        doubling = [j for j in range(len(self.stages)) if self.stages[j][2]][::-1]
        middle = line.events(self.start, self.size) if line else []
        run = [lambda: self.copy(0).start()]
        for j in range(len(self.stages)):
            def after(j=j):
                self.finish(j)
                if j + 1 < len(self.stages):
                    self.copy(j + 1).start()
                elif middle:
                    middle[0]()
                else:
                    self.back_start(doubling[0])
            run.append(after)
        for i in range(1, len(middle)):
            def after_line(i=i):
                middle[i]()
                if i + 1 == len(middle):
                    self.back_start(doubling[0])
            run.append(after_line)
        for i, j in enumerate(doubling):
            def after_back(i=i, j=j):
                self.back(j).wait()
                if i + 1 < len(doubling):
                    self.back_start(doubling[i + 1])
            run.append(after_back)
        return run


class Line:
    def __init__(self, data, land, group, landed, place, send_sem, recv_sem):
        self.data, self.land, self.group, self.landed = data, land, group, landed
        self.place, self.send_sem, self.recv_sem = place, send_sem, recv_sem
        self.end = (place == 0) | (place == 3)
        self.inner = (place == 1) | (place == 2)

    def copy(self, step, target, start, size):
        return pltpu.make_async_remote_copy(
            src_ref=self.data.at[self.group, :, aligned(start, size)],
            dst_ref=self.land.at[self.group, :, pl.ds(self.landed + step * size, size)],
            send_sem=self.send_sem.at[self.group, step], recv_sem=self.recv_sem.at[self.group, step],
            device_id={"mp": target}, device_id_type=MESH)

    def events(self, start, size):
        inward = jnp.where(self.place < 2, 1, 2)
        across = jnp.where(self.place < 2, 2, 1)
        outward = jnp.where(self.place < 2, 0, 3)
        first = self.copy(0, inward, start, size)
        second = self.copy(1, across, start, size)
        third = self.copy(2, outward, start, size)
        unit = row_step(size)

        def take(step, add):
            def move(r, _):
                at = aligned(start + r * unit, unit)
                more = self.land[self.group, 0, aligned(self.landed + step * size + r * unit, unit), :]
                if add:
                    more = self.data[self.group, 0, at, :] + more
                self.data[self.group, 0, at, :] = more
                return 0

            lax.fori_loop(0, size // unit, move, 0)

        def begin():
            pl.when(self.end)(first.start)

        def swap():
            @pl.when(self.inner)
            def _():
                first.wait_recv()
                take(0, True)
                second.start()

        def hand_back():
            @pl.when(self.inner)
            def _():
                second.wait()
                take(1, True)
                third.start()

        def close():
            @pl.when(self.inner)
            def _():
                third.wait_send()

            @pl.when(self.end)
            def _():
                first.wait_send()
                third.wait_recv()
                take(2, False)

        return [begin, swap, hand_back, close]


def bit_list(size):
    return [1 << b for b in range(size.bit_length() - 1)]


def far_first(count):
    table = []
    for m in range(count):
        order = []
        for k in range(count - 1, 0, -1):
            order += [c for c in (m + k, m - k) if 0 <= c < count]
        table.append(order + [m])
    return table


def backward_layer(count, data_count, heads_dev, tail_points,
                   lengths, pair_ids, x_seq, weight, q_in, k_in, v_in, att_t, lse, grad_in, mixed_grad, g_in,
                   token_grad, g_out, own_out,
                   a_buf, a_land, b_buf, b_land, b_parts, own_buf, parts, land, both_all, x_acc, dq_acc, delta_all,
                   w_acc, bias_acc, col_acc, table_acc,
                   load_sem, a_send, a_recv, a_free, l_send, l_recv, b_send, b_recv, s_send, s_recv, r_send, r_recv):
    seq, turn = pl.program_id(0), pl.program_id(1)
    seqs, pairs = token_grad.shape[0], weight.shape[0]
    rows, width = token_grad.shape[1], token_grad.shape[2]
    place, data_at = lax.axis_index("mp"), lax.axis_index("dp")
    where_at = {"mp": place, "dp": data_at}
    point = seq * count + turn
    data_bits, place_bits = bit_list(data_count), bit_list(count)
    swapped = [{2: 4, 4: 2}.get(b, b) for b in data_bits]

    order = far_first(count)
    chunk = sum(jnp.where((place == m) & (turn == i), order[m][i], 0)
                for m in range(count) for i in range(count))

    in_line = count == 4
    a_sums = [
        Reducer(a_buf, a_land, g, a_buf.shape[2],
                [("dp", b) for b in (data_bits, swapped)[g]] + [("mp", b) for b in place_bits if not in_line],
                where_at, a_send, a_recv, a_free)
        for g in range(2)]
    a_events = [
        a.events(Line(a_buf, a_land, g, a.landed, place, l_send, l_recv) if in_line else None)
        for g, a in enumerate(a_sums)]
    b_sums = [
        Reducer(b_buf, b_land, g, b_buf.shape[2], [("dp", b) for b in (data_bits, swapped)[g]],
                where_at, b_send, b_recv)
        for g in range(2)]

    def send_part(s, c, downward):
        slot = jnp.where((place - 1 == c) & (downward == 1), count, c)
        return pltpu.make_async_remote_copy(
            src_ref=parts.at[s, c], dst_ref=land.at[s, slot],
            send_sem=s_send.at[s, c], recv_sem=s_recv.at[s, slot],
            device_id={"mp": place - 1 if downward else place + 1}, device_id_type=MESH)

    def await_part(s, slot):
        pltpu.make_async_remote_copy(
            src_ref=land.at[s, slot], dst_ref=land.at[s, slot],
            send_sem=s_send.at[s, 0], recv_sem=s_recv.at[s, slot],
            device_id={"mp": (place + 1) % count}, device_id_type=MESH).wait_recv()

    def combine(s, k):
        for downward in (0, 1):
            c = place - k if downward else place + k
            go = ((c >= 0) & (place + 1 < count)) if downward else ((c < count) & (place >= 1))

            @pl.when(go)
            def _():
                await_part(s, c)
                parts[s, c] = parts[s, c] + land[s, c]
                send_part(s, c, downward).start()

    def conclude(s):
        for downward in (0, 1):
            slot = count if downward else place

            @pl.when((place + 1 < count) if downward else (place >= 1))
            def _():
                await_part(s, slot)
                token_grad[s] += land[s, slot].astype(F32)

    def load():
        return pltpu.make_async_copy(g_in, a_buf, load_sem.at[0])

    def store():
        return pltpu.make_async_copy(a_buf, g_out, load_sem.at[1])

    partners = [flip(data_at, b) for b in data_bits]

    @pl.when(point == 0)
    def _():
        greet(place, count, partners)
        load().start()
        w_acc[...] = jnp.zeros_like(w_acc)
        bias_acc[...] = jnp.zeros_like(bias_acc)
        table_acc[...] = jnp.zeros_like(table_acc)
        await_greetings(count, partners)
        load().wait()
        for events in a_events:
            events[0]()

    @pl.when(turn == 0)
    def _():
        col_acc[...] = jnp.zeros_like(col_acc)
        dq_acc[...] = jnp.zeros_like(dq_acc)
        for p in range(pairs):
            prod = grad_in[0, :, p * PAIR:(p + 1) * PAIR].astype(F32).T * att_t[0, p]
            delta_all[p, 0:1, :] = jnp.sum(prod[:HD], axis=0, keepdims=True)
            delta_all[p, 1:2, :] = jnp.sum(prod[HD:], axis=0, keepdims=True)

    length = lengths[seq]
    at = aligned(chunk * rows, rows, rows)
    own = aligned(place * rows, rows, rows)
    def pair_step(p, _):
        lanes = aligned(p * PAIR, PAIR, PAIR)
        q_pair = q_in[0, p]
        grad_pair = grad_in[0, :, lanes]
        k_blk = k_in[0, p, at, :]
        v_blk = v_in[0, p, at, :]
        keep = (lax.broadcasted_iota(jnp.int32, (rows, rows), 0) + chunk * rows) < length
        dk = jnp.zeros((rows, PAIR), F32)
        dv = jnp.zeros((rows, PAIR), F32)
        for h in range(2):
            q_head, g_head = one_head(q_pair, h), one_head(grad_pair, h)
            s = jnp.where(keep, nt(k_blk, q_head) * LOG2E, NEGATIVE)
            pr = jnp.exp2(s - lse[0, p, h:h + 1, :])
            dp = nt(v_blk, g_head)
            ds = (pr * (dp - delta_all[p, h:h + 1, :])).astype(BF16)
            dv += nn(pr.astype(BF16), g_head)
            dk += nn(ds, q_head)
            dq_acc[p, h] += tn(k_blk, ds)
        dv = dv.astype(BF16)
        both = jnp.concatenate([dk.astype(BF16), dv], axis=1)
        both_all[p] = both
        bias_acc[1:2, lanes] += jnp.sum(dv.astype(F32), axis=0, keepdims=True)
        return 0

    lax.fori_loop(0, pairs, pair_step, 0, unroll=4)
    x_acc[...] = sum(nn(both_all[p], weight[p, PAIR:, :]) for p in range(pairs))
    for p in range(pairs):
        w_acc[p, PAIR:, :] += tn(both_all[p], x_seq[0, at, :])

    @pl.when(turn < count - 1)
    def _():
        parts[seq, chunk] = x_acc[...].astype(BF16)
        for downward in (0, 1):
            @pl.when((place == (count - 1 if downward else 0)) & (chunk != place))
            def _():
                send_part(seq, chunk, downward).start()

    @pl.when(turn == count - 1)
    def _():
        def query_step(p, _):
            lanes = aligned(p * PAIR, PAIR, PAIR)
            dq_t = jnp.concatenate(
                [dq_acc[p, h, h * HD:(h + 1) * HD, :] for h in range(2)], axis=0) * (HD ** -0.5)
            dq = dq_t.T.astype(BF16)
            x_acc[...] += nn(dq, weight[p, :PAIR, :])
            w_acc[p, :PAIR, :] += tn(dq, x_seq[0, own, :])
            bias_acc[0:1, lanes] += jnp.sum(dq.astype(F32), axis=0, keepdims=True)
            return 0

        lax.fori_loop(0, pairs, query_step, 0)
        x_acc[...] += mixed_grad[0].astype(F32)
        token_grad[seq] = x_acc[...]

    col_acc[0:1, :] += jnp.sum(x_acc[...], axis=0, keepdims=True)

    @pl.when(turn == count - 1)
    def _():
        line = lax.broadcasted_iota(jnp.int32, table_acc.shape, 0)
        table_acc[...] += jnp.where(line == pair_ids[seq], col_acc[0:1, :], 0.0)

    slots = {2: 2, 1: 4} if count == 4 else {k: count + (count - 2 - k) for k in range(1, count - 1)}
    for k in range(count - 2, 0, -1):
        turns, seq_back = slots[k] % count, slots[k] // count

        @pl.when((turn == turns) & (seq >= seq_back))
        def _():
            combine(seq - seq_back, k)

    @pl.when((turn == count - 1) & (seq >= 1))
    def _():
        conclude(seq - 1)

    total = seqs * count
    later = len(a_events[0]) - 1
    in_tail = []
    for e in range(1, later + 1):
        when_at = tail_points[e - 1] if tail_points else (e * total) // (later + 1)
        if when_at >= total:
            in_tail.append(e)
            continue

        @pl.when(point == when_at)
        def _():
            for events in a_events:
                events[e]()

    @pl.when(point == total - 1)
    def _():
        last = seqs - 1
        base = heads_dev * 3 * HD
        half = count // 2
        for m in range(count):
            g, slot = m // half, m % half
            if heads_dev == 2:
                b_buf[g, slot, 0:base, :] = w_acc[m].astype(BF16)
            else:
                for j in range(3):
                    lo = j * PAIR + (m % 2) * HD
                    b_buf[g, slot, j * HD:(j + 1) * HD, :] = w_acc[m // 2, lo:lo + HD, :].astype(BF16)
            b_buf[g, slot, base:base + 16, :] = bias_acc[...].astype(BF16)
            b_buf[g, slot, base + 16:base + 32, :] = table_acc[...].astype(BF16)
            rest = b_buf.shape[2] - base - 32
            b_buf[g, slot, base + 32:, :] = jnp.zeros((rest, width), BF16)
        stages = len(b_sums[0].stages)
        for b in b_sums:
            b.copy(0).start()
        tail_k = [k for k in range(count - 2, 0, -1) if slots[k] >= count]
        for j in range(stages):
            for b in b_sums:
                b.finish(j)
                if j + 1 < stages:
                    b.copy(j + 1).start()
            if tail_k:
                combine(last, tail_k.pop(0))
        strip = b_sums[0].size
        mine = place // half
        start = jnp.where(mine == 0, b_sums[0].start, b_sums[1].start)

        def scatter(k):
            target = (place + k) % count
            g = target // half
            begin = jnp.where(g == 0, b_sums[0].start, b_sums[1].start)
            return pltpu.make_async_remote_copy(
                src_ref=b_buf.at[g, target % half, aligned(begin, strip)],
                dst_ref=b_parts.at[k - 1],
                send_sem=r_send.at[k - 1], recv_sem=r_recv.at[k - 1],
                device_id={"mp": target}, device_id_type=MESH)

        for k in range(1, count):
            scatter(k).start()
        for k in tail_k:
            combine(last, k)
        for e in in_tail:
            for events in a_events:
                events[e]()
        store().start()
        for k in range(1, count):
            scatter(k).wait()
        home = b_buf[mine, place % half, aligned(start, strip), :].astype(F32)
        for k in range(1, count):
            home += b_parts[k - 1].astype(F32)
        own_buf[aligned(start, strip), :] = home.astype(BF16)

        def back(j):
            partner = jnp.where(mine == 0, b_sums[0].stages[j][1], b_sums[1].stages[j][1])
            keep = jnp.where(mine == 0, b_sums[0].stages[j][3], b_sums[1].stages[j][3])
            size = b_sums[0].stages[j][5]
            view = own_buf.at[aligned(keep, size)]
            return pltpu.make_async_remote_copy(
                src_ref=view, dst_ref=view, send_sem=r_send.at[count - 1 + j],
                recv_sem=r_recv.at[count - 1 + j], device_id={"dp": partner}, device_id_type=MESH)

        for j in reversed(range(stages)):
            back(j).start()
            back(j).wait()
        own_out[...] = own_buf[...]
        conclude(last)
        store().wait()
        for s in range(seqs):
            for k in range(1, count):
                for downward in (0, 1):
                    c = place - k if downward else place + k

                    @pl.when((c >= 0) if downward else (c < count))
                    def _():
                        send_part(s, c, downward).wait_send()


def call_backward(count, data_count, heads_dev, lengths, pair_ids, x_all, weight, q, k, v, att_t, lse,
                  grad, mixed_grad, g_all):
    seqs, full, width = x_all.shape
    rows = full // count
    pairs = weight.shape[0]
    a_rows = g_all.shape[0] // 2
    base = heads_dev * 3 * HD
    slot_rows = -(-(base + 32) // 128) * 128
    data_bits, place_bits = bit_list(data_count), bit_list(count)

    def landing(size, bits):
        landed = 0
        for _ in range(bits):
            size = size // 2 if (size // 2) % 16 == 0 else size
            landed += size
        return landed, size

    if count == 4:
        a_landed, strip = landing(a_rows, len(data_bits))
        a_landed += 3 * strip
    else:
        a_landed, _ = landing(a_rows, len(data_bits) + len(place_bits))
    b_landed, strip = landing(slot_rows, len(data_bits))
    a_stages, b_stages = len(data_bits) + len(place_bits), len(data_bits)
    tail_points = TAIL_POINTS if (count, data_count) == (4, 8) else None
    in_smem = pl.BlockSpec(memory_space=pltpu.SMEM)
    in_hbm = pl.BlockSpec(memory_space=pl.ANY)
    seq_block = lambda shape, mode=None: pl.BlockSpec(
        (1,) + shape[1:], lambda s, i: (s,) + (0,) * (len(shape) - 1), pipeline_mode=mode)
    shape = jax.ShapeDtypeStruct
    dma = pltpu.SemaphoreType.DMA
    return pl.pallas_call(
        functools.partial(backward_layer, count, data_count, heads_dev, tail_points),
        grid=(seqs, count),
        in_specs=[in_smem, in_smem, seq_block(x_all.shape, CONSTANT), fixed(weight.shape),
                  seq_block(q.shape, CONSTANT), seq_block(k.shape),
                  seq_block(v.shape), seq_block(att_t.shape, CONSTANT),
                  seq_block(lse.shape), seq_block(grad.shape), seq_block(mixed_grad.shape), in_hbm],
        out_specs=[fixed((seqs, rows, width)), in_hbm, fixed((slot_rows, width))],
        out_shape=[
            shape((seqs, rows, width), F32),
            shape((2, 1, a_rows, width), BF16),
            shape((slot_rows, width), BF16),
        ],
        scratch_shapes=[
            pltpu.VMEM((2, 1, a_rows, width), BF16),
            pltpu.VMEM((2, 1, a_landed, width), BF16),
            pltpu.VMEM((2, count // 2, slot_rows, width), BF16),
            pltpu.VMEM((2, count // 2, b_landed, width), BF16),
            pltpu.VMEM((count - 1, strip, width), BF16),
            pltpu.VMEM((slot_rows, width), BF16),
            pltpu.VMEM((seqs, count, rows, width), BF16),
            pltpu.VMEM((seqs, count + 1, rows, width), BF16),
            pltpu.VMEM((pairs, rows, 2 * PAIR), BF16),
            pltpu.VMEM((rows, width), F32),
            pltpu.VMEM((pairs, 2, PAIR, rows), F32),
            pltpu.VMEM((pairs, 8, rows), F32),
            pltpu.VMEM((pairs, 3 * PAIR, width), F32),
            pltpu.VMEM((16, width), F32),
            pltpu.VMEM((8, width), F32),
            pltpu.VMEM((16, width), F32),
            dma((2,)), dma((2, 2 * a_stages)), dma((2, 2 * a_stages)),
            pltpu.SemaphoreType.REGULAR((2, a_stages)), dma((2, 3)), dma((2, 3)),
            dma((2, b_stages)), dma((2, b_stages)),
            dma((seqs, count)), dma((seqs, count + 1)),
            dma((count - 1 + b_stages,)), dma((count - 1 + b_stages,)),
        ],
        cost_estimate=pl.CostEstimate(flops=200 * 10 ** 9, bytes_accessed=60 << 20,
                                      transcendentals=seqs * pairs * 2 * full * rows),
        compiler_params=pltpu.CompilerParams(
            collective_id=1, has_side_effects=True, vmem_limit_bytes=VMEM_LIMIT),
        name="backward_layer",
    )(lengths, pair_ids, x_all, weight, q, k, v, att_t, lse, grad, mixed_grad,
      g_all.reshape(2, 1, a_rows, width))


def finish(place_ref, last_rows, in_rows, out_strip, vector_rows, own, token_in, result_in,
           last_grad, in_grad, out_grad, out_bias, in_bias, last_bias,
           qkv_grad, q_bias_grad, v_bias_grad, table, token_out, result_out, *, heads_dev):
    width = own.shape[1]
    place = place_ref[0]
    last_grad[...] = last_rows[...].astype(F32)
    in_grad[...] = in_rows[...].astype(F32)
    token_out[...] = token_in[...]
    result_out[...] = result_in[...]

    @pl.when(pl.program_id(0) == pl.num_programs(0) - 1)
    def _():
        base = heads_dev * 3 * HD
        bias_len = heads_dev * HD
        out_grad[...] = out_strip[...].astype(F32)
        vectors = vector_rows[0:16, :].astype(F32)
        parts = in_bias.shape[1] // width
        for c in range(parts):
            in_bias[:, c * width:(c + 1) * width] = vectors[c:c + 1]
        last_bias[...] = vectors[parts:parts + 1]
        out_bias[...] = vectors[parts + 1:parts + 2]
        turned = own[:base, :].astype(F32).T
        parts = []
        for h in range(heads_dev):
            for j in range(3):
                lo = (j * heads_dev + h) * HD
                parts.append(turned[:, lo:lo + HD])
        qkv_grad[...] = jnp.concatenate(parts, axis=1)
        if heads_dev == 2:
            rows = own[base:base + 16, pl.ds(pl.multiple_of(place * PAIR, PAIR), PAIR)].astype(F32)
        else:
            rows = own[base:base + 16, pl.ds(pl.multiple_of((place // 2) * PAIR, PAIR), PAIR)].astype(F32)
            rows = jnp.where(place % 2 == 0, rows[:, :HD], rows[:, HD:])
        q_bias_grad[...] = rows[0:1, :bias_len]
        v_bias_grad[...] = rows[1:2, :bias_len]
        table[...] = own[base + 16:base + 32, :].astype(F32)[:table.shape[0]]


def call_finish(place, sums, own, token_grad, result, heads_dev, hidden, table_rows):
    seqs, rows, width = token_grad.shape
    cut = width
    tail = width // 2
    parts = hidden // cut
    base = heads_dev * 3 * HD
    out_rows = heads_dev * HD
    shape = jax.ShapeDtypeStruct
    strip = lambda: pl.BlockSpec((seqs, rows // parts, width), lambda i, *_: (0, i, 0))
    return pl.pallas_call(
        functools.partial(finish, heads_dev=heads_dev),
        grid_spec=pltpu.PrefetchScalarGridSpec(
            num_scalar_prefetch=1,
            grid=(parts,),
            in_specs=[pl.BlockSpec((cut, width), lambda i, *_: (i, 0)),
                      pl.BlockSpec((cut, width), lambda i, *_: (parts + i, 0)),
                      pl.BlockSpec((out_rows, width), lambda i, at: (2 * hidden // out_rows + at[0], 0)),
                      pl.BlockSpec((tail, width), lambda i, *_: ((2 * hidden + width) // tail, 0)),
                      fixed(own.shape), strip(), strip()],
            out_specs=[pl.BlockSpec((cut, width), lambda i, *_: (i, 0)),
                       pl.BlockSpec((cut, width), lambda i, *_: (0, i)),
                       fixed((out_rows, width)), fixed((1, width)), fixed((1, hidden)), fixed((1, width)),
                       fixed((width, base)), fixed((1, out_rows)), fixed((1, out_rows)),
                       fixed((table_rows, width)), strip(), strip()],
        ),
        out_shape=[shape((hidden, width), F32), shape((width, hidden), F32), shape((out_rows, width), F32),
                   shape((1, width), F32), shape((1, hidden), F32), shape((1, width), F32),
                   shape((width, base), F32), shape((1, out_rows), F32), shape((1, out_rows), F32),
                   shape((table_rows, width), F32), shape(token_grad.shape, F32), shape(result.shape, BF16)],
        compiler_params=pltpu.CompilerParams(vmem_limit_bytes=VMEM_LIMIT),
        name="finish",
    )(place, sums, sums, sums, sums, own, token_grad, result)


def body(
    tokens,
    pair_ids,
    lengths,
    pair_embed,
    qkv_weight,
    q_bias,
    v_bias,
    out_weight,
    out_bias,
    ffn_in_weight,
    ffn_in_bias,
    ffn_out_weight,
    ffn_out_bias,
    cotangent,
):
    local_rows, seqs, width = tokens.shape
    table_rows = pair_embed.shape[0]
    count = lax.axis_size("mp")
    place = lax.axis_index("mp").astype(jnp.int32).reshape(1)
    tok = jnp.transpose(tokens, (1, 0, 2))
    cot = jnp.transpose(cotangent, (1, 0, 2))
    bias_len = q_bias.shape[0]
    (x_all, w_pairs, q, k, v, att_t, lse, result, mixed_grad, att_grad, g_all) = call_layer(
        count, lengths, pair_ids, tok, pair_embed, cot, qkv_weight, q_bias[None], v_bias[None],
        out_weight, out_bias[None], ffn_in_weight, ffn_in_bias[None], ffn_out_weight,
        ffn_out_bias[None])
    heads_dev = bias_len // HD
    tokens_grad, g_sum, own = call_backward(
        count, lax.axis_size("dp"), heads_dev, lengths, pair_ids, x_all, w_pairs, q, k, v, att_t, lse,
        att_grad, mixed_grad, g_all)

    hidden = ffn_in_weight.shape[1]
    (g_last_sum, g_in_sum, g_out_own, out_bias_sum, in_bias_sum, last_bias_sum, qkv_sum, qb_sum, vb_sum,
     table_sum, tokens_grad, result) = call_finish(
        place, g_sum.reshape(-1, width), own, tokens_grad, result, heads_dev, hidden, table_rows)
    return (
        jnp.transpose(result, (1, 0, 2)),
        jnp.transpose(tokens_grad, (1, 0, 2)),
        table_sum,
        qkv_sum,
        qb_sum.reshape(-1),
        vb_sum.reshape(-1),
        g_out_own,
        out_bias_sum.reshape(-1),
        g_in_sum,
        in_bias_sum.reshape(-1),
        g_last_sum,
        last_bias_sum.reshape(-1),
    )


def solution(mesh):
    return jax.shard_map(
        body,
        mesh=mesh,
        in_specs=(
            P("mp", "dp", None),
            P("dp"),
            P("dp"),
            P(),
            P(None, "mp"),
            P("mp"),
            P("mp"),
            P("mp", None),
            P(),
            P(),
            P(),
            P(),
            P(),
            P("mp", "dp", None),
        ),
        out_specs=(
            P("mp", "dp", None),
            P("mp", "dp", None),
            P(),
            P(None, "mp"),
            P("mp"),
            P("mp"),
            P("mp", None),
            P(),
            P(),
            P(),
            P(),
            P(),
        ),
        check_vma=False,
    )
```

```python
import functools
import math

import jax
import jax.numpy as jnp
from jax import lax
from jax.experimental import pallas as pl
from jax.experimental.pallas import tpu as pltpu
from jax.sharding import PartitionSpec as P

HD = 64
PAIR = 2 * HD
NEGATIVE = -1e30
LOG2E = math.log2(math.e)
F32 = jnp.float32
BF16 = jnp.bfloat16
VMEM_LIMIT = 60 * 1024 * 1024


def nn(a, b):
    return jnp.dot(a, b, preferred_element_type=F32)


def nt(a, b):
    return lax.dot_general(a, b, (((1,), (1,)), ((), ())), preferred_element_type=F32)


def tn(a, b):
    return lax.dot_general(a, b, (((0,), (0,)), ((), ())), preferred_element_type=F32)


def head_lanes(rows, head):
    lane = lax.broadcasted_iota(jnp.int32, (rows, PAIR), 1)
    return (lane >= head * HD) & (lane < (head + 1) * HD)


def one_head(pair_rows, head):
    return jnp.where(head_lanes(pair_rows.shape[0], head), pair_rows, jnp.zeros_like(pair_rows))


def fold8(values, op):
    rows, lanes = values.shape
    return op(values.reshape(rows // 8, 8, lanes), axis=0)


MESH = pl.DeviceIdType.MESH
CONSTANT = pl.Buffered(1)
PIECES = 8
UNROLL = 4
TAIL_POINTS = (0, 2, 3, 5, 7, 9, 10, 12, 12)


class Relay:
    def __init__(self, place, count, view, send_sem, recv_sem):
        self.place, self.count, self.view = place, count, view
        self.send_sem, self.recv_sem = send_sem, recv_sem

    def copy(self, chunk, downward, step):
        return pltpu.make_async_remote_copy(
            src_ref=self.view(chunk), dst_ref=self.view(chunk),
            send_sem=self.send_sem(downward, step), recv_sem=self.recv_sem(chunk),
            device_id={"mp": self.place - 1 if downward else self.place + 1},
            device_id_type=MESH)

    def each(self, step):
        for downward in (0, 1):
            chunk = self.place + step if downward else self.place - step
            exists = chunk < self.count if downward else chunk >= 0
            onward = self.place >= 1 if downward else self.place + 1 < self.count
            yield downward, chunk, exists, onward

    def advance(self, step):
        for downward, chunk, exists, onward in self.each(step):
            if step:
                @pl.when(exists)
                def _():
                    self.copy(chunk, downward, step).wait_recv()
            if step < self.count - 1:
                @pl.when(exists & onward)
                def _():
                    self.copy(chunk, downward, step).start()

    def drain(self):
        for step in range(self.count - 1):
            for downward, chunk, exists, onward in self.each(step):
                @pl.when(exists & onward)
                def _():
                    self.copy(chunk, downward, step).wait_send()


def greet(place, count, partners):
    barrier = pltpu.get_barrier_semaphore()
    for partner in partners:
        pl.semaphore_signal(barrier, 1, device_id={"dp": partner}, device_id_type=MESH)
    for k in range(1, count):
        pl.semaphore_signal(barrier, 1, device_id={"mp": (place + k) % count}, device_id_type=MESH)


def await_greetings(count, partners):
    pl.semaphore_wait(pltpu.get_barrier_semaphore(), len(partners) + count - 1)


def flip(index, bit):
    return index + bit - 2 * bit * ((index // bit) % 2)


def near_first(count):
    return [order[::-1] for order in far_first(count)]


def forward_layer(count, heads_dev,
                  lengths, pair_ids, tok, embed, cot, qkv_w, q_bias, v_bias, out_w, b_out,
                  w_in, b_in, w_last, b_last,
                  x_out, w_out, q_out, k_out, v_out, att_t_out, lse_out,
                  result, mixed_grad, att_grad, g_all,
                  x_all, w_all, w_o, bias_land, biases, acc, stats, att_rows_all, grads, grad_rows,
                  x_send, x_recv, x_copy, w_send, w_recv, plane_send, plane_recv, bias_send, bias_recv):
    seq, turn = pl.program_id(0), pl.program_id(1)
    seqs, pairs = tok.shape[0], w_out.shape[0]
    rows, width = tok.shape[1], tok.shape[2]
    hidden = w_in.shape[1]
    base = heads_dev * 4 * HD
    piece_rows = base // PIECES
    place, data_at = lax.axis_index("mp"), lax.axis_index("dp")
    order = near_first(count)
    chunk = sum(jnp.where((place == m) & (turn == i), order[m][i], 0)
                for m in range(count) for i in range(count))

    def x_relay(s):
        return Relay(
            place, count,
            lambda c: x_all.at[s, pl.ds(pl.multiple_of(c * rows, rows), rows)],
            lambda downward, step: x_send.at[s, downward * (count - 1) + step],
            lambda c: x_recv.at[s, c])

    core, near_x, near_y = [(data_at // bit) % 2 for bit in (1, 2, 4)]
    piece = near_x + 2 * near_y + 4 * core

    def w_span(start, size):
        return pl.ds(pl.multiple_of(start * piece_rows, piece_rows), size * piece_rows)

    w_relay = Relay(
        place, count, lambda c: w_all.at[c, w_span(piece, 1)],
        lambda downward, step: w_send.at[downward * (count - 1) + step],
        lambda c: w_recv.at[c])
    partners = [flip(data_at, 2), flip(data_at, 4), flip(flip(data_at, 2), 4), flip(data_at, 1)]

    def plane(stage):
        span = w_span(4 * core, 4) if stage == 3 else w_span(piece, 1)
        copies = []
        for k in range(1, count):
            source = (place + k) % count
            copies.append(pltpu.make_async_remote_copy(
                src_ref=w_all.at[source, span], dst_ref=w_all.at[source, span],
                send_sem=plane_send.at[stage, k - 1], recv_sem=plane_recv.at[stage, k - 1],
                device_id={"dp": partners[stage]}, device_id_type=MESH))
        return copies

    def bias_copies():
        copies = []
        for k in range(1, count):
            copies.append(pltpu.make_async_remote_copy(
                src_ref=bias_land.at[0], dst_ref=bias_land.at[k],
                send_sem=bias_send.at[k - 1], recv_sem=bias_recv.at[k - 1],
                device_id={"mp": (place + k) % count}, device_id_type=MESH))
        return copies

    @pl.when((seq == 0) & (turn == 0))
    def _():
        greet(place, count, partners)
        turned = qkv_w[...].T
        parts = []
        for j in range(3):
            for h in range(heads_dev):
                parts.append(turned[(h * 3 + j) * HD:(h * 3 + j + 1) * HD])
        w_all[place, 0:heads_dev * 3 * HD, :] = jnp.concatenate(parts, axis=0)
        w_all[place, heads_dev * 3 * HD:base, :] = out_w[...]
        line = lax.broadcasted_iota(jnp.int32, bias_land.shape[1:], 0)
        bias_land[0] = jnp.where(
            line == 0, q_bias[...].astype(F32),
            jnp.where(line == 1, v_bias[...].astype(F32), 0.0)).astype(BF16)
        await_greetings(count, partners)
        w_relay.advance(0)
        for copy in bias_copies():
            copy.start()
        own = pl.ds(pl.multiple_of(place * rows, rows), rows)

        def embed_rows(s):
            row = embed[pl.ds(pair_ids[s], 1), :]
            x_all[s, own, :] = (tok[s].astype(F32) + row).astype(BF16)

        embed_rows(0)
        if count > 2:
            w_relay.advance(1)
        x_relay(0).advance(0)
        for s in range(1, seqs):
            embed_rows(s)
        for step in range(2 if count > 2 else 1, count):
            w_relay.advance(step)
        across = [plane(stage) for stage in range(3)]
        for copies in across:
            for copy in copies:
                copy.start()
        grads[...] = jnp.zeros_like(grads)
        grad_rows[...] = jnp.zeros_like(grad_rows)
        x_relay(0).advance(1)
        for copies in across:
            for copy in copies:
                copy.wait()
        for copy in plane(3):
            copy.start()
        for copy in bias_copies():
            copy.wait()
        for p in range(pairs):
            if heads_dev == 2:
                both = bias_land[(place + count - p) % count].astype(F32)
            else:
                both = jnp.concatenate(
                    [bias_land[(place + count - 2 * p - half) % count].astype(F32) for half in range(2)],
                    axis=1)
            biases[:, p * PAIR:(p + 1) * PAIR] = both
        for copy in plane(3):
            copy.wait()
        w_relay.drain()
        for p in range(pairs):
            if heads_dev == 2:
                w_out[p] = w_all[p, 0:3 * PAIR, :]
                w_o[p * PAIR:(p + 1) * PAIR, :] = w_all[p, 3 * PAIR:4 * PAIR, :]
            else:
                for half in range(2):
                    for j in range(4):
                        strip = w_all[2 * p + half, j * HD:(j + 1) * HD, :]
                        if j < 3:
                            w_out[p, j * PAIR + half * HD:j * PAIR + (half + 1) * HD, :] = strip
                        else:
                            w_o[p * PAIR + half * HD:p * PAIR + (half + 1) * HD, :] = strip

    def hbm_copy(s):
        return pltpu.make_async_copy(x_all.at[s], x_out.at[s], x_copy.at[s])

    for t in range(2, count - 1):
        @pl.when(turn == t - 1)
        def _():
            x_relay(seq).advance(t)
    if count > 2:
        @pl.when(turn == count - 1)
        def _():
            x_relay(seq).advance(count - 1)

    @pl.when((turn == max(count - 3, 0)) & (seq + 1 < seqs))
    def _():
        x_relay(seq + 1).advance(0)

    length = lengths[seq]
    own = pl.ds(pl.multiple_of(place * rows, rows), rows)
    at = pl.ds(pl.multiple_of(chunk * rows, rows), rows)

    @pl.when(turn == 0)
    def _():
        acc[...] = jnp.zeros_like(acc)
        line = lax.broadcasted_iota(jnp.int32, stats.shape, 1)
        stats[...] = jnp.where(line < 2, NEGATIVE, 0.0)

        def query_step(p, _):
            lanes = pl.ds(pl.multiple_of(p * PAIR, PAIR), PAIR)
            q_pair = (nt(x_all[seq, own, :], w_out[p, 0:PAIR, :]) + biases[0:1, lanes]).astype(BF16)
            q_out[0, p] = q_pair * BF16(HD ** -0.5)
            return 0

        lax.fori_loop(0, pairs, query_step, 0)

    for p in range(pairs):
        kv = nt(x_all[seq, at, :], w_out[p, PAIR:3 * PAIR, :])
        k_out[0, p, at, :] = kv[:, :PAIR].astype(BF16)
        v_out[0, p, at, :] = (kv[:, PAIR:] + biases[1:2, p * PAIR:(p + 1) * PAIR]).astype(BF16)

    def pair_step(p, _):
        k_blk, v_blk, q_pair = k_out[0, p, at, :], v_out[0, p, at, :], q_out[0, p]
        keep = (lax.broadcasted_iota(jnp.int32, (rows, rows), 0) + chunk * rows) < length
        scores = [jnp.where(keep, nt(k_blk, one_head(q_pair, h)), NEGATIVE) for h in range(2)]
        before = [stats[p, h:h + 1, :] for h in range(2)]
        tops = [jnp.maximum(before[h], jnp.max(scores[h], axis=0, keepdims=True) * LOG2E) for h in range(2)]
        probs = [jnp.exp2(scores[h] * LOG2E - tops[h]) for h in range(2)]
        added = tn(v_blk, jnp.concatenate([pr.astype(BF16) for pr in probs], axis=1))
        for h in range(2):
            half = slice(h * HD, (h + 1) * HD)
            shrink = jnp.exp2(before[h] - tops[h])
            stats[p, h:h + 1, :] = tops[h]
            stats[p, 2 + h:3 + h, :] = (
                stats[p, 2 + h:3 + h, :] * shrink + jnp.sum(probs[h], axis=0, keepdims=True))
            acc[p, half, :] = acc[p, half, :] * shrink + added[half, h * rows:(h + 1) * rows]
        return 0

    lax.fori_loop(0, pairs, pair_step, 0, unroll=UNROLL)

    @pl.when(turn == count - 1)
    def _():
        hbm_copy(seq).start()

        @pl.when(seq + 1 < seqs)
        def _():
            x_relay(seq + 1).advance(1)
        for p in range(pairs):
            total = stats[p, 2:4, :]
            inverse = 1.0 / total
            att_t = jnp.concatenate(
                [acc[p, h * HD:(h + 1) * HD, :] * inverse[h:h + 1] for h in range(2)], axis=0)
            att_t_out[0, p] = att_t
            att_rows_all[:, p * PAIR:(p + 1) * PAIR] = att_t.T.astype(BF16)
            lse_out[0, p] = jnp.concatenate(
                [stats[p, 0:2, :] + jnp.log2(total), jnp.zeros((6, rows), F32)], axis=0)

        cot_rows = cot[0]
        att_rows = att_rows_all[...]
        row = embed[pl.ds(pair_ids[seq], 1), :]
        mixed = (tok[seq].astype(F32) + row) + (nn(att_rows, w_o[...]) + b_out[...])
        mixed_low = mixed.astype(BF16)
        out_sum = mixed + b_last[...]
        back_sum = cot_rows.astype(F32)
        root = math.sqrt(2.0 / math.pi)
        for c in range(hidden // width):
            at = slice(c * width, (c + 1) * width)
            pre = nn(mixed_low, w_in[:, at]) + b_in[:, at]
            square = pre * pre
            th = jnp.tanh(root * pre * (1.0 + 0.044715 * square))
            half = 0.5 * (1.0 + th)
            act = (pre * half).astype(BF16)
            slope = half + (0.5 * root) * pre * (1.0 - th * th) * (1.0 + (3 * 0.044715) * square)
            out_sum += nn(act, w_last[at, :])
            back = (nt(cot_rows, w_last[at, :]) * slope).astype(BF16)
            grad_rows[c:c + 1, :] += jnp.sum(back.astype(F32), axis=0, keepdims=True)
            back_sum += nt(back, w_in[:, at])
            grads[at, :] += tn(act, cot_rows)
            grads[hidden + c * width:hidden + (c + 1) * width, :] += tn(mixed_low, back)
        result[0] = out_sum.astype(BF16)
        back_low = back_sum.astype(BF16)
        mixed_grad[0] = back_low
        at = hidden // width
        grad_rows[at:at + 1, :] += jnp.sum(cot_rows.astype(F32), axis=0, keepdims=True)
        grad_rows[at + 1:at + 2, :] += jnp.sum(back_low.astype(F32), axis=0, keepdims=True)
        grads[2 * hidden:, :] += tn(att_rows, back_low)
        att_grad[0] = nt(back_low, w_o[...]).astype(BF16)

    @pl.when((seq == seqs - 1) & (turn == count - 1))
    def _():
        def narrow(j, _):
            at = pl.ds(pl.multiple_of(j * width, width), width)
            g_all[at, :] = grads[at, :].astype(BF16)
            return 0

        lax.fori_loop(0, grads.shape[0] // width, narrow, 0)
        rest = g_all.shape[0] - grads.shape[0]
        g_all[grads.shape[0]:, :] = jnp.concatenate(
            [grad_rows[...], jnp.zeros((rest - 8, width), F32)], axis=0).astype(BF16)
        for s in range(seqs):
            x_relay(s).drain()
            hbm_copy(s).wait()


def fixed(shape):
    return pl.BlockSpec(shape, lambda *_: (0,) * len(shape), pipeline_mode=CONSTANT)


def call_layer(count, lengths, pair_ids, tok, embed, cot, qkv_w, q_bias, v_bias, out_w, b_out,
               w_in, b_in, w_last, b_last):
    seqs, rows, width = tok.shape
    hidden = w_in.shape[1]
    heads_dev = qkv_w.shape[1] // (3 * HD)
    full = count * rows
    pairs = width // PAIR
    g_rows = -(-(2 * hidden + width + 16) // 256) * 256
    in_smem = pl.BlockSpec(memory_space=pltpu.SMEM)
    per_seq = lambda: pl.BlockSpec((1, rows, width), lambda s, p: (s, 0, 0))
    per_pair = lambda *tail: pl.BlockSpec((1, pairs) + tail, lambda s, p: (s, 0, 0, 0))
    shape = jax.ShapeDtypeStruct
    return pl.pallas_call(
        functools.partial(forward_layer, count, heads_dev),
        grid=(seqs, count),
        in_specs=[in_smem, in_smem, fixed(tok.shape), fixed(embed.shape), per_seq(), fixed(qkv_w.shape),
                  fixed(q_bias.shape), fixed(v_bias.shape), fixed(out_w.shape), fixed(b_out.shape),
                  fixed(w_in.shape), fixed(b_in.shape), fixed(w_last.shape), fixed(b_last.shape)],
        out_specs=[pl.BlockSpec(memory_space=pl.ANY), fixed((pairs, 3 * PAIR, width)),
                   per_pair(rows, PAIR), per_pair(full, PAIR), per_pair(full, PAIR),
                   per_pair(PAIR, rows), per_pair(8, rows),
                   per_seq(), per_seq(), per_seq(), fixed((g_rows, width))],
        out_shape=[
            shape((seqs, full, width), BF16),
            shape((pairs, 3 * PAIR, width), BF16),
            shape((seqs, pairs, rows, PAIR), BF16),
            shape((seqs, pairs, full, PAIR), BF16),
            shape((seqs, pairs, full, PAIR), BF16),
            shape((seqs, pairs, PAIR, rows), F32),
            shape((seqs, pairs, 8, rows), F32),
            shape((seqs, rows, width), BF16),
            shape((seqs, rows, width), BF16),
            shape((seqs, rows, width), BF16),
            shape((g_rows, width), BF16),
        ],
        scratch_shapes=[
            pltpu.VMEM((seqs, full, width), BF16),
            pltpu.VMEM((count, heads_dev * 4 * HD, width), BF16),
            pltpu.VMEM((width, width), BF16),
            pltpu.VMEM((count, 16, heads_dev * HD), BF16),
            pltpu.VMEM((16, width), F32),
            pltpu.VMEM((pairs, PAIR, rows), F32),
            pltpu.VMEM((pairs, 8, rows), F32),
            pltpu.VMEM((rows, width), BF16),
            pltpu.VMEM((2 * hidden + width, width), F32),
            pltpu.VMEM((8, width), F32),
            pltpu.SemaphoreType.DMA((seqs, 2 * (count - 1))),
            pltpu.SemaphoreType.DMA((seqs, count)),
            pltpu.SemaphoreType.DMA((seqs,)),
            pltpu.SemaphoreType.DMA((2 * (count - 1),)),
            pltpu.SemaphoreType.DMA((count,)),
            pltpu.SemaphoreType.DMA((4, count - 1)),
            pltpu.SemaphoreType.DMA((4, count - 1)),
            pltpu.SemaphoreType.DMA((count - 1,)),
            pltpu.SemaphoreType.DMA((count - 1,)),
        ],
        cost_estimate=pl.CostEstimate(flops=120 * 10 ** 9, bytes_accessed=60 << 20,
                                      transcendentals=seqs * pairs * 2 * full * rows),
        compiler_params=pltpu.CompilerParams(
            collective_id=0, has_side_effects=True, vmem_limit_bytes=VMEM_LIMIT),
        name="forward_layer",
    )(lengths, pair_ids, tok, embed, cot, qkv_w, q_bias, v_bias, out_w, b_out, w_in, b_in, w_last, b_last)


def row_step(size):
    for step in (256, 160, 128, 80, 64, 32, 16):
        if size % step == 0:
            return step
    return size


def aligned(start, size, unit=16):
    return pl.ds(pl.multiple_of(start, unit), size)


class Reducer:
    def __init__(self, data, land, group, rows, bits, where_at, send_sem, recv_sem, free_sem=None):
        self.data, self.land, self.group = data, land, group
        self.send_sem, self.recv_sem, self.free_sem = send_sem, recv_sem, free_sem
        self.stages, self.landed = [], 0
        start, size = 0, rows
        for axis, bit in bits:
            index = where_at[axis]
            digit = (index // bit) % 2
            halves = (size // 2) % 16 == 0
            if halves:
                size //= 2
                keep, other = start + digit * size, start + (1 - digit) * size
            else:
                keep = other = start
            self.stages.append((axis, flip(index, bit), halves, keep, other, size, self.landed))
            self.landed += size
            start = keep
        self.start, self.size = start, size

    def copy(self, j):
        axis, partner, _, _, other, size, landed = self.stages[j]
        return pltpu.make_async_remote_copy(
            src_ref=self.data.at[self.group, :, aligned(other, size)],
            dst_ref=self.land.at[self.group, :, pl.ds(landed, size)],
            send_sem=self.send_sem.at[self.group, j],
            recv_sem=self.recv_sem.at[self.group, j],
            device_id={axis: partner}, device_id_type=MESH)

    def finish(self, j):
        self.copy(j).wait()
        axis, partner, halves, keep, _, size, landed = self.stages[j]
        if self.free_sem is not None and halves:
            pl.semaphore_signal(self.free_sem.at[self.group, j], 1, device_id={axis: partner},
                                device_id_type=MESH)
        step = row_step(size)
        slots = self.data.shape[1]
        for slot in range(slots):
            def add(r, _):
                at = aligned(keep + r * step, step)
                more = self.land[self.group, slot, aligned(landed + r * step, step), :]
                self.data[self.group, slot, at, :] = self.data[self.group, slot, at, :] + more
                return 0

            lax.fori_loop(0, size // step, add, 0)

    def back(self, j):
        axis, partner, _, keep, _, size, _ = self.stages[j]
        view = self.data.at[self.group, :, aligned(keep, size)]
        at = len(self.stages) + j
        return pltpu.make_async_remote_copy(
            src_ref=view, dst_ref=view, send_sem=self.send_sem.at[self.group, at],
            recv_sem=self.recv_sem.at[self.group, at],
            device_id={axis: partner}, device_id_type=MESH)

    def back_start(self, j):
        pl.semaphore_wait(self.free_sem.at[self.group, j], 1)
        self.back(j).start()

    def events(self, line=None):
        doubling = [j for j in range(len(self.stages)) if self.stages[j][2]][::-1]
        middle = line.events(self.start, self.size) if line else []
        run = [lambda: self.copy(0).start()]
        for j in range(len(self.stages)):
            def after(j=j):
                self.finish(j)
                if j + 1 < len(self.stages):
                    self.copy(j + 1).start()
                elif middle:
                    middle[0]()
                else:
                    self.back_start(doubling[0])
            run.append(after)
        for i in range(1, len(middle)):
            def after_line(i=i):
                middle[i]()
                if i + 1 == len(middle):
                    self.back_start(doubling[0])
            run.append(after_line)
        for i, j in enumerate(doubling):
            def after_back(i=i, j=j):
                self.back(j).wait()
                if i + 1 < len(doubling):
                    self.back_start(doubling[i + 1])
            run.append(after_back)
        return run


class Line:
    def __init__(self, data, land, group, landed, place, send_sem, recv_sem):
        self.data, self.land, self.group, self.landed = data, land, group, landed
        self.place, self.send_sem, self.recv_sem = place, send_sem, recv_sem
        self.end = (place == 0) | (place == 3)
        self.inner = (place == 1) | (place == 2)

    def copy(self, step, target, start, size):
        return pltpu.make_async_remote_copy(
            src_ref=self.data.at[self.group, :, aligned(start, size)],
            dst_ref=self.land.at[self.group, :, pl.ds(self.landed + step * size, size)],
            send_sem=self.send_sem.at[self.group, step], recv_sem=self.recv_sem.at[self.group, step],
            device_id={"mp": target}, device_id_type=MESH)

    def events(self, start, size):
        inward = jnp.where(self.place < 2, 1, 2)
        across = jnp.where(self.place < 2, 2, 1)
        outward = jnp.where(self.place < 2, 0, 3)
        first = self.copy(0, inward, start, size)
        second = self.copy(1, across, start, size)
        third = self.copy(2, outward, start, size)
        unit = row_step(size)

        def take(step, add):
            def move(r, _):
                at = aligned(start + r * unit, unit)
                more = self.land[self.group, 0, aligned(self.landed + step * size + r * unit, unit), :]
                if add:
                    more = self.data[self.group, 0, at, :] + more
                self.data[self.group, 0, at, :] = more
                return 0

            lax.fori_loop(0, size // unit, move, 0)

        def begin():
            pl.when(self.end)(first.start)

        def swap():
            @pl.when(self.inner)
            def _():
                first.wait_recv()
                take(0, True)
                second.start()

        def hand_back():
            @pl.when(self.inner)
            def _():
                second.wait()
                take(1, True)
                third.start()

        def close():
            @pl.when(self.inner)
            def _():
                third.wait_send()

            @pl.when(self.end)
            def _():
                first.wait_send()
                third.wait_recv()
                take(2, False)

        return [begin, swap, hand_back, close]


def bit_list(size):
    return [1 << b for b in range(size.bit_length() - 1)]


def far_first(count):
    table = []
    for m in range(count):
        order = []
        for k in range(count - 1, 0, -1):
            order += [c for c in (m + k, m - k) if 0 <= c < count]
        table.append(order + [m])
    return table


def backward_layer(count, data_count, heads_dev, tail_points,
                   lengths, pair_ids, x_seq, weight, q_in, k_in, v_in, att_t, lse, grad_in, mixed_grad, g_in,
                   token_grad, g_out, own_out,
                   a_buf, a_land, b_buf, b_land, b_parts, own_buf, parts, land, both_all, x_acc, dq_acc, delta_all,
                   w_acc, bias_acc, col_acc, table_acc,
                   load_sem, a_send, a_recv, a_free, l_send, l_recv, b_send, b_recv, s_send, s_recv, r_send, r_recv):
    seq, turn = pl.program_id(0), pl.program_id(1)
    seqs, pairs = token_grad.shape[0], weight.shape[0]
    rows, width = token_grad.shape[1], token_grad.shape[2]
    place, data_at = lax.axis_index("mp"), lax.axis_index("dp")
    where_at = {"mp": place, "dp": data_at}
    point = seq * count + turn
    data_bits, place_bits = bit_list(data_count), bit_list(count)
    swapped = [{2: 4, 4: 2}.get(b, b) for b in data_bits]

    order = far_first(count)
    chunk = sum(jnp.where((place == m) & (turn == i), order[m][i], 0)
                for m in range(count) for i in range(count))

    in_line = count == 4
    a_sums = [
        Reducer(a_buf, a_land, g, a_buf.shape[2],
                [("dp", b) for b in (data_bits, swapped)[g]] + [("mp", b) for b in place_bits if not in_line],
                where_at, a_send, a_recv, a_free)
        for g in range(2)]
    a_events = [
        a.events(Line(a_buf, a_land, g, a.landed, place, l_send, l_recv) if in_line else None)
        for g, a in enumerate(a_sums)]
    b_sums = [
        Reducer(b_buf, b_land, g, b_buf.shape[2], [("dp", b) for b in (data_bits, swapped)[g]],
                where_at, b_send, b_recv)
        for g in range(2)]

    def send_part(s, c, downward):
        slot = jnp.where((place - 1 == c) & (downward == 1), count, c)
        return pltpu.make_async_remote_copy(
            src_ref=parts.at[s, c], dst_ref=land.at[s, slot],
            send_sem=s_send.at[s, c], recv_sem=s_recv.at[s, slot],
            device_id={"mp": place - 1 if downward else place + 1}, device_id_type=MESH)

    def await_part(s, slot):
        pltpu.make_async_remote_copy(
            src_ref=land.at[s, slot], dst_ref=land.at[s, slot],
            send_sem=s_send.at[s, 0], recv_sem=s_recv.at[s, slot],
            device_id={"mp": (place + 1) % count}, device_id_type=MESH).wait_recv()

    def combine(s, k):
        for downward in (0, 1):
            c = place - k if downward else place + k
            go = ((c >= 0) & (place + 1 < count)) if downward else ((c < count) & (place >= 1))

            @pl.when(go)
            def _():
                await_part(s, c)
                parts[s, c] = parts[s, c] + land[s, c]
                send_part(s, c, downward).start()

    def conclude(s):
        for downward in (0, 1):
            slot = count if downward else place

            @pl.when((place + 1 < count) if downward else (place >= 1))
            def _():
                await_part(s, slot)
                token_grad[s] += land[s, slot].astype(F32)

    def load():
        return pltpu.make_async_copy(g_in, a_buf, load_sem.at[0])

    def store():
        return pltpu.make_async_copy(a_buf, g_out, load_sem.at[1])

    partners = [flip(data_at, b) for b in data_bits]

    @pl.when(point == 0)
    def _():
        greet(place, count, partners)
        load().start()
        w_acc[...] = jnp.zeros_like(w_acc)
        bias_acc[...] = jnp.zeros_like(bias_acc)
        table_acc[...] = jnp.zeros_like(table_acc)
        await_greetings(count, partners)
        load().wait()
        for events in a_events:
            events[0]()

    @pl.when(turn == 0)
    def _():
        col_acc[...] = jnp.zeros_like(col_acc)
        dq_acc[...] = jnp.zeros_like(dq_acc)
        for p in range(pairs):
            prod = grad_in[0, :, p * PAIR:(p + 1) * PAIR].astype(F32).T * att_t[0, p]
            delta_all[p, 0:1, :] = jnp.sum(prod[:HD], axis=0, keepdims=True)
            delta_all[p, 1:2, :] = jnp.sum(prod[HD:], axis=0, keepdims=True)

    length = lengths[seq]
    at = aligned(chunk * rows, rows, rows)
    own = aligned(place * rows, rows, rows)
    def pair_step(p, _):
        lanes = aligned(p * PAIR, PAIR, PAIR)
        q_pair = q_in[0, p]
        grad_pair = grad_in[0, :, lanes]
        k_blk = k_in[0, p, at, :]
        v_blk = v_in[0, p, at, :]
        keep = (lax.broadcasted_iota(jnp.int32, (rows, rows), 0) + chunk * rows) < length
        dk = jnp.zeros((rows, PAIR), F32)
        dv = jnp.zeros((rows, PAIR), F32)
        for h in range(2):
            q_head, g_head = one_head(q_pair, h), one_head(grad_pair, h)
            s = jnp.where(keep, nt(k_blk, q_head) * LOG2E, NEGATIVE)
            pr = jnp.exp2(s - lse[0, p, h:h + 1, :])
            dp = nt(v_blk, g_head)
            ds = (pr * (dp - delta_all[p, h:h + 1, :])).astype(BF16)
            dv += nn(pr.astype(BF16), g_head)
            dk += nn(ds, q_head)
            dq_acc[p, h] += tn(k_blk, ds)
        dv = dv.astype(BF16)
        both = jnp.concatenate([dk.astype(BF16), dv], axis=1)
        both_all[p] = both
        bias_acc[1:2, lanes] += jnp.sum(dv.astype(F32), axis=0, keepdims=True)
        return 0

    lax.fori_loop(0, pairs, pair_step, 0, unroll=4)
    x_acc[...] = sum(nn(both_all[p], weight[p, PAIR:, :]) for p in range(pairs))
    for p in range(pairs):
        w_acc[p, PAIR:, :] += tn(both_all[p], x_seq[0, at, :])

    @pl.when(turn < count - 1)
    def _():
        parts[seq, chunk] = x_acc[...].astype(BF16)
        for downward in (0, 1):
            @pl.when((place == (count - 1 if downward else 0)) & (chunk != place))
            def _():
                send_part(seq, chunk, downward).start()

    @pl.when(turn == count - 1)
    def _():
        def query_step(p, _):
            lanes = aligned(p * PAIR, PAIR, PAIR)
            dq_t = jnp.concatenate(
                [dq_acc[p, h, h * HD:(h + 1) * HD, :] for h in range(2)], axis=0) * (HD ** -0.5)
            dq = dq_t.T.astype(BF16)
            x_acc[...] += nn(dq, weight[p, :PAIR, :])
            w_acc[p, :PAIR, :] += tn(dq, x_seq[0, own, :])
            bias_acc[0:1, lanes] += jnp.sum(dq.astype(F32), axis=0, keepdims=True)
            return 0

        lax.fori_loop(0, pairs, query_step, 0)
        x_acc[...] += mixed_grad[0].astype(F32)
        token_grad[seq] = x_acc[...]

    col_acc[0:1, :] += jnp.sum(x_acc[...], axis=0, keepdims=True)

    @pl.when(turn == count - 1)
    def _():
        line = lax.broadcasted_iota(jnp.int32, table_acc.shape, 0)
        table_acc[...] += jnp.where(line == pair_ids[seq], col_acc[0:1, :], 0.0)

    slots = {2: 2, 1: 4} if count == 4 else {k: count + (count - 2 - k) for k in range(1, count - 1)}
    for k in range(count - 2, 0, -1):
        turns, seq_back = slots[k] % count, slots[k] // count

        @pl.when((turn == turns) & (seq >= seq_back))
        def _():
            combine(seq - seq_back, k)

    @pl.when((turn == count - 1) & (seq >= 1))
    def _():
        conclude(seq - 1)

    total = seqs * count
    later = len(a_events[0]) - 1
    in_tail = []
    for e in range(1, later + 1):
        when_at = tail_points[e - 1] if tail_points else (e * total) // (later + 1)
        if when_at >= total:
            in_tail.append(e)
            continue

        @pl.when(point == when_at)
        def _():
            for events in a_events:
                events[e]()

    @pl.when(point == total - 1)
    def _():
        last = seqs - 1
        base = heads_dev * 3 * HD
        half = count // 2
        for m in range(count):
            g, slot = m // half, m % half
            if heads_dev == 2:
                b_buf[g, slot, 0:base, :] = w_acc[m].astype(BF16)
            else:
                for j in range(3):
                    lo = j * PAIR + (m % 2) * HD
                    b_buf[g, slot, j * HD:(j + 1) * HD, :] = w_acc[m // 2, lo:lo + HD, :].astype(BF16)
            b_buf[g, slot, base:base + 16, :] = bias_acc[...].astype(BF16)
            b_buf[g, slot, base + 16:base + 32, :] = table_acc[...].astype(BF16)
            rest = b_buf.shape[2] - base - 32
            b_buf[g, slot, base + 32:, :] = jnp.zeros((rest, width), BF16)
        stages = len(b_sums[0].stages)
        for b in b_sums:
            b.copy(0).start()
        tail_k = [k for k in range(count - 2, 0, -1) if slots[k] >= count]
        if tail_k:
            combine(last, tail_k.pop(0))
        for j in range(stages):
            for b in b_sums:
                b.finish(j)
                if j + 1 < stages:
                    b.copy(j + 1).start()
            if tail_k:
                combine(last, tail_k.pop(0))
        strip = b_sums[0].size
        mine = place // half
        start = jnp.where(mine == 0, b_sums[0].start, b_sums[1].start)

        def scatter(k):
            target = (place + k) % count
            g = target // half
            begin = jnp.where(g == 0, b_sums[0].start, b_sums[1].start)
            return pltpu.make_async_remote_copy(
                src_ref=b_buf.at[g, target % half, aligned(begin, strip)],
                dst_ref=b_parts.at[k - 1],
                send_sem=r_send.at[k - 1], recv_sem=r_recv.at[k - 1],
                device_id={"mp": target}, device_id_type=MESH)

        for k in range(1, count):
            scatter(k).start()
        for k in tail_k:
            combine(last, k)
        for e in in_tail[:-1]:
            for events in a_events:
                events[e]()
        for k in range(1, count):
            scatter(k).wait()
        home = b_buf[mine, place % half, aligned(start, strip), :].astype(F32)
        for k in range(1, count):
            home += b_parts[k - 1].astype(F32)
        own_buf[aligned(start, strip), :] = home.astype(BF16)

        def back(j):
            partner = jnp.where(mine == 0, b_sums[0].stages[j][1], b_sums[1].stages[j][1])
            keep = jnp.where(mine == 0, b_sums[0].stages[j][3], b_sums[1].stages[j][3])
            size = b_sums[0].stages[j][5]
            view = own_buf.at[aligned(keep, size)]
            return pltpu.make_async_remote_copy(
                src_ref=view, dst_ref=view, send_sem=r_send.at[count - 1 + j],
                recv_sem=r_recv.at[count - 1 + j], device_id={"dp": partner}, device_id_type=MESH)

        for j in reversed(range(stages)):
            back(j).start()
            back(j).wait()
            if j == stages - 1:
                for e in in_tail[-1:]:
                    for events in a_events:
                        events[e]()
                store().start()
        own_out[...] = own_buf[...]
        conclude(last)
        store().wait()
        for s in range(seqs):
            for k in range(1, count):
                for downward in (0, 1):
                    c = place - k if downward else place + k

                    @pl.when((c >= 0) if downward else (c < count))
                    def _():
                        send_part(s, c, downward).wait_send()


def call_backward(count, data_count, heads_dev, lengths, pair_ids, x_all, weight, q, k, v, att_t, lse,
                  grad, mixed_grad, g_all):
    seqs, full, width = x_all.shape
    rows = full // count
    pairs = weight.shape[0]
    a_rows = g_all.shape[0] // 2
    base = heads_dev * 3 * HD
    slot_rows = -(-(base + 32) // 128) * 128
    data_bits, place_bits = bit_list(data_count), bit_list(count)

    def landing(size, bits):
        landed = 0
        for _ in range(bits):
            size = size // 2 if (size // 2) % 16 == 0 else size
            landed += size
        return landed, size

    if count == 4:
        a_landed, strip = landing(a_rows, len(data_bits))
        a_landed += 3 * strip
    else:
        a_landed, _ = landing(a_rows, len(data_bits) + len(place_bits))
    b_landed, strip = landing(slot_rows, len(data_bits))
    a_stages, b_stages = len(data_bits) + len(place_bits), len(data_bits)
    tail_points = TAIL_POINTS if (count, data_count) == (4, 8) else None
    in_smem = pl.BlockSpec(memory_space=pltpu.SMEM)
    in_hbm = pl.BlockSpec(memory_space=pl.ANY)
    seq_block = lambda shape, mode=None: pl.BlockSpec(
        (1,) + shape[1:], lambda s, i: (s,) + (0,) * (len(shape) - 1), pipeline_mode=mode)
    shape = jax.ShapeDtypeStruct
    dma = pltpu.SemaphoreType.DMA
    return pl.pallas_call(
        functools.partial(backward_layer, count, data_count, heads_dev, tail_points),
        grid=(seqs, count),
        in_specs=[in_smem, in_smem, seq_block(x_all.shape, CONSTANT), fixed(weight.shape),
                  seq_block(q.shape, CONSTANT), seq_block(k.shape),
                  seq_block(v.shape), seq_block(att_t.shape, CONSTANT),
                  seq_block(lse.shape), seq_block(grad.shape), seq_block(mixed_grad.shape), in_hbm],
        out_specs=[fixed((seqs, rows, width)), in_hbm, fixed((slot_rows, width))],
        out_shape=[
            shape((seqs, rows, width), F32),
            shape((2, 1, a_rows, width), BF16),
            shape((slot_rows, width), BF16),
        ],
        scratch_shapes=[
            pltpu.VMEM((2, 1, a_rows, width), BF16),
            pltpu.VMEM((2, 1, a_landed, width), BF16),
            pltpu.VMEM((2, count // 2, slot_rows, width), BF16),
            pltpu.VMEM((2, count // 2, b_landed, width), BF16),
            pltpu.VMEM((count - 1, strip, width), BF16),
            pltpu.VMEM((slot_rows, width), BF16),
            pltpu.VMEM((seqs, count, rows, width), BF16),
            pltpu.VMEM((seqs, count + 1, rows, width), BF16),
            pltpu.VMEM((pairs, rows, 2 * PAIR), BF16),
            pltpu.VMEM((rows, width), F32),
            pltpu.VMEM((pairs, 2, PAIR, rows), F32),
            pltpu.VMEM((pairs, 8, rows), F32),
            pltpu.VMEM((pairs, 3 * PAIR, width), F32),
            pltpu.VMEM((16, width), F32),
            pltpu.VMEM((8, width), F32),
            pltpu.VMEM((16, width), F32),
            dma((2,)), dma((2, 2 * a_stages)), dma((2, 2 * a_stages)),
            pltpu.SemaphoreType.REGULAR((2, a_stages)), dma((2, 3)), dma((2, 3)),
            dma((2, b_stages)), dma((2, b_stages)),
            dma((seqs, count)), dma((seqs, count + 1)),
            dma((count - 1 + b_stages,)), dma((count - 1 + b_stages,)),
        ],
        cost_estimate=pl.CostEstimate(flops=200 * 10 ** 9, bytes_accessed=60 << 20,
                                      transcendentals=seqs * pairs * 2 * full * rows),
        compiler_params=pltpu.CompilerParams(
            collective_id=1, has_side_effects=True, vmem_limit_bytes=VMEM_LIMIT),
        name="backward_layer",
    )(lengths, pair_ids, x_all, weight, q, k, v, att_t, lse, grad, mixed_grad,
      g_all.reshape(2, 1, a_rows, width))


def finish(place_ref, last_rows, in_rows, out_strip, vector_rows, own, token_in, result_in,
           last_grad, in_grad, out_grad, out_bias, in_bias, last_bias,
           qkv_grad, q_bias_grad, v_bias_grad, table, token_out, result_out, *, heads_dev):
    width = own.shape[1]
    place = place_ref[0]
    last_grad[...] = last_rows[...].astype(F32)
    in_grad[...] = in_rows[...].astype(F32)
    token_out[...] = token_in[...]
    result_out[...] = result_in[...]

    @pl.when(pl.program_id(0) == pl.num_programs(0) - 1)
    def _():
        base = heads_dev * 3 * HD
        bias_len = heads_dev * HD
        out_grad[...] = out_strip[...].astype(F32)
        vectors = vector_rows[0:16, :].astype(F32)
        parts = in_bias.shape[1] // width
        for c in range(parts):
            in_bias[:, c * width:(c + 1) * width] = vectors[c:c + 1]
        last_bias[...] = vectors[parts:parts + 1]
        out_bias[...] = vectors[parts + 1:parts + 2]
        turned = own[:base, :].astype(F32).T
        parts = []
        for h in range(heads_dev):
            for j in range(3):
                lo = (j * heads_dev + h) * HD
                parts.append(turned[:, lo:lo + HD])
        qkv_grad[...] = jnp.concatenate(parts, axis=1)
        if heads_dev == 2:
            rows = own[base:base + 16, pl.ds(pl.multiple_of(place * PAIR, PAIR), PAIR)].astype(F32)
        else:
            rows = own[base:base + 16, pl.ds(pl.multiple_of((place // 2) * PAIR, PAIR), PAIR)].astype(F32)
            rows = jnp.where(place % 2 == 0, rows[:, :HD], rows[:, HD:])
        q_bias_grad[...] = rows[0:1, :bias_len]
        v_bias_grad[...] = rows[1:2, :bias_len]
        table[...] = own[base + 16:base + 32, :].astype(F32)[:table.shape[0]]


def call_finish(place, sums, own, token_grad, result, heads_dev, hidden, table_rows):
    seqs, rows, width = token_grad.shape
    cut = width
    tail = width // 2
    parts = hidden // cut
    base = heads_dev * 3 * HD
    out_rows = heads_dev * HD
    shape = jax.ShapeDtypeStruct
    strip = lambda: pl.BlockSpec((seqs, rows // parts, width), lambda i, *_: (0, i, 0))
    return pl.pallas_call(
        functools.partial(finish, heads_dev=heads_dev),
        grid_spec=pltpu.PrefetchScalarGridSpec(
            num_scalar_prefetch=1,
            grid=(parts,),
            in_specs=[pl.BlockSpec((cut, width), lambda i, *_: (i, 0)),
                      pl.BlockSpec((cut, width), lambda i, *_: (parts + i, 0)),
                      pl.BlockSpec((out_rows, width), lambda i, at: (2 * hidden // out_rows + at[0], 0)),
                      pl.BlockSpec((tail, width), lambda i, *_: ((2 * hidden + width) // tail, 0)),
                      fixed(own.shape), strip(), strip()],
            out_specs=[pl.BlockSpec((cut, width), lambda i, *_: (i, 0)),
                       pl.BlockSpec((cut, width), lambda i, *_: (0, i)),
                       fixed((out_rows, width)), fixed((1, width)), fixed((1, hidden)), fixed((1, width)),
                       fixed((width, base)), fixed((1, out_rows)), fixed((1, out_rows)),
                       fixed((table_rows, width)), strip(), strip()],
        ),
        out_shape=[shape((hidden, width), F32), shape((width, hidden), F32), shape((out_rows, width), F32),
                   shape((1, width), F32), shape((1, hidden), F32), shape((1, width), F32),
                   shape((width, base), F32), shape((1, out_rows), F32), shape((1, out_rows), F32),
                   shape((table_rows, width), F32), shape(token_grad.shape, F32), shape(result.shape, BF16)],
        compiler_params=pltpu.CompilerParams(vmem_limit_bytes=VMEM_LIMIT),
        name="finish",
    )(place, sums, sums, sums, sums, own, token_grad, result)


def body(
    tokens,
    pair_ids,
    lengths,
    pair_embed,
    qkv_weight,
    q_bias,
    v_bias,
    out_weight,
    out_bias,
    ffn_in_weight,
    ffn_in_bias,
    ffn_out_weight,
    ffn_out_bias,
    cotangent,
):
    local_rows, seqs, width = tokens.shape
    table_rows = pair_embed.shape[0]
    count = lax.axis_size("mp")
    place = lax.axis_index("mp").astype(jnp.int32).reshape(1)
    tok = jnp.transpose(tokens, (1, 0, 2))
    cot = jnp.transpose(cotangent, (1, 0, 2))
    bias_len = q_bias.shape[0]
    (x_all, w_pairs, q, k, v, att_t, lse, result, mixed_grad, att_grad, g_all) = call_layer(
        count, lengths, pair_ids, tok, pair_embed, cot, qkv_weight, q_bias[None], v_bias[None],
        out_weight, out_bias[None], ffn_in_weight, ffn_in_bias[None], ffn_out_weight,
        ffn_out_bias[None])
    heads_dev = bias_len // HD
    tokens_grad, g_sum, own = call_backward(
        count, lax.axis_size("dp"), heads_dev, lengths, pair_ids, x_all, w_pairs, q, k, v, att_t, lse,
        att_grad, mixed_grad, g_all)

    hidden = ffn_in_weight.shape[1]
    (g_last_sum, g_in_sum, g_out_own, out_bias_sum, in_bias_sum, last_bias_sum, qkv_sum, qb_sum, vb_sum,
     table_sum, tokens_grad, result) = call_finish(
        place, g_sum.reshape(-1, width), own, tokens_grad, result, heads_dev, hidden, table_rows)
    return (
        jnp.transpose(result, (1, 0, 2)),
        jnp.transpose(tokens_grad, (1, 0, 2)),
        table_sum,
        qkv_sum,
        qb_sum.reshape(-1),
        vb_sum.reshape(-1),
        g_out_own,
        out_bias_sum.reshape(-1),
        g_in_sum,
        in_bias_sum.reshape(-1),
        g_last_sum,
        last_bias_sum.reshape(-1),
    )


def solution(mesh):
    return jax.shard_map(
        body,
        mesh=mesh,
        in_specs=(
            P("mp", "dp", None),
            P("dp"),
            P("dp"),
            P(),
            P(None, "mp"),
            P("mp"),
            P("mp"),
            P("mp", None),
            P(),
            P(),
            P(),
            P(),
            P(),
            P("mp", "dp", None),
        ),
        out_specs=(
            P("mp", "dp", None),
            P("mp", "dp", None),
            P(),
            P(None, "mp"),
            P("mp"),
            P("mp"),
            P("mp", None),
            P(),
            P(),
            P(),
            P(),
            P(),
        ),
        check_vma=False,
    )
```
